32 devices in a mesh: tm: 4 (over z), tok: 2 (over y), rep: 4 (over x, core).
Axes of the slice: x: 2, y: 2, z: 4, core: 2. Of those that a mesh axis runs over, the one named last changes fastest.
Arguments:
- x_branch: bfloat16 [8, 1024, 1024], P(('tok', 'rep'), 'tm'), may hold values from -6 to 6
- z_gate: bfloat16 [8, 1024, 1024], P(('tok', 'rep'), 'tm'), may hold values from -6 to 6
- b_input: bfloat16 [8, 1024, 128], P(('tok', 'rep'), 'tm'), may hold values from -6 to 6
- c_input: bfloat16 [8, 1024, 128], P(('tok', 'rep'), 'tm'), may hold values from -0.59765625 to 0.59765625
- step_raw: float32 [8, 16, 1024], P(('tok', 'rep'), None, 'tm'), may hold values from -4 to 4
- rate_log: float32 [16], replicated, may hold values from -3.5 to 1
- step_bias: float32 [16], replicated, may hold values from -4.5 to -3
- skip_gain: float32 [16], replicated, may hold values from 0.5 to 2
- norm_gain: float32 [1024], replicated, may hold values from 0.5 to 1.5
- out_weight: bfloat16 [1024, 1024], P(('tok', 'rep')), may hold values from -0.1875 to 0.1875
- out_grad: bfloat16 [8, 1024, 1024], P(('tok', 'rep'), 'tm'), may hold values from -6 to 6
Outputs:
- mixed_out: bfloat16 [8, 1024, 1024], P(('tok', 'rep'), 'tm')
- x_grad: bfloat16 [8, 1024, 1024], P(('tok', 'rep'), 'tm')
- z_grad: bfloat16 [8, 1024, 1024], P(('tok', 'rep'), 'tm')
- b_grad: bfloat16 [8, 1024, 128], P(('tok', 'rep'), 'tm')
- c_grad: bfloat16 [8, 1024, 128], P(('tok', 'rep'), 'tm')
- step_grad: float32 [8, 16, 1024], P(('tok', 'rep'), None, 'tm')
- rate_grad: float32 [16], replicated
- bias_grad: float32 [16], replicated
- skip_grad: float32 [16], replicated
- gain_grad: float32 [1024], replicated
- weight_grad: bfloat16 [1024, 1024], P(('tok', 'rep'))
The draws below stay inside these ranges and needn't reach their ends.
All inputs are finite; a program needn't handle non-finite values.
Results may differ from the reference program's by a relative error of at most 0.0085.
Values may be sent and summed in bfloat16 or wider, within the bound.
No kernel may reach another device: no remote copies, remote signals or barrier semaphores. Data moves between devices by JAX's collectives and lax.ppermute only.
A program may use at most 128 MiB of HBM per device.

```python
import jax
import jax.numpy as jnp
from jax import lax

D = 1024
N = 128
H = 16
FR_DEV = 256
DI = 1024
SEQS = 8
LEN = 1024


def level_of(rng, extent, split, least, high):
    def one(axis_at, parts):
        draws = jax.random.uniform(jax.random.fold_in(jax.random.fold_in(rng, 6), axis_at), (parts,), jnp.float32, least / len(split), high / len(split))
        return jnp.repeat(jnp.exp(draws), extent[axis_at] // parts).reshape((-1,) + (1,) * (len(extent) - axis_at - 1))

    loudness = one(*split[0])
    for cut in split[1:]:
        loudness = loudness * one(*cut)
    return loudness


def bell_draw(key, shape, deviation, most, cuts=(), kind=jnp.bfloat16):
    values = deviation * jax.random.normal(key, shape, jnp.float32)
    if cuts:
        values = values * level_of(key, shape, cuts, -0.22, 0.18)
    return jnp.clip(values, -most, most).astype(kind)


def setup_inputs(seed: int = 0) -> dict:
    splits = jax.random.split(jax.random.key(seed), 12)
    return {
        "x_branch": bell_draw(splits[0], (SEQS, LEN, DI), 1.0, 6.0, ((0, 8), (1, 4))),
        "z_gate": bell_draw(splits[1], (SEQS, LEN, DI), 1.0, 6.0, ((0, 8), (1, 4))),
        "b_input": bell_draw(splits[2], (SEQS, LEN, N), 1.0, 6.0, ((0, 8), (1, 4))),
        "c_input": bell_draw(splits[3], (SEQS, LEN, N), 0.1, 0.59765625, ((0, 8), (1, 4))),
        "step_raw": bell_draw(splits[4], (SEQS, H, LEN), 1.0, 4.0, ((0, 8), (2, 4)), jnp.float32),
        "rate_log": jnp.clip(jax.random.uniform(splits[5], (H,), jnp.float32, -3.5, 1.0), -3.5, 1.0),
        "step_bias": jnp.clip(jax.random.uniform(splits[6], (H,), jnp.float32, -4.5, -3.0), -4.5, -3.0),
        "skip_gain": jnp.clip(jax.random.uniform(splits[7], (H,), jnp.float32, 0.5, 2.0), 0.5, 2.0),
        "norm_gain": jnp.clip(1.0 + 0.1 * jax.random.normal(splits[8], (DI,), jnp.float32), 0.5, 1.5),
        "out_weight": bell_draw(splits[9], (DI, D), DI ** -0.5, 0.1875, ((0, 8),)),
        "out_grad": bell_draw(splits[10], (SEQS, LEN, D), 1.0, 6.0, ((0, 8), (1, 4))),
    }


def decay_terms(step_raw, rate_log, step_bias):
    delta = jax.nn.softplus(step_raw + step_bias[None, :, None])
    cumlog = jnp.cumsum(delta * (-jnp.exp(rate_log))[None, :, None], axis=2)
    return (delta, cumlog)

def block_parts(x_feat, b_feat, step_raw, rate_log, step_bias):
    delta, cumlog = decay_terms(step_raw, rate_log, step_bias)
    seqs, length, width = x_feat.shape
    heads = rate_log.shape[0]
    x_heads = x_feat.reshape(seqs, length, heads, width // heads)
    tailing = jnp.exp(cumlog[:, :, -1:] - cumlog) * delta
    weighted = x_heads * tailing.transpose(0, 2, 1)[..., None]
    state = jnp.einsum('sqhp,sqn->shpn', weighted, b_feat, precision=lax.Precision.HIGHEST)
    return (state, jnp.exp(cumlog[:, :, -1]))

def block_output(x_feat, z_feat, b_feat, c_feat, step_raw, rate_log, step_bias, skip_gain, norm_gain, incoming):
    delta, cumlog = decay_terms(step_raw, rate_log, step_bias)
    seqs, length, width = x_feat.shape
    heads = rate_log.shape[0]
    x_heads = x_feat.reshape(seqs, length, heads, width // heads)
    scores = jnp.einsum('sqn,skn->sqk', c_feat.astype(jnp.bfloat16), b_feat.astype(jnp.bfloat16), preferred_element_type=jnp.float32)
    positions = jnp.arange(length)
    later = positions[:, None] >= positions[None, :]
    gaps = cumlog[:, :, :, None] - cumlog[:, :, None, :]
    mixing = jnp.where(later, jnp.exp(jnp.where(later, gaps, 0.0)), 0.0)
    mixing = mixing * scores[:, None] * delta[:, :, None, :]
    within = jnp.einsum('shqk,skhp->sqhp', mixing, x_heads, precision=lax.Precision.HIGHEST)
    carried = jnp.einsum('sqn,shpn->sqhp', c_feat, incoming, precision=lax.Precision.HIGHEST)
    carried = carried * jnp.exp(cumlog).transpose(0, 2, 1)[..., None]
    inner = (within + carried + skip_gain[None, None, :, None] * x_heads).reshape(seqs, length, width)
    gated = inner * jax.nn.silu(z_feat)
    factor = lax.rsqrt(lax.optimization_barrier(jnp.mean(gated * gated, axis=-1, keepdims=True)) + 1e-05)
    return gated * factor * norm_gain

def sequence_normed(x_feat, z_feat, b_feat, c_feat, step_raw, rate_log, step_bias, skip_gain, norm_gain):
    length, width = x_feat.shape
    heads = rate_log.shape[0]
    blocks = length // FR_DEV
    state_size = b_feat.shape[1]
    x_blocks = x_feat.reshape(blocks, 1, FR_DEV, width)
    z_blocks = z_feat.reshape(blocks, 1, FR_DEV, width)
    b_blocks = b_feat.reshape(blocks, 1, FR_DEV, state_size)
    c_blocks = c_feat.reshape(blocks, 1, FR_DEV, state_size)
    s_blocks = step_raw.reshape(heads, blocks, FR_DEV).transpose(1, 0, 2)[:, None]

    def advance(carry, pieces):
        x_piece, z_piece, b_piece, c_piece, s_piece = pieces
        normed = block_output(x_piece, z_piece, b_piece, c_piece, s_piece, rate_log, step_bias, skip_gain, norm_gain, carry)
        state, total = block_parts(x_piece, b_piece, s_piece, rate_log, step_bias)
        return (total[:, :, None, None] * carry + state, normed)
    start = jnp.zeros((1, heads, width // heads, state_size), jnp.float32)
    _, normed = lax.scan(advance, start, (x_blocks, z_blocks, b_blocks, c_blocks, s_blocks))
    return normed.reshape(length, width)

def reference(x_branch, z_gate, b_input, c_input, step_raw, rate_log, step_bias, skip_gain, norm_gain, out_weight, out_grad):

    def per_sequence(carry, items):
        weight_acc, rate_acc, bias_acc, skip_acc, gain_acc = carry
        x_seq, z_seq, b_seq, c_seq, s_seq, g_seq = items
        normed_f, pull = jax.vjp(sequence_normed, x_seq.astype(jnp.float32), z_seq.astype(jnp.float32), b_seq.astype(jnp.float32), c_seq.astype(jnp.float32), s_seq, rate_log, step_bias, skip_gain, norm_gain)
        normed = normed_f.astype(jnp.bfloat16)
        mixed = jnp.dot(normed, out_weight, preferred_element_type=jnp.float32).astype(jnp.bfloat16)
        normed_grad = lax.dot_general(g_seq, out_weight, (((1,), (1,)), ((), ())), preferred_element_type=jnp.float32).astype(jnp.bfloat16)
        grads = pull(normed_grad.astype(jnp.float32))
        weight_acc = weight_acc + lax.dot_general(normed, g_seq, (((0,), (0,)), ((), ())), preferred_element_type=jnp.float32)
        carry = (weight_acc, rate_acc + grads[5], bias_acc + grads[6], skip_acc + grads[7], gain_acc + grads[8])
        outputs = (mixed, grads[0].astype(jnp.bfloat16), grads[1].astype(jnp.bfloat16), grads[2].astype(jnp.bfloat16), grads[3].astype(jnp.bfloat16), grads[4])
        return (carry, outputs)
    heads = rate_log.shape[0]
    width = norm_gain.shape[0]
    start = (jnp.zeros(out_weight.shape, jnp.float32), jnp.zeros((heads,), jnp.float32), jnp.zeros((heads,), jnp.float32), jnp.zeros((heads,), jnp.float32), jnp.zeros((width,), jnp.float32))
    sums, stacked = lax.scan(per_sequence, start, (x_branch, z_gate, b_input, c_input, step_raw, out_grad))
    weight_sum, rate_grad, bias_grad, skip_grad, gain_grad = sums
    mixed_out, x_grad, z_grad, b_grad, c_grad, step_grad = stacked
    return (mixed_out, x_grad, z_grad, b_grad, c_grad, step_grad, rate_grad, bias_grad, skip_grad, gain_grad, weight_sum.astype(jnp.bfloat16))
```

```python
import functools

import jax
import jax.numpy as jnp
from jax import lax
from jax.experimental import pallas as pl
from jax.experimental.pallas import tpu as pltpu
from jax.sharding import PartitionSpec as P

BF = jnp.bfloat16
F32 = jnp.float32
ROWS = ((0,), (0,))
LAST = ((1,), (1,))
VMEM_LIMIT = 56 * 1024 * 1024


def mm(a, b):
    return jnp.dot(a, b, preferred_element_type=F32)


def mm_tn(a, b):
    return lax.dot_general(a, b, (ROWS, ((), ())), preferred_element_type=F32)


def mm_nt(a, b):
    return lax.dot_general(a, b, (LAST, ((), ())), preferred_element_type=F32)


def split(v, parts):
    pieces = []
    for _ in range(parts):
        piece = v.astype(BF)
        pieces.append(piece)
        v = v - piece.astype(F32)
    return pieces


def column(ref):
    row = ref[...].reshape(1, -1)
    heads = row.shape[1]
    i = lax.broadcasted_iota(jnp.int32, (heads, heads), 0)
    j = lax.broadcasted_iota(jnp.int32, (heads, heads), 1)
    return jnp.sum(jnp.where(i == j, row, 0.0), axis=1, keepdims=True)


def head_map(heads, width):
    i = lax.broadcasted_iota(jnp.int32, (heads, width), 0)
    j = lax.broadcasted_iota(jnp.int32, (heads, width), 1)
    wide = width // heads
    return jnp.where((j >= i * wide) & (j < (i + 1) * wide), 1.0, 0.0).astype(F32)


def triangle(length, keep):
    i = lax.broadcasted_iota(jnp.int32, (length, length), 0)
    j = lax.broadcasted_iota(jnp.int32, (length, length), 1)
    return jnp.where(keep(i, j), 1.0, 0.0).astype(BF)


def along_frames(v, tri):
    heads = v.shape[0]
    out = mm(jnp.concatenate(split(v, 3), axis=0), tri)
    return out[:heads] + out[heads : 2 * heads] + out[2 * heads :]


def expand(v, hmap):
    return mm_tn(jnp.concatenate(split(v, 2), axis=0), jnp.concatenate([hmap, hmap], axis=0).astype(BF))


def expand_row(col, hmap):
    return jnp.sum(col * hmap, axis=0, keepdims=True)


def head_sums(y, hmap):
    hb = hmap.astype(BF)
    hi, lo = split(y, 2)
    return mm_nt(hb, hi) + mm_nt(hb, lo)


def decay(s_ref, rate_ref, bias_ref):
    v = s_ref[...] + column(bias_ref)
    e = jnp.exp(-jnp.abs(v))
    u = 1.0 + e
    d = u - 1.0
    log1p = jnp.where(d == 0.0, e, jnp.log(u) * (e / jnp.where(d == 0.0, 1.0, d)))
    delta = jnp.maximum(v, 0.0) + log1p
    a = -jnp.exp(column(rate_ref))
    ld = delta * a
    cum = along_frames(ld, triangle(ld.shape[1], lambda i, j: i <= j))
    return v, delta, a, ld, cum


def call(kernel, outs, *args, smem=(), name=None, scratch=()):
    specs = [
        pl.BlockSpec(memory_space=pltpu.SMEM if k in smem else pltpu.VMEM) for k in range(len(args))
    ]
    return pl.pallas_call(
        kernel,
        out_shape=[jax.ShapeDtypeStruct(s, t) for s, t in outs],
        in_specs=specs,
        out_specs=[pl.BlockSpec(memory_space=pltpu.VMEM)] * len(outs),
        scratch_shapes=list(scratch),
        compiler_params=pltpu.CompilerParams(vmem_limit_bytes=VMEM_LIMIT),
        name=name,
    )(*args)


def state_kernel(x_ref, b_ref, s_ref, rate_ref, bias_ref, state_ref, total_ref):
    _, delta, _, _, cum = decay(s_ref, rate_ref, bias_ref)
    hmap = head_map(cum.shape[0], x_ref.shape[1])
    last = cum[:, -1:]
    tail = expand(jnp.exp(last - cum) * delta, hmap)
    weighted = (x_ref[...].astype(F32) * tail).astype(BF)
    state_ref[...] = mm_tn(b_ref[...], weighted).astype(BF)
    total_ref[...] = expand_row(jnp.exp(last), hmap)


def inner_kernel(x_ref, b_ref, c_ref, s_ref, rate_ref, bias_ref, skip_ref, inner_ref):
    _, delta, _, _, cum = decay(s_ref, rate_ref, bias_ref)
    heads, length = cum.shape
    width = x_ref.shape[1]
    hmap = head_map(heads, width)
    cum_t = cum.T
    x = x_ref[...].astype(F32)
    xd = (x * expand(delta, hmap)).astype(BF)
    skip = expand_row(column(skip_ref), hmap)
    half = length // 2
    scores = mm_nt(c_ref[...], b_ref[...])
    i = lax.broadcasted_iota(jnp.int32, (half, half), 0)
    j = lax.broadcasted_iota(jnp.int32, (half, half), 1)
    diag = i >= j
    s00 = jnp.where(diag, scores[:half, :half], 0.0)
    s10 = scores[half:, :half]
    s11 = jnp.where(diag, scores[half:, half:], 0.0)
    pair = 2 * (width // heads)
    first = lax.broadcasted_iota(jnp.int32, (half, pair), 1) < pair // 2
    for p in range(heads // 2):
        cols = slice(p * pair, (p + 1) * pair)
        upper, lower = [], []
        for h in (2 * p, 2 * p + 1):
            q0, q1 = cum_t[:half, h : h + 1], cum_t[half:, h : h + 1]
            k0, k1 = cum[h : h + 1, :half], cum[h : h + 1, half:]
            m00 = jnp.exp(jnp.minimum(q0 - k0, 0.0)) * s00
            m10 = jnp.exp(jnp.minimum(q1 - k0, 0.0)) * s10
            m11 = jnp.exp(jnp.minimum(q1 - k1, 0.0)) * s11
            upper.append(m00.astype(BF))
            lower.append(jnp.concatenate([m10.astype(BF), m11.astype(BF)], axis=1))
        y0 = mm(jnp.concatenate(upper, axis=0), xd[:half, cols])
        y1 = mm(jnp.concatenate(lower, axis=0), xd[:, cols])
        inner_ref[:half, cols] = jnp.where(first, y0[:half], y0[half:]) + skip[:, cols] * x[:half, cols]
        inner_ref[half:, cols] = jnp.where(first, y1[:half], y1[half:]) + skip[:, cols] * x[half:, cols]


def weight_kernel(idx_ref, g_ref, *refs):
    pieces, (full_ref, ng_ref) = refs[:-2], refs[-2:]
    me = idx_ref[0]
    rows, half = pieces[0].shape[0], pieces[0].shape[1] // 2

    def place(k):
        return pl.ds(pl.multiple_of((me ^ k) * rows, rows), rows)

    w, wc, wx, wxc, wy, wyc, d1, d2, d1c, d2c = pieces
    for k, piece in ((0, w), (1, wc), (2, wx), (3, wxc), (4, wy), (5, wyc)):
        full_ref[place(k), :] = piece[...]
    full_ref[place(6), :half] = d1[...]
    full_ref[place(6), half:] = d2[...]
    full_ref[place(7), :half] = d1c[...]
    full_ref[place(7), half:] = d2c[...]
    ng_ref[...] = mm_nt(g_ref[...], full_ref[...]).astype(BF)


def grad_kernel(g_ref, full_ref, ng_ref):
    ng_ref[...] = mm_nt(g_ref[...], full_ref[...]).astype(BF)


def norm_kernel(
    local_ref, inc_ref, c_ref, z_ref, x_ref, s_ref, rate_ref, bias_ref, skip_ref, gain_ref, ng_ref,
    normed_ref, dy_ref, carry_ref, zg_ref, rows_ref, gains_ref, skips_ref,
):
    _, _, _, _, cum = decay(s_ref, rate_ref, bias_ref)
    heads = cum.shape[0]
    width = x_ref.shape[1]
    hmap = head_map(heads, width)
    ec = expand(jnp.exp(cum), hmap)
    inner = local_ref[...] + mm(c_ref[...], inc_ref[...]) * ec
    z = z_ref[...].astype(F32)
    sig = 1.0 / (1.0 + jnp.exp(-z))
    silu = z * sig
    gated = inner * silu
    gain = gain_ref[...].reshape(1, -1)
    r = lax.rsqrt(jnp.mean(gated * gated, axis=1, keepdims=True) + 1e-05)
    nhat = gated * r
    normed_ref[...] = (nhat * gain).astype(BF)
    ng = ng_ref[...].astype(F32)
    prod = ng * nhat
    gains_ref[...] = jnp.sum(prod, axis=0, keepdims=True)
    m = jnp.mean(prod * gain, axis=1, keepdims=True)
    dgated = r * (ng * gain - nhat * m)
    dinner = dgated * silu
    dy = dinner.astype(BF)
    dy_ref[...] = dy
    carry_ref[...] = mm_tn(c_ref[...], (dinner * ec).astype(BF)).astype(BF)
    zg_ref[...] = (dgated * inner * (sig + silu * (1.0 - sig))).astype(BF)
    x = x_ref[...].astype(F32)
    dyf = dy.astype(F32)
    skip = expand_row(column(skip_ref), hmap)
    rows_ref[...] = head_sums(dyf * (inner - skip * x), hmap)
    skips_ref[...] = jnp.sum(jnp.sum(dinner * x, axis=0, keepdims=True) * hmap, axis=1, keepdims=True)


def outer_kernel(idx_ref, normed_ref, g_ref, mine_ref, other_ref):
    me = idx_ref[0]
    rows = mine_ref.shape[1]
    for k in range(8):
        cols = pl.ds(pl.multiple_of((me ^ k) * rows, rows), rows)
        part = mm_tn(normed_ref[:, cols], g_ref[...]).astype(BF)
        if k % 2 == 0:
            mine_ref[k // 2] = part
        else:
            other_ref[k // 2] = part


def outer_full_kernel(normed_ref, g_ref, out_ref):
    out_ref[...] = mm_tn(normed_ref[...], g_ref[...])


def add_pair_kernel(mine_ref, got_ref, a_keep, a_send, b_keep, b_send):
    half = mine_ref.shape[2] // 2

    def total(k, cols):
        return mine_ref[k, :, cols].astype(F32) + got_ref[k, :, cols].astype(F32)

    left, right = slice(0, half), slice(half, 2 * half)
    a_keep[0], a_keep[1] = total(0, left), total(2, left)
    a_send[0], a_send[1] = total(1, left).astype(BF), total(3, left).astype(BF)
    b_keep[0], b_keep[1] = total(0, right), total(1, right)
    b_send[0], b_send[1] = total(2, right).astype(BF), total(3, right).astype(BF)


def add_second_kernel(a_ref, ga_ref, b_ref, gb_ref, a_keep, a_send, b_keep, b_send):
    a_keep[...] = a_ref[0] + ga_ref[0].astype(F32)
    a_send[...] = (a_ref[1] + ga_ref[1].astype(F32)).astype(BF)
    b_keep[...] = b_ref[0] + gb_ref[0].astype(F32)
    b_send[...] = (b_ref[1] + gb_ref[1].astype(F32)).astype(BF)


def add_third_kernel(pos_ref, a_ref, ga_ref, b_ref, gb_ref, keep_ref, *refs):
    sends, scratch = refs[:-1], refs[-1]
    half = a_ref.shape[1]
    count = len(sends) + 1
    rows = a_ref.shape[0] // count
    scratch[:, :half] = a_ref[...] + ga_ref[...].astype(F32)
    scratch[:, half:] = b_ref[...] + gb_ref[...].astype(F32)
    z = pos_ref[1]

    def quarter(k):
        return scratch[pl.ds(pl.multiple_of(lax.rem(z + k, count) * rows, rows), rows), :]

    keep_ref[...] = quarter(0)
    for k, send in enumerate(sends):
        send[...] = quarter(k + 1).astype(BF)


def add_quarter_kernel(*refs):
    keep_ref, gots, out_ref = refs[0], refs[1:-1], refs[-1]
    total = keep_ref[...]
    for got in gots:
        total = total + got[...].astype(F32)
    out_ref[...] = total.astype(BF)


def join_kernel(pos_ref, *refs):
    pieces, out_ref = refs[:-1], refs[-1]
    count = len(pieces)
    rows = pieces[0].shape[0]
    z = pos_ref[1]
    for k, piece in enumerate(pieces):
        at = lax.rem(z + count - k, count) * rows
        out_ref[pl.ds(pl.multiple_of(at, rows), rows), :] = piece[...]


def back_kernel(
    x_ref, b_ref, c_ref, s_ref, rate_ref, bias_ref, skip_ref, dy_ref, inc_ref, normed_ref, full_ref,
    mixed_ref, cg_ref, xg_ref, bg_ref, cols_ref, dxw_ref,
):
    _, delta, _, _, cum = decay(s_ref, rate_ref, bias_ref)
    heads, length = cum.shape
    width = x_ref.shape[1]
    hmap = head_map(heads, width)
    cum_t = cum.T
    delta_e = expand(delta, hmap)
    xd = (x_ref[...].astype(F32) * delta_e).astype(BF)
    dy = dy_ref[...]
    half = length // 2
    scores = mm_nt(b_ref[...], c_ref[...])
    i = lax.broadcasted_iota(jnp.int32, (half, half), 0)
    j = lax.broadcasted_iota(jnp.int32, (half, half), 1)
    diag = j >= i
    s00 = jnp.where(diag, scores[:half, :half], 0.0)
    s01 = scores[:half, half:]
    s11 = jnp.where(diag, scores[half:, half:], 0.0)
    pair = 2 * (width // heads)
    first = lax.broadcasted_iota(jnp.int32, (half, pair), 1) < pair // 2
    whole_first = lax.broadcasted_iota(jnp.int32, (length, pair), 1) < pair // 2
    d00 = jnp.zeros((half, half), F32)
    d01 = jnp.zeros((half, half), F32)
    d11 = jnp.zeros((half, half), F32)
    none = jnp.zeros((length, pair), BF)
    for p in range(heads // 2):
        cols = slice(p * pair, (p + 1) * pair)
        xp, dp = xd[:, cols], dy[:, cols]
        stacked = jnp.concatenate([jnp.where(whole_first, xp, none), jnp.where(whole_first, none, xp)], axis=0)
        dm = mm_nt(stacked, dp)
        upper, lower = [], []
        for n, h in enumerate((2 * p, 2 * p + 1)):
            k0, k1 = cum_t[:half, h : h + 1], cum_t[half:, h : h + 1]
            q0, q1 = cum[h : h + 1, :half], cum[h : h + 1, half:]
            l00 = jnp.exp(jnp.minimum(q0 - k0, 0.0))
            l01 = jnp.exp(jnp.minimum(q1 - k0, 0.0))
            l11 = jnp.exp(jnp.minimum(q1 - k1, 0.0))
            at = n * length
            d00 = d00 + l00 * dm[at : at + half, :half]
            d01 = d01 + l01 * dm[at : at + half, half:]
            d11 = d11 + l11 * dm[at + half : at + length, half:]
            upper.append(jnp.concatenate([(l00 * s00).astype(BF), (l01 * s01).astype(BF)], axis=1))
            lower.append((l11 * s11).astype(BF))
        y0 = mm(jnp.concatenate(upper, axis=0), dp)
        y1 = mm(jnp.concatenate(lower, axis=0), dp[half:])
        dxw_ref[:half, cols] = jnp.where(first, y0[:half], y0[half:])
        dxw_ref[half:, cols] = jnp.where(first, y1[:half], y1[half:])
    d00 = jnp.where(diag, d00, 0.0).astype(BF)
    d01 = d01.astype(BF)
    d11 = jnp.where(diag, d11, 0.0).astype(BF)
    c0, c1 = c_ref[:half, :], c_ref[half:, :]
    b0, b1 = b_ref[:half, :], b_ref[half:, :]
    bg_ref[:half, :] = (mm(d00, c0) + mm(d01, c1)).astype(BF)
    bg_ref[half:, :] = mm(d11, c1).astype(BF)
    ec = expand(jnp.exp(cum), hmap)
    carried = mm_nt((dy.astype(F32) * ec).astype(BF), inc_ref[...])
    cg_ref[:half, :] = (carried[:half] + mm_tn(d00, b0).astype(BF).astype(F32)).astype(BF)
    cg_ref[half:, :] = (carried[half:] + (mm_tn(d01, b0) + mm_tn(d11, b1)).astype(BF).astype(F32)).astype(BF)
    dxw = dxw_ref[...]
    cols_ref[...] = head_sums(xd.astype(F32) * dxw, hmap)
    skip = expand_row(column(skip_ref), hmap)
    xg_ref[...] = delta_e * dxw + skip * dy.astype(F32)
    mixed_ref[...] = mm(normed_ref[...], full_ref[...]).astype(BF)


def last_kernel(
    x_ref, b_ref, s_ref, rate_ref, bias_ref, later_ref, inc_ref, xg_ref, bg_ref, rows_ref, cols_ref, gains_ref, skips_ref,
    x_out, b_out, step_out, sums_out,
):
    v, delta, a, ld, cum = decay(s_ref, rate_ref, bias_ref)
    heads, length = cum.shape
    width = x_ref.shape[1]
    hmap = head_map(heads, width)
    last = cum[:, -1:]
    tailing = jnp.exp(last - cum)
    tail = tailing * delta
    tail_e = expand(tail, hmap)
    x = x_ref[...].astype(F32)
    later = later_ref[...]
    dweighted = mm(b_ref[...], later)
    x_out[...] = (xg_ref[...] + tail_e * dweighted).astype(BF)
    weighted = (x * tail_e).astype(BF)
    b_out[...] = (bg_ref[...].astype(F32) + mm_nt(weighted, later)).astype(BF)
    dtail = head_sums(x * dweighted, hmap)
    cross = jnp.sum(later.astype(F32) * inc_ref[...].astype(F32), axis=0, keepdims=True)
    dtotal = jnp.sum(cross * hmap, axis=1, keepdims=True) * jnp.exp(last)
    cols = cols_ref[...]
    dld = along_frames(rows_ref[...] - cols, triangle(length, lambda i, j: i >= j))
    dld = dld + along_frames(dtail * tail, triangle(length, lambda i, j: i < j)) + dtotal
    ddelta = cols / delta + dtail * tailing + a * dld
    dstep = ddelta / (1.0 + jnp.exp(-v))
    step_out[...] = dstep
    drate = jnp.sum(dld * ld, axis=1, keepdims=True)
    dbias = jnp.sum(dstep, axis=1, keepdims=True)
    i = lax.broadcasted_iota(jnp.int32, (heads, 128), 0)
    j = lax.broadcasted_iota(jnp.int32, (heads, 128), 1)

    def lay(col, at):
        return jnp.sum(jnp.where(j == i + at, col, 0.0), axis=0, keepdims=True)

    small = lay(drate, 0) + lay(dbias, heads) + lay(skips_ref[...], 2 * heads)
    sums_out[:, :width] = jnp.broadcast_to(gains_ref[...], (sums_out.shape[0], width))
    sums_out[:, width:] = jnp.broadcast_to(small, (sums_out.shape[0], 128))


def sums_kernel(all_ref, out_ref):
    out_ref[...] = jnp.sum(all_ref[...], axis=0, keepdims=True)


def chain(value, total, axis, reverse):
    count = lax.axis_size(axis)
    incoming = jnp.zeros(value.shape, BF)
    for hop in range(count - 1):
        at = count - 1 - hop if reverse else hop
        to = at - 1 if reverse else at + 1
        send = (incoming.astype(F32) * total + value.astype(F32)).astype(BF)
        incoming = incoming + lax.ppermute(send, axis, [(at, to)])
    return incoming


def scan_far(value, total, axis, reverse):
    count = lax.axis_size(axis)
    position = lax.axis_index(axis)
    decayed, state = total, value.astype(F32)
    step = 1
    while step < count:
        pairs = [(k, k - step) for k in range(step, count)] if reverse else [(k, k + step) for k in range(count - step)]
        inside = position + step < count if reverse else position >= step
        got_state = lax.ppermute(state.astype(BF), axis, pairs).astype(F32)
        got_total = lax.ppermute(decayed, axis, pairs)
        state = jnp.where(inside, decayed * got_state + state, state)
        decayed = jnp.where(inside, decayed * got_total, decayed)
        step *= 2
    pairs = [(k, k - 1) for k in range(1, count)] if reverse else [(k, k + 1) for k in range(count - 1)]
    return lax.ppermute(state.astype(BF), axis, pairs)


def shards(x_branch, z_gate, b_input, c_input, step_raw, rate_log, step_bias, skip_gain, norm_gain, out_weight, out_grad):
    seqs, length, width = x_branch.shape
    model = out_grad.shape[2]
    heads = rate_log.shape[0]
    state_size = b_input.shape[2]
    x, z, b, c, s, g = x_branch[0], z_gate[0], b_input[0], c_input[0], step_raw[0], out_grad[0]
    n_tm, n_tok, n_rep = lax.axis_size("tm"), lax.axis_size("tok"), lax.axis_size("rep")
    rep, tok, tm = lax.axis_index("rep"), lax.axis_index("tok"), lax.axis_index("tm")
    near = (n_tok, n_rep) == (2, 4)
    rows = out_weight.shape[0]
    full = (width, model)
    wide = (length, width)
    place = jnp.stack([tok * n_rep + rep, tm]).astype(jnp.int32)
    core = [(k, k ^ 1) for k in range(4)]
    side = [(k, k ^ 2) for k in range(4)]
    front = [(0, 1), (1, 0)]
    scan = chain if n_tm <= 4 else scan_far

    state, total = call(
        state_kernel, [((state_size, width), BF), ((1, width), F32)], x, b, s, rate_log, step_bias, name="state"
    )
    if near:
        half = model // 2
        wx = lax.ppermute(out_weight, "rep", side)
        wy = lax.ppermute(out_weight, "tok", front)
        wc = lax.ppermute(out_weight, "rep", core)
        d1 = lax.ppermute(wx[:, :half], "tok", front)
        d2 = lax.ppermute(wy[:, half:], "rep", side)
        wxc = lax.ppermute(wx, "rep", core)
        wyc = lax.ppermute(wy, "rep", core)
        d1c = lax.ppermute(d1, "rep", core)
        d2c = lax.ppermute(d2, "rep", core)
    incoming = scan(state, total, "tm", False)
    (local,) = call(inner_kernel, [(wide, F32)], x, b, c, s, rate_log, step_bias, skip_gain, name="inner")
    if near:
        weight, ng = call(
            weight_kernel, [(full, BF), (wide, BF)], place, g, out_weight, wc, wx, wxc, wy, wyc, d1, d2, d1c, d2c,
            smem=(0,), name="normed_grad",
        )
    else:
        weight = lax.all_gather(out_weight, ("tok", "rep"), axis=0, tiled=True)
        (ng,) = call(grad_kernel, [(wide, BF)], g, weight, name="normed_grad")
    normed, dy, carry, zg, row_sums, gains, skips = call(
        norm_kernel,
        [(wide, BF), (wide, BF), ((state_size, width), BF), (wide, BF), ((heads, length), F32), ((1, width), F32), ((heads, 1), F32)],
        local, incoming, c, z, x, s, rate_log, step_bias, skip_gain, norm_gain, ng, name="norm",
    )
    later = scan(carry, total, "tm", True)
    if near:
        block = (4, rows, model)
        mine, other = call(outer_kernel, [(block, BF), (block, BF)], place, normed, g, smem=(0,), name="outer")
        got = lax.ppermute(other, "rep", core)
        cut = (2, rows, half)
        a_keep, a_send, b_keep, b_send = call(
            add_pair_kernel, [(cut, F32), (cut, BF), (cut, F32), (cut, BF)], mine, got, name="add_pair"
        )
        ga = lax.ppermute(a_send, "rep", side)
        gb = lax.ppermute(b_send, "tok", front)
        cut = (rows, half)
        a_keep, a_send, b_keep, b_send = call(
            add_second_kernel, [(cut, F32), (cut, BF), (cut, F32), (cut, BF)], a_keep, ga, b_keep, gb, name="add_second"
        )
        ga = lax.ppermute(a_send, "tok", front)
        gb = lax.ppermute(b_send, "rep", side)
        part = (rows // n_tm, model)
        keep, *sends = call(
            add_third_kernel, [(part, F32)] + [(part, BF)] * (n_tm - 1), place, a_keep, ga, b_keep, gb,
            smem=(0,), name="add_third", scratch=[pltpu.VMEM((rows, model), F32)],
        )
        ahead = [[(i, (i + k) % n_tm) for i in range(n_tm)] for k in range(1, n_tm)]
        gots = [lax.ppermute(v, "tm", pairs) for v, pairs in zip(sends, ahead)]
        (quarter,) = call(add_quarter_kernel, [(part, BF)], keep, *gots, name="add_quarter")
        pieces = [quarter] + [lax.ppermute(quarter, "tm", pairs) for pairs in ahead]
        (weight_grad,) = call(join_kernel, [((rows, model), BF)], place, *pieces, smem=(0,), name="join")
    else:
        (outer,) = call(outer_full_kernel, [(full, F32)], normed, g, name="outer")
        share = lax.psum_scatter(outer, ("tok", "rep"), scatter_dimension=0, tiled=True)
        weight_grad = lax.psum(share, "tm").astype(BF)
    mixed, c_grad, xg, bg, col_sums = call(
        back_kernel,
        [(wide, BF), ((length, state_size), BF), (wide, F32), ((length, state_size), BF), ((heads, length), F32)],
        x, b, c, s, rate_log, step_bias, skip_gain, dy, incoming, normed, weight,
        name="back", scratch=[pltpu.VMEM(wide, F32)],
    )
    devices = n_tm * n_tok * n_rep
    copies = devices if near else 1
    x_grad, b_grad, step_grad, sums = call(
        last_kernel,
        [(wide, BF), ((length, state_size), BF), ((heads, length), F32), ((copies, width + 128), F32)],
        x, b, s, rate_log, step_bias, later, incoming, xg, bg, row_sums, col_sums, gains, skips, name="last",
    )
    everywhere = ("tm", "tok", "rep")
    if near:
        sums = lax.all_to_all(sums, everywhere, 0, 0, tiled=True)
        (sums,) = call(sums_kernel, [((1, width + 128), F32)], sums, name="sums")
    else:
        sums = lax.psum(sums, everywhere)
    sums = sums[0]
    gain_grad = sums[:width]
    rate_grad = sums[width : width + heads]
    bias_grad = sums[width + heads : width + 2 * heads]
    skip_grad = sums[width + 2 * heads : width + 3 * heads]
    return (
        mixed[None], x_grad[None], zg[None], b_grad[None], c_grad[None], step_grad[None],
        rate_grad, bias_grad, skip_grad, gain_grad, weight_grad,
    )


def solution(mesh):
    tokens = P(("tok", "rep"), "tm", None)
    frames = P(("tok", "rep"), None, "tm")
    weight = P(("tok", "rep"), None)
    return jax.shard_map(
        shards,
        mesh=mesh,
        in_specs=(tokens, tokens, tokens, tokens, frames, P(), P(), P(), P(), weight, tokens),
        out_specs=(tokens, tokens, tokens, tokens, tokens, frames, P(), P(), P(), P(), weight),
        check_vma=False,
    )
```

```python
import functools

import jax
import jax.numpy as jnp
from jax import lax
from jax.experimental import pallas as pl
from jax.experimental.pallas import tpu as pltpu
from jax.sharding import PartitionSpec as P

BF = jnp.bfloat16
F32 = jnp.float32
ROWS = ((0,), (0,))
LAST = ((1,), (1,))
CHUNKS = 8
HBM_BYTES_PER_US = 3.69e6
TM = 4
VMEM_LIMIT = 24 * 1024 * 1024


def mm(a, b):
    return jnp.dot(a, b, preferred_element_type=F32)


def mm_tn(a, b):
    return lax.dot_general(a, b, (ROWS, ((), ())), preferred_element_type=F32)


def mm_nt(a, b):
    return lax.dot_general(a, b, (LAST, ((), ())), preferred_element_type=F32)


def split(v, parts):
    pieces = []
    for _ in range(parts):
        piece = v.astype(BF)
        pieces.append(piece)
        v = v - piece.astype(F32)
    return pieces


def column(ref):
    row = ref[...].reshape(1, -1)
    heads = row.shape[1]
    i = lax.broadcasted_iota(jnp.int32, (heads, heads), 0)
    j = lax.broadcasted_iota(jnp.int32, (heads, heads), 1)
    return jnp.sum(jnp.where(i == j, row, 0.0), axis=1, keepdims=True)


def head_map(heads, width):
    i = lax.broadcasted_iota(jnp.int32, (heads, width), 0)
    j = lax.broadcasted_iota(jnp.int32, (heads, width), 1)
    wide = width // heads
    return jnp.where((j >= i * wide) & (j < (i + 1) * wide), 1.0, 0.0).astype(F32)


def triangle(length, keep):
    i = lax.broadcasted_iota(jnp.int32, (length, length), 0)
    j = lax.broadcasted_iota(jnp.int32, (length, length), 1)
    return jnp.where(keep(i, j), 1.0, 0.0).astype(BF)


def along_frames(v, tri):
    heads = v.shape[0]
    out = mm(jnp.concatenate(split(v, 3), axis=0), tri)
    return out[:heads] + out[heads : 2 * heads] + out[2 * heads :]


def expand(v, hmap):
    return mm_tn(jnp.concatenate(split(v, 2), axis=0), jnp.concatenate([hmap, hmap], axis=0).astype(BF))


def expand_row(col, hmap):
    return jnp.sum(col * hmap, axis=0, keepdims=True)


def head_sums(y, hmap):
    hb = hmap.astype(BF)
    hi, lo = split(y, 2)
    return mm_nt(hb, hi) + mm_nt(hb, lo)


def decay(s_ref, rate_ref, bias_ref):
    v = s_ref[...] + column(bias_ref)
    e = jnp.exp(-jnp.abs(v))
    u = 1.0 + e
    d = u - 1.0
    log1p = jnp.where(d == 0.0, e, jnp.log(u) * (e / jnp.where(d == 0.0, 1.0, d)))
    delta = jnp.maximum(v, 0.0) + log1p
    a = -jnp.exp(column(rate_ref))
    ld = delta * a
    cum = along_frames(ld, triangle(ld.shape[1], lambda i, j: i <= j))
    return v, delta, a, ld, cum


class Coming:
    def __init__(self, source, target, semaphore):
        self.copy = pltpu.make_async_copy(source, target, semaphore)
        self.copy.start()
        self.target, self.waited = target, False

    def ready(self):
        if not self.waited:
            self.copy.wait()
            self.waited = True
        return self.target


def near_by(shape, dtype):
    return pltpu.VMEM(shape, dtype)


def away(shape, dtype):
    return pltpu.HBM(shape, dtype)


def free(shape, dtype):
    return jax.ShapeDtypeStruct(shape, dtype)


def call(kernel, outs, far, *args, smem=(), name=None, scratch=(), after=(), beside=(), us=3):
    waits = len(after) + len(beside)
    specs = [pl.BlockSpec(memory_space=pl.ANY)] * len(far)
    specs += [
        pl.BlockSpec(memory_space=pltpu.SMEM if k in smem else pltpu.VMEM) for k in range(len(args))
    ]
    specs += [pl.BlockSpec(memory_space=pl.ANY)] * waits
    first, used = len(far), len(far) + len(args)
    landing = [pltpu.VMEM(v.shape, v.dtype) for v in far]
    semaphores = [pltpu.SemaphoreType.DMA((len(far),))] if far else []

    def body(*refs):
        refs, own = list(refs), len(far)
        coming = []
        if far:
            refs, targets, semaphore = refs[: -own - 1], refs[-own - 1 : -1], refs[-1]
            coming = [Coming(refs[k], targets[k], semaphore.at[k]) for k in range(own)]
        kernel(*coming, *refs[first:used], *refs[used + waits :])
        for one in coming:
            one.ready()

    return pl.pallas_call(
        body,
        out_shape=[where(shape, dtype) for shape, dtype, where in outs],
        in_specs=specs,
        out_specs=[pl.BlockSpec(memory_space=pltpu.VMEM)] * len(outs),
        scratch_shapes=list(scratch) + landing + semaphores,
        compiler_params=pltpu.CompilerParams(vmem_limit_bytes=VMEM_LIMIT),
        cost_estimate=pl.CostEstimate(flops=0, bytes_accessed=int(us * HBM_BYTES_PER_US), transcendentals=0),
        name=name,
    )(*[pltpu.with_memory_space_constraint(v, pltpu.HBM) for v in far], *args, *[pltpu.with_memory_space_constraint(v, pltpu.HBM) for v in after], *beside)


def store_decay(aux_ref, rows_ref, v, delta, a, ld, cum, skip, gain):
    heads = cum.shape[0]
    for k, value in enumerate((v, delta, ld, cum, jnp.broadcast_to(a, cum.shape))):
        aux_ref[k * heads : (k + 1) * heads, :] = value
    rows_ref[0:1, :] = skip
    rows_ref[1:2, :] = gain


def load_decay(aux_ref):
    heads = aux_ref.shape[0] // 5
    return [aux_ref[k * heads : (k + 1) * heads, :] for k in range(5)]


def store_parts(out_ref, state, row):
    count, blocks = out_ref.shape[0], row.shape[1] // 128
    rows = state.shape[0] // count
    tail = [v[:, n * 128 : (n + 1) * 128].astype(F32) for v in split(row, 2) for n in range(blocks)]
    tail = jnp.concatenate(tail, axis=0).astype(BF)
    for k in range(count):
        for n in range(blocks):
            out_ref[k, n * rows : (n + 1) * rows, :] = state[k * rows : (k + 1) * rows, n * 128 : (n + 1) * 128]
        out_ref[k, blocks * rows :, :] = tail


def payload_kernel(s_in, rate_in, bias_in, b_in, x_in, skip_in, gain_in, aux_ref, rows_ref, *outs):
    v, delta, a, ld, cum = decay(s_in.ready(), rate_in.ready(), bias_in.ready())
    x_ref, b_ref = x_in.ready(), b_in.ready()
    width = x_ref.shape[1]
    hmap = head_map(cum.shape[0], width)
    skip = expand_row(column(skip_in.ready()), hmap)
    store_decay(aux_ref, rows_ref, v, delta, a, ld, cum, skip, gain_in.ready()[...].reshape(1, -1))
    last = cum[:, -1:]
    tail = expand(jnp.exp(last - cum) * delta, hmap)
    weighted = (x_ref[...].astype(F32) * tail).astype(BF)
    state = mm_tn(b_ref[...], weighted).astype(BF)
    total = expand_row(jnp.exp(last), hmap)
    if len(outs) == 2:
        outs[0][...] = state
        outs[1][...] = total
        return
    (out_ref,) = outs
    store_parts(out_ref, state, total)


def part_decay(all_ref, k, n, rows, blocks):
    pair = all_ref[k, blocks * rows :, :].astype(F32)
    return pair[n : n + 1] + pair[blocks + n : blocks + n + 1]


def prefix_kernel(all_ref, out_ref):
    count, rows, width = out_ref.shape
    blocks = width // 128
    for n in range(blocks):
        cols = slice(n * 128, (n + 1) * 128)
        carried = jnp.zeros((rows, 128), F32)
        for k in range(count):
            out_ref[k, :, cols] = carried.astype(BF)
            if k + 1 < count:
                state = all_ref[k, n * rows : (n + 1) * rows, :].astype(F32)
                carried = state + part_decay(all_ref, k, n, rows, blocks) * carried


def suffix_kernel(grads_ref, all_ref, out_ref, gains_ref):
    count, rows, width = out_ref.shape
    blocks = width // 128
    for n in range(blocks):
        cols = slice(n * 128, (n + 1) * 128)
        carried = jnp.zeros((rows, 128), F32)
        for k in reversed(range(count)):
            out_ref[k, :, cols] = carried.astype(BF)
            if k > 0:
                grad = grads_ref[k, n * rows : (n + 1) * rows, :].astype(F32)
                carried = grad + part_decay(all_ref, k, n, rows, blocks) * carried
    gains = sum(grads_ref[k, blocks * rows :, :].astype(F32) for k in range(count))
    gains_ref[...] = gains[:blocks] + gains[blocks:]


def inner_kernel(b_in, c_in, x_in, aux_ref, rows_ref, inner_ref):
    _, delta, _, cum, _ = load_decay(aux_ref)
    x_ref, b_ref, c_ref = x_in.ready(), b_in.ready(), c_in.ready()
    heads, length = cum.shape
    width = x_ref.shape[1]
    hmap = head_map(heads, width)
    cum_t = cum.T
    x = x_ref[...].astype(F32)
    xd = (x * expand(delta, hmap)).astype(BF)
    skip = rows_ref[0:1, :]
    half = length // 2
    scores = mm_nt(c_ref[...], b_ref[...])
    i = lax.broadcasted_iota(jnp.int32, (half, half), 0)
    j = lax.broadcasted_iota(jnp.int32, (half, half), 1)
    diag = i >= j
    s00 = jnp.where(diag, scores[:half, :half], 0.0)
    s10 = scores[half:, :half]
    s11 = jnp.where(diag, scores[half:, half:], 0.0)
    pair = 2 * (width // heads)
    first = lax.broadcasted_iota(jnp.int32, (half, pair), 1) < pair // 2
    for p in range(heads // 2):
        cols = slice(p * pair, (p + 1) * pair)
        upper, lower = [], []
        for h in (2 * p, 2 * p + 1):
            q0, q1 = cum_t[:half, h : h + 1], cum_t[half:, h : h + 1]
            k0, k1 = cum[h : h + 1, :half], cum[h : h + 1, half:]
            m00 = jnp.exp(jnp.minimum(q0 - k0, 0.0)) * s00
            m10 = jnp.exp(jnp.minimum(q1 - k0, 0.0)) * s10
            m11 = jnp.exp(jnp.minimum(q1 - k1, 0.0)) * s11
            upper.append(m00.astype(BF))
            lower.append(jnp.concatenate([m10.astype(BF), m11.astype(BF)], axis=1))
        y0 = mm(jnp.concatenate(upper, axis=0), xd[:half, cols])
        y1 = mm(jnp.concatenate(lower, axis=0), xd[:, cols])
        inner_ref[:half, cols] = jnp.where(first, y0[:half], y0[half:]) + skip[:, cols] * x[:half, cols]
        inner_ref[half:, cols] = jnp.where(first, y1[:half], y1[half:]) + skip[:, cols] * x[half:, cols]


def weight_kernel(*refs):
    pieces, g_in, idx_ref, full_ref, ng_ref = [v.ready() for v in refs[:8]], *refs[8:]
    me = idx_ref[0]
    rows = pieces[0].shape[0]
    for k, piece in enumerate(pieces):
        full_ref[pl.ds(pl.multiple_of((me ^ k) * rows, rows), rows), :] = piece[...]
    ng_ref[...] = mm_nt(g_in.ready()[...], full_ref[...]).astype(BF)


def grad_kernel(g_ref, full_ref, ng_ref):
    ng_ref[...] = mm_nt(g_ref[...], full_ref[...]).astype(BF)


def norm_kernel(c_in, z_in, idx_ref, aux_ref, params_ref, local_ref, inc_ref, normed_ref, other_ref, inner_ref, factor_ref, ec_ref):
    _, _, _, cum, _ = load_decay(aux_ref)
    c_ref, z_ref = c_in.ready(), z_in.ready()
    heads, length = cum.shape
    width = z_ref.shape[1]
    hmap = head_map(heads, width)
    ec_ref[...] = expand(jnp.exp(cum), hmap)
    inner_ref[...] = mm(c_ref[...], inc_ref[...])
    gain = params_ref[1:2, :]
    step = length // CHUNKS

    for n in range(CHUNKS):
        at = slice(n * step, (n + 1) * step)
        inner = local_ref[at, :] + inner_ref[at, :] * ec_ref[at, :]
        inner_ref[at, :] = inner
        z = z_ref[at, :].astype(F32)
        gated = inner * (z / (1.0 + jnp.exp(-z)))
        r = lax.rsqrt(jnp.mean(gated * gated, axis=1, keepdims=True) + 1e-05)
        factor_ref[at, :] = jnp.broadcast_to(r, (step, 128))
        normed_ref[at, :] = (gated * r * gain).astype(BF)
    block = other_ref.shape[1] // 4
    for k in range(4):
        at = (2 * k + 1 - lax.rem(idx_ref[0], 2)) * block
        other_ref[:, k * block : (k + 1) * block] = normed_ref[:, pl.ds(pl.multiple_of(at, block), block)]


def norm_back_kernel(
    c_in, z_in, x_in, aux_ref, params_ref, inner_ref, factor_ref, ng_ref,
    dy_ref, carry_ref, zg_ref, rows_ref, gains_ref, skips_ref,
    ec_ref, de_ref, hi_ref, lo_ref,
):
    _, _, _, cum, _ = load_decay(aux_ref)
    c_ref, z_ref, x_ref = c_in.ready(), z_in.ready(), x_in.ready()
    heads, length = cum.shape
    width = x_ref.shape[1]
    hmap = head_map(heads, width)
    ec_ref[...] = expand(jnp.exp(cum), hmap)
    skip, gain = params_ref[0:1, :], params_ref[1:2, :]
    step = length // CHUNKS
    gains = jnp.zeros((1, width), F32)
    skips = jnp.zeros((1, width), F32)
    for n in range(CHUNKS):
        at = slice(n * step, (n + 1) * step)
        inner = inner_ref[at, :]
        z = z_ref[at, :].astype(F32)
        sig = 1.0 / (1.0 + jnp.exp(-z))
        silu = z * sig
        r = factor_ref[at, 0:1]
        nhat = inner * silu * r
        ng = ng_ref[at, :].astype(F32)
        prod = ng * nhat
        gains = gains + jnp.sum(prod, axis=0, keepdims=True)
        m = jnp.mean(prod * gain, axis=1, keepdims=True)
        dgated = r * (ng * gain - nhat * m)
        dinner = dgated * silu
        dy = dinner.astype(BF)
        dy_ref[at, :] = dy
        de_ref[at, :] = (dinner * ec_ref[at, :]).astype(BF)
        zg_ref[at, :] = (dgated * inner * (sig + silu * (1.0 - sig))).astype(BF)
        x = x_ref[at, :].astype(F32)
        skips = skips + jnp.sum(dinner * x, axis=0, keepdims=True)
        hi_ref[at, :], lo_ref[at, :] = split(dy.astype(F32) * (inner - skip * x), 2)
    carry = mm_tn(c_ref[...], de_ref[...]).astype(BF)
    if len(carry_ref.shape) == 2:
        carry_ref[...] = carry
    else:
        store_parts(carry_ref, carry, gains)
    hb = hmap.astype(BF)
    rows_ref[...] = mm_nt(hb, hi_ref[...]) + mm_nt(hb, lo_ref[...])
    gains_ref[...] = gains
    skips_ref[...] = jnp.sum(skips * hmap, axis=1, keepdims=True)


def outer_kernel(g_in, gc_in, idx_ref, normed_ref, got_ref, keep_ref, *sends):
    g_ref, gc_ref = g_in.ready(), gc_in.ready()
    me = idx_ref[0]
    core, chip = lax.rem(me, 2), me // 2
    rows = keep_ref.shape[0]
    for k, out_ref in enumerate((keep_ref, *sends)):
        mine = pl.ds(pl.multiple_of((2 * (chip ^ k) + core) * rows, rows), rows)
        theirs = pl.ds(pl.multiple_of((chip ^ k) * rows, rows), rows)
        part = mm_tn(normed_ref[:, mine], g_ref[...]) + mm_tn(got_ref[:, theirs], gc_ref[...])
        out_ref[...] = part.astype(out_ref.dtype)


def add_kernel(keep_in, pos_ref, *refs):
    gots, outs, scratch = refs[:3], refs[3:-1], refs[-1]
    total = keep_in.ready()[...]
    for got in gots:
        total = total + got[...].astype(F32)
    scratch[...] = total
    rows = outs[0].shape[0]
    for k, out_ref in enumerate(outs):
        at = lax.rem(pos_ref[1] + k, len(outs)) * rows
        out_ref[...] = scratch[pl.ds(pl.multiple_of(at, rows), rows), :].astype(out_ref.dtype)


def add_quarter_kernel(own_in, *refs):
    gots, out_ref = refs[:-1], refs[-1]
    total = own_in.ready()[...]
    for got in gots:
        total = total + got[...].astype(F32)
    out_ref[...] = total.astype(BF)


def join_kernel(*refs):
    pos_ref, pieces, out_ref = refs[0], refs[1:-1], refs[-1]
    count, rows = len(pieces), pieces[0].shape[0]
    for k, piece in enumerate(pieces):
        at = lax.rem(pos_ref[1] + count - k, count) * rows
        out_ref[pl.ds(pl.multiple_of(at, rows), rows), :] = piece[...]


def outer_full_kernel(normed_ref, g_ref, out_ref):
    out_ref[...] = mm_tn(normed_ref[...], g_ref[...])


def back_kernel(
    dy_in, b_in, c_in, x_in, full_in, aux_ref, params_ref, inc_ref, normed_ref,
    mixed_ref, cg_ref, xg_ref, bg_ref, cols_ref, dxw_ref,
):
    _, delta, _, cum, _ = load_decay(aux_ref)
    x_ref, b_ref, c_ref = x_in.ready(), b_in.ready(), c_in.ready()
    heads, length = cum.shape
    width = x_ref.shape[1]
    hmap = head_map(heads, width)
    cum_t = cum.T
    delta_e = expand(delta, hmap)
    xd = (x_ref[...].astype(F32) * delta_e).astype(BF)
    dy = dy_in.ready()[...]
    half = length // 2
    scores = mm_nt(b_ref[...], c_ref[...])
    i = lax.broadcasted_iota(jnp.int32, (half, half), 0)
    j = lax.broadcasted_iota(jnp.int32, (half, half), 1)
    diag = j >= i
    s00 = jnp.where(diag, scores[:half, :half], 0.0)
    s01 = scores[:half, half:]
    s11 = jnp.where(diag, scores[half:, half:], 0.0)
    pair = 2 * (width // heads)
    first = lax.broadcasted_iota(jnp.int32, (half, pair), 1) < pair // 2
    whole_first = lax.broadcasted_iota(jnp.int32, (length, pair), 1) < pair // 2
    d00 = jnp.zeros((half, half), F32)
    d01 = jnp.zeros((half, half), F32)
    d11 = jnp.zeros((half, half), F32)
    none = jnp.zeros((length, pair), BF)
    for p in range(heads // 2):
        cols = slice(p * pair, (p + 1) * pair)
        xp, dp = xd[:, cols], dy[:, cols]
        stacked = jnp.concatenate([jnp.where(whole_first, xp, none), jnp.where(whole_first, none, xp)], axis=0)
        dm = mm_nt(stacked, dp)
        upper, lower = [], []
        for n, h in enumerate((2 * p, 2 * p + 1)):
            k0, k1 = cum_t[:half, h : h + 1], cum_t[half:, h : h + 1]
            q0, q1 = cum[h : h + 1, :half], cum[h : h + 1, half:]
            l00 = jnp.exp(jnp.minimum(q0 - k0, 0.0))
            l01 = jnp.exp(jnp.minimum(q1 - k0, 0.0))
            l11 = jnp.exp(jnp.minimum(q1 - k1, 0.0))
            at = n * length
            d00 = d00 + l00 * dm[at : at + half, :half]
            d01 = d01 + l01 * dm[at : at + half, half:]
            d11 = d11 + l11 * dm[at + half : at + length, half:]
            upper.append(jnp.concatenate([(l00 * s00).astype(BF), (l01 * s01).astype(BF)], axis=1))
            lower.append((l11 * s11).astype(BF))
        y0 = mm(jnp.concatenate(upper, axis=0), dp)
        y1 = mm(jnp.concatenate(lower, axis=0), dp[half:])
        dxw_ref[:half, cols] = jnp.where(first, y0[:half], y0[half:])
        dxw_ref[half:, cols] = jnp.where(first, y1[:half], y1[half:])
    d00 = jnp.where(diag, d00, 0.0).astype(BF)
    d01 = d01.astype(BF)
    d11 = jnp.where(diag, d11, 0.0).astype(BF)
    c0, c1 = c_ref[:half, :], c_ref[half:, :]
    b0, b1 = b_ref[:half, :], b_ref[half:, :]
    bg_ref[:half, :] = (mm(d00, c0) + mm(d01, c1)).astype(BF)
    bg_ref[half:, :] = mm(d11, c1).astype(BF)
    ec = expand(jnp.exp(cum), hmap)
    carried = mm_nt((dy.astype(F32) * ec).astype(BF), inc_ref[...])
    cg_ref[:half, :] = (carried[:half] + mm_tn(d00, b0).astype(BF).astype(F32)).astype(BF)
    cg_ref[half:, :] = (carried[half:] + (mm_tn(d01, b0) + mm_tn(d11, b1)).astype(BF).astype(F32)).astype(BF)
    dxw = dxw_ref[...]
    cols_ref[...] = head_sums(xd.astype(F32) * dxw, hmap)
    skip = params_ref[0:1, :]
    xg_ref[...] = delta_e * dxw + skip * dy.astype(F32)
    mixed_ref[...] = mm(normed_ref[...], full_in.ready()[...]).astype(BF)


def last_kernel(
    b_in, x_in, rows_in, cols_in, bg_in, xg_in, skips_in, aux_ref, later_ref, inc_ref, *more,
):
    more, (x_out, b_out, step_out, sums_out) = more[:-4], more[-4:]
    v, delta, ld, cum, a = load_decay(aux_ref)
    x_ref, b_ref = x_in.ready(), b_in.ready()
    heads, length = cum.shape
    width = x_ref.shape[1]
    hmap = head_map(heads, width)
    last = cum[:, -1:]
    tailing = jnp.exp(last - cum)
    tail = tailing * delta
    tail_e = expand(tail, hmap)
    x = x_ref[...].astype(F32)
    later = later_ref[...]
    dweighted = mm(b_ref[...], later)
    x_out[...] = (xg_in.ready()[...] + tail_e * dweighted).astype(BF)
    weighted = (x * tail_e).astype(BF)
    b_out[...] = (bg_in.ready()[...].astype(F32) + mm_nt(weighted, later)).astype(BF)
    dtail = head_sums(x * dweighted, hmap)
    cross = jnp.sum(later.astype(F32) * inc_ref[...].astype(F32), axis=0, keepdims=True)
    dtotal = jnp.sum(cross * hmap, axis=1, keepdims=True) * jnp.exp(last)
    cols = cols_in.ready()[...]
    dld = along_frames(rows_in.ready()[...] - cols, triangle(length, lambda i, j: i >= j))
    dld = dld + along_frames(dtail * tail, triangle(length, lambda i, j: i < j)) + dtotal
    ddelta = cols / delta + dtail * tailing + a * dld
    dstep = ddelta / (1.0 + jnp.exp(-v))
    step_out[...] = dstep
    drate = jnp.sum(dld * ld, axis=1, keepdims=True)
    dbias = jnp.sum(dstep, axis=1, keepdims=True)
    i = lax.broadcasted_iota(jnp.int32, (heads, 128), 0)
    j = lax.broadcasted_iota(jnp.int32, (heads, 128), 1)

    def lay(col, at):
        return jnp.sum(jnp.where(j == i + at, col, 0.0), axis=0, keepdims=True)

    small = lay(drate, 0) + lay(dbias, heads) + lay(skips_in.ready()[...], 2 * heads)
    sums_out[0, :, :128] = small
    if len(more) == 2:
        pos_ref, gains_ref = more
        each = gains_ref.shape[0] // TM
        for n in range(each):
            at = pl.ds(pos_ref[1] * each + n, 1)
            sums_out[0, :, (n + 1) * 128 : (n + 2) * 128] = gains_ref[at, :]
        for k in range(1, sums_out.shape[0]):
            sums_out[k] = sums_out[0]
    else:
        sums_out[0, :, 128:] = more[0][...]


def sums_kernel(all_in, rate_out, bias_out, skip_out, gain_out):
    every = all_in.ready()[...]
    heads = rate_out.shape[0]
    small = jnp.sum(every[:, 0, :128], axis=0)
    rate_out[...] = small[:heads]
    bias_out[...] = small[heads : 2 * heads]
    skip_out[...] = small[2 * heads : 3 * heads]
    share = every.shape[2] - 128
    parts = gain_out.shape[0] // share
    group = every.shape[0] // parts
    for k in range(parts):
        gain_out[k * share : (k + 1) * share] = jnp.sum(every[k * group : (k + 1) * group, 0, 128:], axis=0)


def scan_far(value, total, axis, reverse):
    count = lax.axis_size(axis)
    position = lax.axis_index(axis)
    decayed, state = total, value.astype(F32)
    step = 1
    while step < count:
        pairs = [(k, k - step) for k in range(step, count)] if reverse else [(k, k + step) for k in range(count - step)]
        inside = position + step < count if reverse else position >= step
        got_state = lax.ppermute(state.astype(BF), axis, pairs).astype(F32)
        got_total = lax.ppermute(decayed, axis, pairs)
        state = jnp.where(inside, decayed * got_state + state, state)
        decayed = jnp.where(inside, decayed * got_total, decayed)
        step *= 2
    pairs = [(k, k - 1) for k in range(1, count)] if reverse else [(k, k + 1) for k in range(count - 1)]
    return lax.ppermute(state.astype(BF), axis, pairs)


def shards(x_branch, z_gate, b_input, c_input, step_raw, rate_log, step_bias, skip_gain, norm_gain, out_weight, out_grad):
    seqs, length, width = x_branch.shape
    model = out_grad.shape[2]
    heads = rate_log.shape[0]
    state_size = b_input.shape[2]
    x, z, b, c, s, g = x_branch[0], z_gate[0], b_input[0], c_input[0], step_raw[0], out_grad[0]
    n_tm, n_tok, n_rep = lax.axis_size("tm"), lax.axis_size("tok"), lax.axis_size("rep")
    rep, tok, tm = lax.axis_index("rep"), lax.axis_index("tok"), lax.axis_index("tm")
    near = (n_tm, n_tok, n_rep) == (4, 2, 4)
    rows = out_weight.shape[0]
    full = (width, model)
    wide = (length, width)
    place = jnp.stack([tok * n_rep + rep, tm]).astype(jnp.int32)
    core = [(k, k ^ 1) for k in range(4)]
    side = [(k, k ^ 2) for k in range(4)]
    front = [(0, 1), (1, 0)]
    diagonal = [(k, k ^ 6) for k in range(8)]

    raw = (s, rate_log, step_bias, b, x, skip_gain, norm_gain)
    aux_shapes = [((5 * heads, length), F32, near_by), ((8, width), F32, near_by)]
    if near:
        part = (n_tm, state_size // n_tm)
        blocks_of = width // 128
        part_shape = (n_tm, blocks_of * part[1] + 2 * blocks_of, 128)
        aux, params, payload = call(
            payload_kernel, aux_shapes + [(part_shape, BF, away)], raw, name="state", us=3,
        )
        blocks = lax.all_to_all(payload, "tm", 0, 0, tiled=True)
        gc = lax.ppermute(g, "rep", core)
        wx = lax.ppermute(out_weight, "rep", side)
        wy = lax.ppermute(out_weight, "tok", front)
        wd = lax.ppermute(out_weight, ("tok", "rep"), diagonal)
        wc, wxc, wyc, wdc = (lax.ppermute(v, "rep", core) for v in (out_weight, wx, wy, wd))
        (local,) = call(
            inner_kernel, [(wide, F32, near_by)], (b, c, x), aux, params, name="inner", us=5, after=(payload,)
        )
        (prefixes,) = call(prefix_kernel, [(part + (width,), BF, away)], (), blocks, name="prefix", us=1, beside=(local,))
        incoming = lax.all_to_all(prefixes, "tm", 0, 0, tiled=True).reshape(state_size, width)
        pieces = (out_weight, wc, wx, wxc, wy, wyc, wd, wdc)
        weight, ng = call(
            weight_kernel, [(full, BF, away), (wide, BF, near_by)], (*pieces, g), place,
            smem=(0,), name="normed_grad", us=10, after=(prefixes,),
        )
    else:
        aux, params, state, total = call(
            payload_kernel, aux_shapes + [((state_size, width), BF, free), ((1, width), F32, free)], raw, name="state", us=3
        )
        incoming = scan_far(state, total, "tm", False)
        (local,) = call(inner_kernel, [(wide, F32, near_by)], (b, c, x), aux, params, name="inner", us=5)
        weight = lax.all_gather(out_weight, ("tok", "rep"), axis=0, tiled=True)
        (ng,) = call(grad_kernel, [(wide, BF, near_by)], (), g, weight, name="normed_grad", us=10)
    normed, other, inner, factor = call(
        norm_kernel,
        [(wide, BF, near_by), ((length, width // 2), BF, away), (wide, F32, near_by), ((length, 128), F32, near_by)],
        (c, z), place, aux, params, local, incoming, name="norm", us=4, smem=(0,), scratch=[pltpu.VMEM(wide, F32)], after=(weight,),
    )
    dy, carry, zg, row_sums, gains, skips = call(
        norm_back_kernel,
        [
            (wide, BF, away), (part_shape if near else (state_size, width), BF, away), (wide, BF, away),
            ((heads, length), F32, away), ((1, width), F32, away), ((heads, 1), F32, away),
        ],
        (c, z, x), aux, params, inner, factor, ng, name="norm_back", us=6,
        scratch=[pltpu.VMEM(wide, F32)] + [pltpu.VMEM(wide, BF)] * 3,
    )

    def back(*after):
        return call(
            back_kernel,
            [
                (wide, BF, away), ((length, state_size), BF, away), (wide, F32, away), ((length, state_size), BF, away),
                ((heads, length), F32, away),
            ],
            (dy, b, c, x, weight), aux, params, incoming, normed,
            name="back", us=14, scratch=[pltpu.VMEM(wide, F32)], after=after,
        )

    everywhere = ("tm", "tok", "rep")
    ahead = [[(i, (i + k) % n_tm) for i in range(n_tm)] for k in range(1, n_tm)]

    def last(row, far, *more):
        return call(
            last_kernel,
            [(wide, BF, away), ((length, state_size), BF, away), ((heads, length), F32, away), (row, F32, away)],
            (b, x, row_sums, col_sums, bg, xg, skips), aux, later, incoming, *more, name="last", us=6, after=far,
            smem=(3,) if near else (),
        )

    if near:
        block = (rows, model)
        theirs = lax.ppermute(other, "rep", core)
        keep, sx, sy, sd = call(
            outer_kernel, [(block, F32, away)] + [(block, BF, away)] * 3, (g, gc), place, normed, theirs,
            smem=(0,), name="outer", us=4, after=(carry,),
        )
        gx = lax.ppermute(sx, "rep", side)
        gy = lax.ppermute(sy, "tok", front)
        gd = lax.ppermute(sd, ("tok", "rep"), diagonal)
        grads = lax.all_to_all(carry, "tm", 0, 0, tiled=True)
        suffixes, gains = call(
            suffix_kernel, [(part + (width,), BF, away), ((blocks_of, 128), F32, near_by)], (), grads, blocks,
            name="suffix", us=1, after=(keep,),
        )
        later = lax.all_to_all(suffixes, "tm", 0, 0, tiled=True).reshape(state_size, width)
        mixed, c_grad, xg, bg, col_sums = back(suffixes)
        quarter = (rows // n_tm, model)
        own, *sends = call(
            add_kernel, [(quarter, F32, away)] + [(quarter, BF, away)] * (n_tm - 1), (keep,), place, gx, gy, gd,
            smem=(0,), name="add_chips", us=3, scratch=[pltpu.VMEM(block, F32)], after=(col_sums,),
        )
        gots = [lax.ppermute(v, "tm", pairs) for v, pairs in zip(sends, ahead)]
        row = (n_tm * n_tok * n_rep, 1, 128 + width // n_tm)
        x_grad, b_grad, step_grad, sums = last(row, (own,), place, gains)
        (total_quarter,) = call(
            add_quarter_kernel, [(quarter, BF, away)], (own,), *gots, name="add_blocks", us=2, after=(step_grad,)
        )
        quarters = [total_quarter] + [lax.ppermute(total_quarter, "tm", pairs) for pairs in ahead]
        (weight_grad,) = call(join_kernel, [(block, BF, away)], (), place, *quarters, smem=(0,), name="join", us=3)
        sums = lax.all_to_all(sums, everywhere, 0, 0, tiled=True)
    else:
        later = scan_far(carry, total, "tm", True)
        (outer,) = call(outer_full_kernel, [(full, F32, free)], (), normed, g, name="outer", us=4)
        share = lax.psum_scatter(outer, ("tok", "rep"), scatter_dimension=0, tiled=True)
        weight_grad = lax.psum(share, "tm").astype(BF)
        mixed, c_grad, xg, bg, col_sums = back()
        x_grad, b_grad, step_grad, sums = last((1, 1, 128 + width), (), gains)
        sums = lax.psum(sums, everywhere)
    rate_grad, bias_grad, skip_grad, gain_grad = call(
        sums_kernel, [((heads,), F32, away)] * 3 + [((width,), F32, away)], (sums,), name="sums", us=2
    )
    return (
        mixed[None], x_grad[None], zg[None], b_grad[None], c_grad[None], step_grad[None],
        rate_grad, bias_grad, skip_grad, gain_grad, weight_grad,
    )


def solution(mesh):
    tokens = P(("tok", "rep"), "tm", None)
    frames = P(("tok", "rep"), None, "tm")
    weight = P(("tok", "rep"), None)
    return jax.shard_map(
        shards,
        mesh=mesh,
        in_specs=(tokens, tokens, tokens, tokens, frames, P(), P(), P(), P(), weight, tokens),
        out_specs=(tokens, tokens, tokens, tokens, tokens, frames, P(), P(), P(), P(), weight),
        check_vma=False,
    )
```

```python
import functools

import jax
import jax.numpy as jnp
from jax import lax
from jax.experimental import pallas as pl
from jax.experimental.pallas import tpu as pltpu
from jax.sharding import PartitionSpec as P

BF = jnp.bfloat16
F32 = jnp.float32
ROWS = ((0,), (0,))
LAST = ((1,), (1,))
CHUNKS = 8
VMEM_LIMIT = 24 * 1024 * 1024


def mm(a, b):
    return jnp.dot(a, b, preferred_element_type=F32)


def mm_tn(a, b):
    return lax.dot_general(a, b, (ROWS, ((), ())), preferred_element_type=F32)


def mm_nt(a, b):
    return lax.dot_general(a, b, (LAST, ((), ())), preferred_element_type=F32)


def split(v, parts):
    pieces = []
    for _ in range(parts):
        piece = v.astype(BF)
        pieces.append(piece)
        v = v - piece.astype(F32)
    return pieces


def column(ref):
    row = ref[...].reshape(1, -1)
    heads = row.shape[1]
    i = lax.broadcasted_iota(jnp.int32, (heads, heads), 0)
    j = lax.broadcasted_iota(jnp.int32, (heads, heads), 1)
    return jnp.sum(jnp.where(i == j, row, 0.0), axis=1, keepdims=True)


def head_map(heads, width):
    i = lax.broadcasted_iota(jnp.int32, (heads, width), 0)
    j = lax.broadcasted_iota(jnp.int32, (heads, width), 1)
    wide = width // heads
    return jnp.where((j >= i * wide) & (j < (i + 1) * wide), 1.0, 0.0).astype(F32)


def triangle(length, keep):
    i = lax.broadcasted_iota(jnp.int32, (length, length), 0)
    j = lax.broadcasted_iota(jnp.int32, (length, length), 1)
    return jnp.where(keep(i, j), 1.0, 0.0).astype(BF)


def along_frames(v, tri):
    heads = v.shape[0]
    out = mm(jnp.concatenate(split(v, 3), axis=0), tri)
    return out[:heads] + out[heads : 2 * heads] + out[2 * heads :]


def expand(v, hmap):
    return mm_tn(jnp.concatenate(split(v, 2), axis=0), jnp.concatenate([hmap, hmap], axis=0).astype(BF))


def expand_row(col, hmap):
    return jnp.sum(col * hmap, axis=0, keepdims=True)


def head_sums(y, hmap):
    hb = hmap.astype(BF)
    hi, lo = split(y, 2)
    return mm_nt(hb, hi) + mm_nt(hb, lo)


def decay(s_ref, rate_ref, bias_ref):
    v = s_ref[...] + column(bias_ref)
    e = jnp.exp(-jnp.abs(v))
    u = 1.0 + e
    d = u - 1.0
    log1p = jnp.where(d == 0.0, e, jnp.log(u) * (e / jnp.where(d == 0.0, 1.0, d)))
    delta = jnp.maximum(v, 0.0) + log1p
    a = -jnp.exp(column(rate_ref))
    ld = delta * a
    cum = along_frames(ld, triangle(ld.shape[1], lambda i, j: i <= j))
    return v, delta, a, ld, cum


class Coming:
    def __init__(self, source, target, semaphore):
        self.copy = pltpu.make_async_copy(source, target, semaphore)
        self.copy.start()
        self.target, self.waited = target, False

    def ready(self):
        if not self.waited:
            self.copy.wait()
            self.waited = True
        return self.target


def near_by(shape, dtype):
    return pltpu.VMEM(shape, dtype)


def away(shape, dtype):
    return pltpu.HBM(shape, dtype)


def free(shape, dtype):
    return jax.ShapeDtypeStruct(shape, dtype)


def call(kernel, outs, far, *args, smem=(), name=None, scratch=(), after=(), beside=()):
    waits = len(after) + len(beside)
    specs = [pl.BlockSpec(memory_space=pl.ANY)] * len(far)
    specs += [
        pl.BlockSpec(memory_space=pltpu.SMEM if k in smem else pltpu.VMEM) for k in range(len(args))
    ]
    specs += [pl.BlockSpec(memory_space=pl.ANY)] * waits
    first, used = len(far), len(far) + len(args)
    landing = [pltpu.VMEM(v.shape, v.dtype) for v in far]
    semaphores = [pltpu.SemaphoreType.DMA((len(far),))] if far else []

    def body(*refs):
        refs, own = list(refs), len(far)
        coming = []
        if far:
            refs, targets, semaphore = refs[: -own - 1], refs[-own - 1 : -1], refs[-1]
            coming = [Coming(refs[k], targets[k], semaphore.at[k]) for k in range(own)]
        kernel(*coming, *refs[first:used], *refs[used + waits :])
        for one in coming:
            one.ready()

    return pl.pallas_call(
        body,
        out_shape=[where(shape, dtype) for shape, dtype, where in outs],
        in_specs=specs,
        out_specs=[pl.BlockSpec(memory_space=pltpu.VMEM)] * len(outs),
        scratch_shapes=list(scratch) + landing + semaphores,
        compiler_params=pltpu.CompilerParams(vmem_limit_bytes=VMEM_LIMIT),
        name=name,
    )(*[pltpu.with_memory_space_constraint(v, pltpu.HBM) for v in far], *args, *[pltpu.with_memory_space_constraint(v, pltpu.HBM) for v in after], *beside)


def store_decay(aux_ref, rows_ref, v, delta, a, ld, cum, skip, gain):
    heads = cum.shape[0]
    for k, value in enumerate((v, delta, ld, cum, jnp.broadcast_to(a, cum.shape))):
        aux_ref[k * heads : (k + 1) * heads, :] = value
    rows_ref[0:1, :] = skip
    rows_ref[1:2, :] = gain


def load_decay(aux_ref):
    heads = aux_ref.shape[0] // 5
    return [aux_ref[k * heads : (k + 1) * heads, :] for k in range(5)]


def store_parts(out_ref, state, row):
    count, blocks = out_ref.shape[0], row.shape[1] // 128
    rows = state.shape[0] // count
    tail = [v[:, n * 128 : (n + 1) * 128].astype(F32) for v in split(row, 2) for n in range(blocks)]
    tail = jnp.concatenate(tail, axis=0).astype(BF)
    for k in range(count):
        for n in range(blocks):
            out_ref[k, n * rows : (n + 1) * rows, :] = state[k * rows : (k + 1) * rows, n * 128 : (n + 1) * 128]
        out_ref[k, blocks * rows :, :] = tail


def payload_kernel(s_in, rate_in, bias_in, b_in, x_in, skip_in, gain_in, aux_ref, rows_ref, *outs):
    v, delta, a, ld, cum = decay(s_in.ready(), rate_in.ready(), bias_in.ready())
    x_ref, b_ref = x_in.ready(), b_in.ready()
    width = x_ref.shape[1]
    hmap = head_map(cum.shape[0], width)
    skip = expand_row(column(skip_in.ready()), hmap)
    store_decay(aux_ref, rows_ref, v, delta, a, ld, cum, skip, gain_in.ready()[...].reshape(1, -1))
    last = cum[:, -1:]
    tail = expand(jnp.exp(last - cum) * delta, hmap)
    weighted = (x_ref[...].astype(F32) * tail).astype(BF)
    state = mm_tn(b_ref[...], weighted).astype(BF)
    total = expand_row(jnp.exp(last), hmap)
    if len(outs) == 2:
        outs[0][...] = state
        outs[1][...] = total
        return
    (out_ref,) = outs
    store_parts(out_ref, state, total)


def part_decay(all_ref, k, n, rows, blocks):
    pair = all_ref[k, blocks * rows :, :].astype(F32)
    return pair[n : n + 1] + pair[blocks + n : blocks + n + 1]


def prefix_kernel(all_ref, out_ref):
    count, rows, width = out_ref.shape
    blocks = width // 128
    for n in range(blocks):
        cols = slice(n * 128, (n + 1) * 128)
        carried = jnp.zeros((rows, 128), F32)
        for k in range(count):
            out_ref[k, :, cols] = carried.astype(BF)
            if k + 1 < count:
                state = all_ref[k, n * rows : (n + 1) * rows, :].astype(F32)
                carried = state + part_decay(all_ref, k, n, rows, blocks) * carried


def suffix_kernel(grads_ref, all_ref, pos_ref, *refs):
    outs, gains_ref, out_ref = refs[:-2], refs[-2], refs[-1]
    count, rows, width = out_ref.shape
    blocks = width // 128
    for n in range(blocks):
        cols = slice(n * 128, (n + 1) * 128)
        carried = jnp.zeros((rows, 128), F32)
        for k in reversed(range(count)):
            out_ref[k, :, cols] = carried.astype(BF)
            if k > 0:
                grad = grads_ref[k, n * rows : (n + 1) * rows, :].astype(F32)
                carried = grad + part_decay(all_ref, k, n, rows, blocks) * carried
    for k, part_ref in enumerate(outs):
        part_ref[...] = out_ref[lax.rem(pos_ref[1] + k, count)]
    gains = sum(grads_ref[k, blocks * rows :, :].astype(F32) for k in range(count))
    gains_ref[...] = gains[:blocks] + gains[blocks:]


def inner_kernel(b_in, c_in, x_in, aux_ref, rows_ref, inner_ref):
    _, delta, _, cum, _ = load_decay(aux_ref)
    x_ref, b_ref, c_ref = x_in.ready(), b_in.ready(), c_in.ready()
    heads, length = cum.shape
    width = x_ref.shape[1]
    hmap = head_map(heads, width)
    cum_t = cum.T
    x = x_ref[...].astype(F32)
    xd = (x * expand(delta, hmap)).astype(BF)
    skip = rows_ref[0:1, :]
    half = length // 2
    scores = mm_nt(c_ref[...], b_ref[...])
    i = lax.broadcasted_iota(jnp.int32, (half, half), 0)
    j = lax.broadcasted_iota(jnp.int32, (half, half), 1)
    diag = i >= j
    s00 = jnp.where(diag, scores[:half, :half], 0.0)
    s10 = scores[half:, :half]
    s11 = jnp.where(diag, scores[half:, half:], 0.0)
    pair = 2 * (width // heads)
    first = lax.broadcasted_iota(jnp.int32, (half, pair), 1) < pair // 2
    for p in range(heads // 2):
        cols = slice(p * pair, (p + 1) * pair)
        upper, lower = [], []
        for h in (2 * p, 2 * p + 1):
            q0, q1 = cum_t[:half, h : h + 1], cum_t[half:, h : h + 1]
            k0, k1 = cum[h : h + 1, :half], cum[h : h + 1, half:]
            m00 = jnp.exp(jnp.minimum(q0 - k0, 0.0)) * s00
            m10 = jnp.exp(jnp.minimum(q1 - k0, 0.0)) * s10
            m11 = jnp.exp(jnp.minimum(q1 - k1, 0.0)) * s11
            upper.append(m00.astype(BF))
            lower.append(jnp.concatenate([m10.astype(BF), m11.astype(BF)], axis=1))
        y0 = mm(jnp.concatenate(upper, axis=0), xd[:half, cols])
        y1 = mm(jnp.concatenate(lower, axis=0), xd[:, cols])
        inner_ref[:half, cols] = jnp.where(first, y0[:half], y0[half:]) + skip[:, cols] * x[:half, cols]
        inner_ref[half:, cols] = jnp.where(first, y1[:half], y1[half:]) + skip[:, cols] * x[half:, cols]


def weight_kernel(*refs):
    pieces, g_in, idx_ref, full_ref, ng_ref = [v.ready() for v in refs[:8]], *refs[8:]
    me = idx_ref[0]
    rows = pieces[0].shape[0]
    for k, piece in enumerate(pieces):
        full_ref[pl.ds(pl.multiple_of((me ^ k) * rows, rows), rows), :] = piece[...]
    ng_ref[...] = mm_nt(g_in.ready()[...], full_ref[...]).astype(BF)


def grad_kernel(g_ref, full_ref, ng_ref):
    ng_ref[...] = mm_nt(g_ref[...], full_ref[...]).astype(BF)


def norm_kernel(c_in, z_in, idx_ref, aux_ref, params_ref, local_ref, inc_ref, normed_ref, other_ref, inner_ref, factor_ref, ec_ref):
    _, _, _, cum, _ = load_decay(aux_ref)
    c_ref, z_ref = c_in.ready(), z_in.ready()
    heads, length = cum.shape
    width = z_ref.shape[1]
    hmap = head_map(heads, width)
    ec_ref[...] = expand(jnp.exp(cum), hmap)
    inner_ref[...] = mm(c_ref[...], inc_ref[...])
    gain = params_ref[1:2, :]
    step = length // CHUNKS

    for n in range(CHUNKS):
        at = slice(n * step, (n + 1) * step)
        inner = local_ref[at, :] + inner_ref[at, :] * ec_ref[at, :]
        inner_ref[at, :] = inner
        z = z_ref[at, :].astype(F32)
        gated = inner * (z / (1.0 + jnp.exp(-z)))
        r = lax.rsqrt(jnp.mean(gated * gated, axis=1, keepdims=True) + 1e-05)
        factor_ref[at, :] = jnp.broadcast_to(r, (step, 128))
        normed_ref[at, :] = (gated * r * gain).astype(BF)
    block = other_ref.shape[1] // 4
    for k in range(4):
        at = (2 * k + 1 - lax.rem(idx_ref[0], 2)) * block
        other_ref[:, k * block : (k + 1) * block] = normed_ref[:, pl.ds(pl.multiple_of(at, block), block)]


def norm_back_kernel(
    c_in, z_in, x_in, aux_ref, params_ref, inner_ref, factor_ref, ng_ref,
    dy_ref, carry_ref, zg_ref, rows_ref, gains_ref, skips_ref,
    ec_ref, de_ref, hi_ref, lo_ref,
):
    _, _, _, cum, _ = load_decay(aux_ref)
    c_ref, z_ref, x_ref = c_in.ready(), z_in.ready(), x_in.ready()
    heads, length = cum.shape
    width = x_ref.shape[1]
    hmap = head_map(heads, width)
    ec_ref[...] = expand(jnp.exp(cum), hmap)
    skip, gain = params_ref[0:1, :], params_ref[1:2, :]
    step = length // CHUNKS
    gains = jnp.zeros((1, width), F32)
    skips = jnp.zeros((1, width), F32)
    for n in range(CHUNKS):
        at = slice(n * step, (n + 1) * step)
        inner = inner_ref[at, :]
        z = z_ref[at, :].astype(F32)
        sig = 1.0 / (1.0 + jnp.exp(-z))
        silu = z * sig
        r = factor_ref[at, 0:1]
        nhat = inner * silu * r
        ng = ng_ref[at, :].astype(F32)
        prod = ng * nhat
        gains = gains + jnp.sum(prod, axis=0, keepdims=True)
        m = jnp.mean(prod * gain, axis=1, keepdims=True)
        dgated = r * (ng * gain - nhat * m)
        dinner = dgated * silu
        dy = dinner.astype(BF)
        dy_ref[at, :] = dy
        de_ref[at, :] = (dinner * ec_ref[at, :]).astype(BF)
        zg_ref[at, :] = (dgated * inner * (sig + silu * (1.0 - sig))).astype(BF)
        x = x_ref[at, :].astype(F32)
        skips = skips + jnp.sum(dinner * x, axis=0, keepdims=True)
        hi_ref[at, :], lo_ref[at, :] = split(dy.astype(F32) * (inner - skip * x), 2)
    carry = mm_tn(c_ref[...], de_ref[...]).astype(BF)
    if len(carry_ref.shape) == 2:
        carry_ref[...] = carry
    else:
        store_parts(carry_ref, carry, gains)
    hb = hmap.astype(BF)
    rows_ref[...] = mm_nt(hb, hi_ref[...]) + mm_nt(hb, lo_ref[...])
    gains_ref[...] = gains
    skips_ref[...] = jnp.sum(skips * hmap, axis=1, keepdims=True)


def outer_kernel(g_in, gc_in, idx_ref, normed_ref, got_ref, out_ref):
    g_ref, gc_ref = g_in.ready(), gc_in.ready()
    core = lax.rem(idx_ref[0], 2)
    chips, rows = out_ref.shape[:2]
    for k in range(chips):
        mine = pl.ds(pl.multiple_of((2 * k + core) * rows, rows), rows)
        part = mm_tn(normed_ref[:, mine], g_ref[...]) + mm_tn(got_ref[:, k * rows : (k + 1) * rows], gc_ref[...])
        out_ref[k] = part.astype(BF)


def add_kernel(all_ref, out_ref):
    total = all_ref[0].astype(F32)
    for k in range(1, all_ref.shape[0]):
        total = total + all_ref[k].astype(F32)
    total = total.astype(BF)
    rows = out_ref.shape[1]
    for k in range(out_ref.shape[0]):
        out_ref[k] = total[k * rows : (k + 1) * rows]


def mixed_kernel(full_in, normed_ref, mixed_ref):
    mixed_ref[...] = mm(normed_ref[...], full_in.ready()[...]).astype(BF)


def join_kernel(*refs):
    pos_ref, pieces, out_ref = refs[0], refs[1:-1], refs[-1]
    count, rows = len(pieces), pieces[0].shape[0]
    for k, piece in enumerate(pieces):
        at = lax.rem(pos_ref[1] + count - k, count) * rows
        out_ref[pl.ds(pl.multiple_of(at, rows), rows), :] = piece[...]


def outer_full_kernel(normed_ref, g_ref, out_ref):
    out_ref[...] = mm_tn(normed_ref[...], g_ref[...])


def back_kernel(
    dy_in, b_in, c_in, x_in, aux_ref, params_ref, inc_ref,
    cg_ref, xg_ref, bg_ref, cols_ref, dxw_ref,
):
    _, delta, _, cum, _ = load_decay(aux_ref)
    x_ref, b_ref, c_ref = x_in.ready(), b_in.ready(), c_in.ready()
    heads, length = cum.shape
    width = x_ref.shape[1]
    hmap = head_map(heads, width)
    cum_t = cum.T
    delta_e = expand(delta, hmap)
    xd = (x_ref[...].astype(F32) * delta_e).astype(BF)
    dy = dy_in.ready()[...]
    half = length // 2
    scores = mm_nt(b_ref[...], c_ref[...])
    i = lax.broadcasted_iota(jnp.int32, (half, half), 0)
    j = lax.broadcasted_iota(jnp.int32, (half, half), 1)
    diag = j >= i
    s00 = jnp.where(diag, scores[:half, :half], 0.0)
    s01 = scores[:half, half:]
    s11 = jnp.where(diag, scores[half:, half:], 0.0)
    pair = 2 * (width // heads)
    first = lax.broadcasted_iota(jnp.int32, (half, pair), 1) < pair // 2
    whole_first = lax.broadcasted_iota(jnp.int32, (length, pair), 1) < pair // 2
    d00 = jnp.zeros((half, half), F32)
    d01 = jnp.zeros((half, half), F32)
    d11 = jnp.zeros((half, half), F32)
    none = jnp.zeros((length, pair), BF)
    for p in range(heads // 2):
        cols = slice(p * pair, (p + 1) * pair)
        xp, dp = xd[:, cols], dy[:, cols]
        stacked = jnp.concatenate([jnp.where(whole_first, xp, none), jnp.where(whole_first, none, xp)], axis=0)
        dm = mm_nt(stacked, dp)
        upper, lower = [], []
        for n, h in enumerate((2 * p, 2 * p + 1)):
            k0, k1 = cum_t[:half, h : h + 1], cum_t[half:, h : h + 1]
            q0, q1 = cum[h : h + 1, :half], cum[h : h + 1, half:]
            l00 = jnp.exp(jnp.minimum(q0 - k0, 0.0))
            l01 = jnp.exp(jnp.minimum(q1 - k0, 0.0))
            l11 = jnp.exp(jnp.minimum(q1 - k1, 0.0))
            at = n * length
            d00 = d00 + l00 * dm[at : at + half, :half]
            d01 = d01 + l01 * dm[at : at + half, half:]
            d11 = d11 + l11 * dm[at + half : at + length, half:]
            upper.append(jnp.concatenate([(l00 * s00).astype(BF), (l01 * s01).astype(BF)], axis=1))
            lower.append((l11 * s11).astype(BF))
        y0 = mm(jnp.concatenate(upper, axis=0), dp)
        y1 = mm(jnp.concatenate(lower, axis=0), dp[half:])
        dxw_ref[:half, cols] = jnp.where(first, y0[:half], y0[half:])
        dxw_ref[half:, cols] = jnp.where(first, y1[:half], y1[half:])
    d00 = jnp.where(diag, d00, 0.0).astype(BF)
    d01 = d01.astype(BF)
    d11 = jnp.where(diag, d11, 0.0).astype(BF)
    c0, c1 = c_ref[:half, :], c_ref[half:, :]
    b0, b1 = b_ref[:half, :], b_ref[half:, :]
    bg_ref[:half, :] = (mm(d00, c0) + mm(d01, c1)).astype(BF)
    bg_ref[half:, :] = mm(d11, c1).astype(BF)
    ec = expand(jnp.exp(cum), hmap)
    carried = mm_nt((dy.astype(F32) * ec).astype(BF), inc_ref[...])
    cg_ref[:half, :] = (carried[:half] + mm_tn(d00, b0).astype(BF).astype(F32)).astype(BF)
    cg_ref[half:, :] = (carried[half:] + (mm_tn(d01, b0) + mm_tn(d11, b1)).astype(BF).astype(F32)).astype(BF)
    dxw = dxw_ref[...]
    cols_ref[...] = head_sums(xd.astype(F32) * dxw, hmap)
    skip = params_ref[0:1, :]
    xg_ref[...] = delta_e * dxw + skip * dy.astype(F32)


def last_kernel(
    gains_here, b_in, x_in, rows_in, cols_in, bg_in, xg_in, skips_in, pos_ref, aux_ref, inc_ref, *more,
):
    parts, (x_out, b_out, step_out, sums_out, later_ref) = more[:-5], more[-5:]
    gains_ref, parts = (parts[0], parts[1:]) if gains_here else (None, parts)
    count, part = len(parts), parts[0].shape[0]
    for k, one in enumerate(parts):
        at = lax.rem(pos_ref[1] + count - k, count) * part
        later_ref[pl.ds(pl.multiple_of(at, part), part), :] = one[...]
    v, delta, ld, cum, a = load_decay(aux_ref)
    x_ref, b_ref = x_in.ready(), b_in.ready()
    heads, length = cum.shape
    width = x_ref.shape[1]
    hmap = head_map(heads, width)
    last = cum[:, -1:]
    tailing = jnp.exp(last - cum)
    tail = tailing * delta
    tail_e = expand(tail, hmap)
    x = x_ref[...].astype(F32)
    later = later_ref[...]
    dweighted = mm(b_ref[...], later)
    x_out[...] = (xg_in.ready()[...] + tail_e * dweighted).astype(BF)
    weighted = (x * tail_e).astype(BF)
    b_out[...] = (bg_in.ready()[...].astype(F32) + mm_nt(weighted, later)).astype(BF)
    dtail = head_sums(x * dweighted, hmap)
    cross = jnp.sum(later.astype(F32) * inc_ref[...].astype(F32), axis=0, keepdims=True)
    dtotal = jnp.sum(cross * hmap, axis=1, keepdims=True) * jnp.exp(last)
    cols = cols_in.ready()[...]
    dld = along_frames(rows_in.ready()[...] - cols, triangle(length, lambda i, j: i >= j))
    dld = dld + along_frames(dtail * tail, triangle(length, lambda i, j: i < j)) + dtotal
    ddelta = cols / delta + dtail * tailing + a * dld
    dstep = ddelta / (1.0 + jnp.exp(-v))
    step_out[...] = dstep
    drate = jnp.sum(dld * ld, axis=1, keepdims=True)
    dbias = jnp.sum(dstep, axis=1, keepdims=True)
    i = lax.broadcasted_iota(jnp.int32, (heads, 128), 0)
    j = lax.broadcasted_iota(jnp.int32, (heads, 128), 1)

    def lay(col, at):
        return jnp.sum(jnp.where(j == i + at, col, 0.0), axis=0, keepdims=True)

    small = lay(drate, 0) + lay(dbias, heads) + lay(skips_in.ready()[...], 2 * heads)
    if gains_ref is None:
        sums_out[0] = small
        return
    each = gains_ref.shape[0] // count
    shares = [gains_ref[pl.ds(pos_ref[1] * each + n, 1), :] for n in range(each)]
    row = jnp.concatenate([small] + shares, axis=1)
    for k in range(sums_out.shape[0]):
        sums_out[k] = row


def sums_kernel(all_in, rate_out, bias_out, skip_out, gain_out):
    every = all_in.ready()[...]
    heads = rate_out.shape[0]
    small = jnp.sum(every[:, 0, :128], axis=0)
    rate_out[...] = small[:heads]
    bias_out[...] = small[heads : 2 * heads]
    skip_out[...] = small[2 * heads : 3 * heads]
    share = every.shape[2] - 128
    parts = gain_out.shape[0] // share
    group = every.shape[0] // parts
    for k in range(parts):
        gain_out[k * share : (k + 1) * share] = jnp.sum(every[k * group : (k + 1) * group, 0, 128:], axis=0)


def scan_far(value, total, axis, reverse):
    count = lax.axis_size(axis)
    position = lax.axis_index(axis)
    decayed, state = total, value.astype(F32)
    step = 1
    while step < count:
        pairs = [(k, k - step) for k in range(step, count)] if reverse else [(k, k + step) for k in range(count - step)]
        inside = position + step < count if reverse else position >= step
        got_state = lax.ppermute(state.astype(BF), axis, pairs).astype(F32)
        got_total = lax.ppermute(decayed, axis, pairs)
        state = jnp.where(inside, decayed * got_state + state, state)
        decayed = jnp.where(inside, decayed * got_total, decayed)
        step *= 2
    pairs = [(k, k - 1) for k in range(1, count)] if reverse else [(k, k + 1) for k in range(count - 1)]
    return lax.ppermute(state.astype(BF), axis, pairs)


def shards(x_branch, z_gate, b_input, c_input, step_raw, rate_log, step_bias, skip_gain, norm_gain, out_weight, out_grad):
    seqs, length, width = x_branch.shape
    model = out_grad.shape[2]
    heads = rate_log.shape[0]
    state_size = b_input.shape[2]
    x, z, b, c, s, g = x_branch[0], z_gate[0], b_input[0], c_input[0], step_raw[0], out_grad[0]
    n_tm, n_tok, n_rep = lax.axis_size("tm"), lax.axis_size("tok"), lax.axis_size("rep")
    rep, tok, tm = lax.axis_index("rep"), lax.axis_index("tok"), lax.axis_index("tm")
    near = (n_tm, n_tok, n_rep) == (4, 2, 4)
    rows = out_weight.shape[0]
    full = (width, model)
    wide = (length, width)
    place = jnp.stack([tok * n_rep + rep, tm]).astype(jnp.int32)
    core = [(k, k ^ 1) for k in range(4)]
    side = [(k, k ^ 2) for k in range(4)]
    front = [(0, 1), (1, 0)]
    diagonal = [(k, k ^ 6) for k in range(8)]

    raw = (s, rate_log, step_bias, b, x, skip_gain, norm_gain)
    aux_shapes = [((5 * heads, length), F32, near_by), ((8, width), F32, near_by)]
    if near:
        part = (n_tm, state_size // n_tm)
        blocks_of = width // 128
        part_shape = (n_tm, blocks_of * part[1] + 2 * blocks_of, 128)
        aux, params, payload = call(
            payload_kernel, aux_shapes + [(part_shape, BF, away)], raw, name="state",
        )
        blocks = lax.all_to_all(payload, "tm", 0, 0, tiled=True)
        gc = lax.ppermute(g, "rep", core)
        wx = lax.ppermute(out_weight, "rep", side)
        wy = lax.ppermute(out_weight, "tok", front)
        wd = lax.ppermute(out_weight, ("tok", "rep"), diagonal)
        wc, wxc, wyc, wdc = (lax.ppermute(v, "rep", core) for v in (out_weight, wx, wy, wd))
        (local,) = call(
            inner_kernel, [(wide, F32, near_by)], (b, c, x), aux, params, name="inner", after=(payload,)
        )
        (prefixes,) = call(prefix_kernel, [(part + (width,), BF, away)], (), blocks, name="prefix", beside=(local,))
        incoming = lax.all_to_all(prefixes, "tm", 0, 0, tiled=True).reshape(state_size, width)
        pieces = (out_weight, wc, wx, wxc, wy, wyc, wd, wdc)
        weight, ng = call(
            weight_kernel, [(full, BF, away), (wide, BF, near_by)], (*pieces, g), place,
            smem=(0,), name="normed_grad", after=(prefixes,),
        )
    else:
        aux, params, state, total = call(
            payload_kernel, aux_shapes + [((state_size, width), BF, free), ((1, width), F32, free)], raw, name="state"
        )
        incoming = scan_far(state, total, "tm", False)
        (local,) = call(inner_kernel, [(wide, F32, near_by)], (b, c, x), aux, params, name="inner")
        weight = lax.all_gather(out_weight, ("tok", "rep"), axis=0, tiled=True)
        (ng,) = call(grad_kernel, [(wide, BF, near_by)], (), g, weight, name="normed_grad")
    normed, other, inner, factor = call(
        norm_kernel,
        [(wide, BF, near_by), ((length, width // 2), BF, away), (wide, F32, near_by), ((length, 128), F32, near_by)],
        (c, z), place, aux, params, local, incoming, name="norm", smem=(0,), scratch=[pltpu.VMEM(wide, F32)], after=(weight,),
    )
    dy, carry, zg, row_sums, gains, skips = call(
        norm_back_kernel,
        [
            (wide, BF, away), (part_shape if near else (state_size, width), BF, away), (wide, BF, away),
            ((heads, length), F32, away), ((1, width), F32, away), ((heads, 1), F32, away),
        ],
        (c, z, x), aux, params, inner, factor, ng, name="norm_back",
        scratch=[pltpu.VMEM(wide, F32)] + [pltpu.VMEM(wide, BF)] * 3,
    )

    def mixed_of(*after):
        return call(mixed_kernel, [(wide, BF, away)], (weight,), normed, name="mixed", after=after)[0]

    def back(*after):
        return call(
            back_kernel,
            [
                ((length, state_size), BF, away), (wide, F32, away), ((length, state_size), BF, away),
                ((heads, length), F32, away),
            ],
            (dy, b, c, x), aux, params, incoming,
            name="back", scratch=[pltpu.VMEM(wide, F32)], after=after,
        )

    everywhere = ("tm", "tok", "rep")

    def last(row, parts, *more, after=()):
        return call(
            functools.partial(last_kernel, bool(more)),
            [(wide, BF, away), ((length, state_size), BF, away), ((heads, length), F32, away), (row, F32, away)],
            (b, x, row_sums, col_sums, bg, xg, skips), place, aux, incoming, *more, *parts, name="last", after=after,
            smem=(0,), scratch=[pltpu.VMEM((state_size, width), BF)],
        )

    ahead = [[(i, (i + k) % n_tm) for i in range(n_tm)] for k in range(1, n_tm)]
    if near:
        theirs = lax.ppermute(other, "rep", core)
        (products,) = call(
            outer_kernel, [((4, rows, model), BF, away)], (g, gc), place, normed, theirs,
            smem=(0,), name="outer", after=(carry,),
        )
        grads = lax.all_to_all(carry, "tm", 0, 0, tiled=True)
        own, *sends, gains = call(
            suffix_kernel, [(part[1:] + (width,), BF, away)] * n_tm + [((blocks_of, 128), F32, near_by)], (), grads, blocks, place,
            name="suffix", smem=(2,), scratch=[pltpu.VMEM(part + (width,), BF)], after=(products,),
        )
        parts = [own] + [lax.ppermute(v, "tm", pairs) for v, pairs in zip(sends, ahead)]
        (products,) = lax.optimization_barrier((products,))
        chips = lax.all_to_all(
            products, ("tok", "rep"), 0, 0, axis_index_groups=[[0, 2, 4, 6], [1, 3, 5, 7]], tiled=True
        )
        c_grad, xg, bg, col_sums = back(own)
        mixed = mixed_of(col_sums)
        quarters = (n_tm, rows // n_tm, model)
        (share,) = call(add_kernel, [(quarters, BF, away)], (), chips, name="add_chips", after=(mixed,), beside=parts[1:])
        shares = lax.all_to_all(share, "tm", 0, 0, tiled=True)
        row = (n_tm * n_tok * n_rep, 1, 128 + width // n_tm)
        x_grad, b_grad, step_grad, sums = last(row, parts, gains, after=(share,))
        (quarter,) = call(add_kernel, [((1,) + quarters[1:], BF, away)], (), shares, name="add_blocks", after=(step_grad,))
        pieces = [quarter[0]] + [lax.ppermute(quarter[0], "tm", pairs) for pairs in ahead]
        (weight_grad,) = call(join_kernel, [((rows, model), BF, away)], (), place, *pieces, smem=(0,), name="join")
        sums = lax.all_to_all(sums, everywhere, 0, 0, tiled=True)
    else:
        later = scan_far(carry, total, "tm", True)
        (outer,) = call(outer_full_kernel, [(full, F32, free)], (), normed, g, name="outer")
        share = lax.psum_scatter(outer, ("tok", "rep"), scatter_dimension=0, tiled=True)
        weight_grad = lax.psum(share, "tm").astype(BF)
        mixed = mixed_of()
        c_grad, xg, bg, col_sums = back()
        x_grad, b_grad, step_grad, sums = last((1, 1, 128), (later,))
        sums = lax.psum(jnp.concatenate([sums, gains[None]], axis=2), everywhere)
    rate_grad, bias_grad, skip_grad, gain_grad = call(
        sums_kernel, [((heads,), F32, away)] * 3 + [((width,), F32, away)], (sums,), name="sums"
    )
    return (
        mixed[None], x_grad[None], zg[None], b_grad[None], c_grad[None], step_grad[None],
        rate_grad, bias_grad, skip_grad, gain_grad, weight_grad,
    )


def solution(mesh):
    tokens = P(("tok", "rep"), "tm", None)
    frames = P(("tok", "rep"), None, "tm")
    weight = P(("tok", "rep"), None)
    return jax.shard_map(
        shards,
        mesh=mesh,
        in_specs=(tokens, tokens, tokens, tokens, frames, P(), P(), P(), P(), weight, tokens),
        out_specs=(tokens, tokens, tokens, tokens, tokens, frames, P(), P(), P(), P(), weight),
        check_vma=False,
    )
```

```python
import functools

import jax
import jax.numpy as jnp
from jax import lax
from jax.experimental import pallas as pl
from jax.experimental.pallas import tpu as pltpu
from jax.sharding import PartitionSpec as P

BF = jnp.bfloat16
F32 = jnp.float32
ROWS = ((0,), (0,))
LAST = ((1,), (1,))
CHUNKS = 8
VMEM_LIMIT = 24 * 1024 * 1024


def mm(a, b):
    return jnp.dot(a, b, preferred_element_type=F32)


def mm_tn(a, b):
    return lax.dot_general(a, b, (ROWS, ((), ())), preferred_element_type=F32)


def mm_nt(a, b):
    return lax.dot_general(a, b, (LAST, ((), ())), preferred_element_type=F32)


def split(v, parts):
    pieces = []
    for _ in range(parts):
        piece = v.astype(BF)
        pieces.append(piece)
        v = v - piece.astype(F32)
    return pieces


def column(ref):
    row = ref[...].reshape(1, -1)
    heads = row.shape[1]
    i = lax.broadcasted_iota(jnp.int32, (heads, heads), 0)
    j = lax.broadcasted_iota(jnp.int32, (heads, heads), 1)
    return jnp.sum(jnp.where(i == j, row, 0.0), axis=1, keepdims=True)


def head_map(heads, width):
    i = lax.broadcasted_iota(jnp.int32, (heads, width), 0)
    j = lax.broadcasted_iota(jnp.int32, (heads, width), 1)
    wide = width // heads
    return jnp.where((j >= i * wide) & (j < (i + 1) * wide), 1.0, 0.0).astype(F32)


def triangle(length, keep):
    i = lax.broadcasted_iota(jnp.int32, (length, length), 0)
    j = lax.broadcasted_iota(jnp.int32, (length, length), 1)
    return jnp.where(keep(i, j), 1.0, 0.0).astype(BF)


def along_frames(v, tri):
    heads = v.shape[0]
    out = mm(jnp.concatenate(split(v, 3), axis=0), tri)
    return out[:heads] + out[heads : 2 * heads] + out[2 * heads :]


def expand(v, hmap):
    return mm_tn(jnp.concatenate(split(v, 2), axis=0), jnp.concatenate([hmap, hmap], axis=0).astype(BF))


def expand_row(col, hmap):
    return jnp.sum(col * hmap, axis=0, keepdims=True)


def head_sums(y, hmap):
    hb = hmap.astype(BF)
    hi, lo = split(y, 2)
    return mm_nt(hb, hi) + mm_nt(hb, lo)


def decay(s_ref, rate_ref, bias_ref):
    v = s_ref[...] + column(bias_ref)
    e = jnp.exp(-jnp.abs(v))
    u = 1.0 + e
    d = u - 1.0
    log1p = jnp.where(d == 0.0, e, jnp.log(u) * (e / jnp.where(d == 0.0, 1.0, d)))
    delta = jnp.maximum(v, 0.0) + log1p
    a = -jnp.exp(column(rate_ref))
    ld = delta * a
    cum = along_frames(ld, triangle(ld.shape[1], lambda i, j: i <= j))
    return v, delta, a, ld, cum


class Coming:
    def __init__(self, source, target, semaphore):
        self.copy = pltpu.make_async_copy(source, target, semaphore)
        self.copy.start()
        self.target, self.waited = target, False

    def ready(self):
        if not self.waited:
            self.copy.wait()
            self.waited = True
        return self.target


def near_by(shape, dtype):
    return pltpu.VMEM(shape, dtype)


def away(shape, dtype):
    return pltpu.HBM(shape, dtype)


def free(shape, dtype):
    return jax.ShapeDtypeStruct(shape, dtype)


def call(kernel, outs, far, *args, name=None, scratch=(), after=(), beside=(), aliases=None, far_operands=(), held=0, loose=False):
    waits = len(after) + len(beside)

    def fix(v):
        return v if loose else pltpu.with_memory_space_constraint(v, pltpu.HBM)

    far_operands = (*far_operands, *range(len(args) - held, len(args)))
    args = args[: len(args) - held] + tuple(fix(v) for v in args[len(args) - held :])
    specs = [pl.BlockSpec(memory_space=pl.ANY)] * len(far)
    specs += [
        pl.BlockSpec(memory_space=pl.ANY if k in far_operands else pltpu.VMEM) for k in range(len(args))
    ]
    specs += [pl.BlockSpec(memory_space=pl.ANY)] * waits
    first, used = len(far), len(far) + len(args)
    landing = [pltpu.VMEM(v.shape, v.dtype) for v in far]
    semaphores = [pltpu.SemaphoreType.DMA((len(far),))] if far else []

    def body(*refs):
        refs, own = list(refs), len(far)
        coming = []
        if far:
            refs, targets, semaphore = refs[: -own - 1], refs[-own - 1 : -1], refs[-1]
            coming = [Coming(refs[k], targets[k], semaphore.at[k]) for k in range(own)]
        kernel(*coming, *refs[first:used], *refs[used + waits :])
        for one in coming:
            one.ready()

    return pl.pallas_call(
        body,
        out_shape=[where(shape, dtype) for shape, dtype, where in outs],
        in_specs=specs,
        out_specs=[
            pl.BlockSpec(memory_space=pl.ANY if k in (aliases or {}).values() else pltpu.VMEM) for k in range(len(outs))
        ],
        scratch_shapes=list(scratch) + landing + semaphores,
        input_output_aliases=aliases or {},
        compiler_params=pltpu.CompilerParams(vmem_limit_bytes=VMEM_LIMIT),
        name=name,
    )(*[fix(v) for v in far], *args, *[pltpu.with_memory_space_constraint(v, pltpu.HBM) for v in after], *beside)


def store_decay(aux_ref, rows_ref, v, delta, a, ld, cum, skip, gain):
    heads = cum.shape[0]
    for k, value in enumerate((v, delta, ld, cum, jnp.broadcast_to(a, cum.shape))):
        aux_ref[k * heads : (k + 1) * heads, :] = value
    rows_ref[0:1, :] = skip
    rows_ref[1:2, :] = gain


def load_decay(aux_ref):
    heads = aux_ref.shape[0] // 5
    return [aux_ref[k * heads : (k + 1) * heads, :] for k in range(5)]


def store_parts(out_ref, state, row):
    count, blocks = out_ref.shape[0], row.shape[1] // 128
    rows = state.shape[0] // count
    tail = [v[:, n * 128 : (n + 1) * 128].astype(F32) for v in split(row, 2) for n in range(blocks)]
    tail = jnp.concatenate(tail, axis=0).astype(BF)
    for k in range(count):
        for n in range(blocks):
            out_ref[k, n * rows : (n + 1) * rows, :] = state[k * rows : (k + 1) * rows, n * 128 : (n + 1) * 128]
        out_ref[k, blocks * rows :, :] = tail


def payload_kernel(s_in, rate_in, bias_in, b_in, x_in, skip_in, gain_in, w_in, aux_ref, rows_ref, w_ref, *outs):
    v, delta, a, ld, cum = decay(s_in.ready(), rate_in.ready(), bias_in.ready())
    x_ref, b_ref = x_in.ready(), b_in.ready()
    width = x_ref.shape[1]
    hmap = head_map(cum.shape[0], width)
    skip = expand_row(column(skip_in.ready()), hmap)
    store_decay(aux_ref, rows_ref, v, delta, a, ld, cum, skip, gain_in.ready()[...].reshape(1, -1))
    last = cum[:, -1:]
    tail = expand(jnp.exp(last - cum) * delta, hmap)
    weighted = (x_ref[...].astype(F32) * tail).astype(BF)
    state = mm_tn(b_ref[...], weighted).astype(BF)
    total = expand_row(jnp.exp(last), hmap)
    w_ref[...] = w_in.ready()[...]
    if len(outs) == 2:
        outs[0][...] = state
        outs[1][...] = total
        return
    outs, out_ref = outs[:-1], outs[-1]
    store_parts(out_ref, state, total)
    for k, part_ref in enumerate(outs):
        part_ref[...] = out_ref[turn(k, len(outs))]


def turn(k, count):
    return lax.rem(lax.axis_index("tm") + k + count, count)


def prefix_kernel(*refs):
    gots, (out_ref, decays_ref, all_ref) = refs[:-3], refs[-3:]
    count, rows, width = out_ref.shape
    for k, got in enumerate(gots):
        all_ref[turn(-k, count)] = got[...]
    blocks = width // 128
    decays = []
    for k in range(count):
        pair = all_ref[k, blocks * rows :, :].astype(F32)
        decays.append(pair[:blocks] + pair[blocks:])
        decays_ref[k * blocks : (k + 1) * blocks, :] = decays[k]
    for n in range(blocks):
        cols = slice(n * 128, (n + 1) * 128)
        carried = jnp.zeros((rows, 128), F32)
        for k in range(count):
            out_ref[k, :, cols] = carried.astype(BF)
            if k + 1 < count:
                state = all_ref[k, n * rows : (n + 1) * rows, :].astype(F32)
                carried = state + decays[k][n : n + 1] * carried


def gather_rows(parts, out_ref):
    count, rows = len(parts), parts[0].shape[0]
    for k, one in enumerate(parts):
        out_ref[pl.ds(pl.multiple_of(turn(-k, count) * rows, rows), rows), :] = one[...]


def suffix_kernel(decays_ref, *refs):
    count = (len(refs) - 3) // 2
    gots, outs, (gains_ref, out_ref, all_ref) = refs[:count], refs[count:-3], refs[-3:]
    _, rows, width = out_ref.shape
    blocks = width // 128
    for k, got in enumerate(gots):
        all_ref[turn(-k, count)] = got[...]
    decays = decays_ref[...]
    for n in range(blocks):
        cols = slice(n * 128, (n + 1) * 128)
        carried = jnp.zeros((rows, 128), F32)
        for k in reversed(range(count)):
            out_ref[k, :, cols] = carried.astype(BF)
            if k > 0:
                grad = all_ref[k, n * rows : (n + 1) * rows, :].astype(F32)
                carried = grad + decays[k * blocks + n : k * blocks + n + 1] * carried
    for k, part_ref in enumerate(outs):
        part_ref[...] = out_ref[turn(k, count)]
    gains = sum(all_ref[k, blocks * rows :, :].astype(F32) for k in range(count))
    gains_ref[...] = gains[:blocks] + gains[blocks:]


def inner_kernel(b_in, c_in, x_in, aux_ref, rows_ref, inner_ref):
    _, delta, _, cum, _ = load_decay(aux_ref)
    x_ref, b_ref, c_ref = x_in.ready(), b_in.ready(), c_in.ready()
    heads, length = cum.shape
    width = x_ref.shape[1]
    hmap = head_map(heads, width)
    cum_t = cum.T
    x = x_ref[...].astype(F32)
    xd = (x * expand(delta, hmap)).astype(BF)
    skip = rows_ref[0:1, :]
    half = length // 2
    scores = mm_nt(c_ref[...], b_ref[...])
    i = lax.broadcasted_iota(jnp.int32, (half, half), 0)
    j = lax.broadcasted_iota(jnp.int32, (half, half), 1)
    diag = i >= j
    s00 = jnp.where(diag, scores[:half, :half], 0.0)
    s10 = scores[half:, :half]
    s11 = jnp.where(diag, scores[half:, half:], 0.0)
    pair = 2 * (width // heads)
    first = lax.broadcasted_iota(jnp.int32, (half, pair), 1) < pair // 2
    for p in range(heads // 2):
        cols = slice(p * pair, (p + 1) * pair)
        upper, lower = [], []
        for h in (2 * p, 2 * p + 1):
            q0, q1 = cum_t[:half, h : h + 1], cum_t[half:, h : h + 1]
            k0, k1 = cum[h : h + 1, :half], cum[h : h + 1, half:]
            m00 = jnp.exp(jnp.minimum(q0 - k0, 0.0)) * s00
            m10 = jnp.exp(jnp.minimum(q1 - k0, 0.0)) * s10
            m11 = jnp.exp(jnp.minimum(q1 - k1, 0.0)) * s11
            upper.append(m00.astype(BF))
            lower.append(jnp.concatenate([m10.astype(BF), m11.astype(BF)], axis=1))
        y0 = mm(jnp.concatenate(upper, axis=0), xd[:half, cols])
        y1 = mm(jnp.concatenate(lower, axis=0), xd[:, cols])
        inner_ref[:half, cols] = jnp.where(first, y0[:half], y0[half:]) + skip[:, cols] * x[:half, cols]
        inner_ref[half:, cols] = jnp.where(first, y1[:half], y1[half:]) + skip[:, cols] * x[half:, cols]


def unit():
    return lax.axis_index("tok") * lax.axis_size("rep") + lax.axis_index("rep")


def weight_pieces(refs, full_ref, semaphore):
    copies = []
    for k, piece in enumerate(refs):
        rows = piece.shape[0]
        at = pl.ds(pl.multiple_of((unit() ^ k) * rows, rows), rows) if len(refs) > 1 else pl.ds(0, rows)
        copies.append(Coming(piece, full_ref.at[at, :], semaphore.at[k]))
    return copies


def weight_kernel(g_in, *refs):
    pieces, (ng_ref, full_ref, semaphore) = refs[:-3], refs[-3:]
    copies = weight_pieces(pieces, full_ref, semaphore)
    g = g_in.ready()[...]
    for one in copies:
        one.ready()
    ng_ref[...] = mm_nt(g, full_ref[...]).astype(BF)


def norm_kernel(
    c_in, z_in, x_in, aux_ref, params_ref, local_ref, ng_ref, inc_ref,
    normed_ref, other_ref, dy_ref, zg_ref, rows_ref, sums_ref, *refs,
):
    carries, (all_ref, inner_ref, ec_ref, de_ref, hi_ref, lo_ref) = refs[:-6], refs[-6:]
    _, _, _, cum, _ = load_decay(aux_ref)
    c_ref, z_ref, x_ref = c_in.ready(), z_in.ready(), x_in.ready()
    heads, length = cum.shape
    width = x_ref.shape[1]
    hmap = head_map(heads, width)
    ec_ref[...] = expand(jnp.exp(cum), hmap)
    inner_ref[...] = mm(c_ref[...], inc_ref[...])
    skip, gain = params_ref[0:1, :], params_ref[1:2, :]
    step = length // CHUNKS
    gains = jnp.zeros((1, width), F32)
    skips = jnp.zeros((1, width), F32)
    for n in range(CHUNKS):
        at = slice(n * step, (n + 1) * step)
        ec = ec_ref[at, :]
        inner = local_ref[at, :] + inner_ref[at, :] * ec
        z = z_ref[at, :].astype(F32)
        sig = 1.0 / (1.0 + jnp.exp(-z))
        silu = z * sig
        gated = inner * silu
        r = lax.rsqrt(jnp.mean(gated * gated, axis=1, keepdims=True) + 1e-05)
        nhat = gated * r
        normed_ref[at, :] = (nhat * gain).astype(BF)
        ng = ng_ref[at, :].astype(F32)
        prod = ng * nhat
        gains = gains + jnp.sum(prod, axis=0, keepdims=True)
        m = jnp.mean(prod * gain, axis=1, keepdims=True)
        dgated = r * (ng * gain - nhat * m)
        dinner = dgated * silu
        dy = dinner.astype(BF)
        dy_ref[at, :] = dy
        de_ref[at, :] = (dinner * ec).astype(BF)
        zg_ref[at, :] = (dgated * inner * (sig + silu * (1.0 - sig))).astype(BF)
        x = x_ref[at, :].astype(F32)
        skips = skips + jnp.sum(dinner * x, axis=0, keepdims=True)
        hi_ref[at, :], lo_ref[at, :] = split(dy.astype(F32) * (inner - skip * x), 2)
    carry = mm_tn(c_ref[...], de_ref[...]).astype(BF)
    if len(carries) == 1:
        carries[0][...] = carry
    else:
        store_parts(all_ref, carry, gains)
        for k, part_ref in enumerate(carries):
            part_ref[...] = all_ref[turn(k, len(carries))]
    hb = hmap.astype(BF)
    rows_ref[...] = mm_nt(hb, hi_ref[...]) + mm_nt(hb, lo_ref[...])
    sums_ref[0:1, :] = gains
    sums_ref[1:2, :] = skips
    block = other_ref.shape[1] // 4
    for k in range(4):
        at = (2 * k + 1 - lax.rem(lax.axis_index("rep"), 2)) * block
        other_ref[:, k * block : (k + 1) * block] = normed_ref[:, pl.ds(pl.multiple_of(at, block), block)]


def outer_kernel(g_in, gc_in, normed_ref, got_ref, out_ref):
    g_ref, gc_ref = g_in.ready(), gc_in.ready()
    core = lax.rem(lax.axis_index("rep"), 2)
    chips, rows = out_ref.shape[:2]
    for k in range(chips):
        mine = pl.ds(pl.multiple_of((2 * k + core) * rows, rows), rows)
        part = mm_tn(normed_ref[:, mine], g_ref[...]) + mm_tn(got_ref[:, k * rows : (k + 1) * rows], gc_ref[...])
        out_ref[k] = part.astype(BF)


def share_kernel(all_ref, *refs):
    outs, total_ref = refs[:-1], refs[-1]
    total = all_ref[0].astype(F32)
    for k in range(1, all_ref.shape[0]):
        total = total + all_ref[k].astype(F32)
    total_ref[...] = total
    rows = outs[0].shape[0]
    for k, out_ref in enumerate(outs):
        part = total_ref[pl.ds(pl.multiple_of(turn(max(k - 1, 0), len(outs) - 1) * rows, rows), rows), :]
        out_ref[...] = part.astype(out_ref.dtype)


def add_kernel(*refs):
    own_ref, gots, out_ref = refs[0], refs[1:-1], refs[-1]
    total = own_ref[...]
    for got in gots:
        total = total + got[...].astype(F32)
    out_ref[...] = total.astype(BF)


def mixed_kernel(weight_in, normed_ref, mixed_ref):
    mixed_ref[...] = mm(normed_ref[...], weight_in.ready()[...]).astype(BF)


def join_kernel(own_in, *refs):
    gather_rows((own_in.ready(),) + refs[:-1], refs[-1])


def outer_full_kernel(normed_ref, g_ref, out_ref):
    out_ref[...] = mm_tn(normed_ref[...], g_ref[...])


def back_kernel(
    dy_in, b_in, c_in, x_in, aux_ref, params_ref, inc_ref,
    cg_ref, xg_ref, bg_ref, cols_ref, dxw_ref,
):
    _, delta, _, cum, _ = load_decay(aux_ref)
    x_ref, b_ref, c_ref = x_in.ready(), b_in.ready(), c_in.ready()
    dy_ref = dy_in.ready()
    heads, length = cum.shape
    width = x_ref.shape[1]
    hmap = head_map(heads, width)
    cum_t = cum.T
    delta_e = expand(delta, hmap)
    xd = (x_ref[...].astype(F32) * delta_e).astype(BF)
    dy = dy_ref[...]
    half = length // 2
    scores = mm_nt(b_ref[...], c_ref[...])
    i = lax.broadcasted_iota(jnp.int32, (half, half), 0)
    j = lax.broadcasted_iota(jnp.int32, (half, half), 1)
    diag = j >= i
    s00 = jnp.where(diag, scores[:half, :half], 0.0)
    s01 = scores[:half, half:]
    s11 = jnp.where(diag, scores[half:, half:], 0.0)
    pair = 2 * (width // heads)
    first = lax.broadcasted_iota(jnp.int32, (half, pair), 1) < pair // 2
    whole_first = lax.broadcasted_iota(jnp.int32, (length, pair), 1) < pair // 2
    d00 = jnp.zeros((half, half), F32)
    d01 = jnp.zeros((half, half), F32)
    d11 = jnp.zeros((half, half), F32)
    none = jnp.zeros((length, pair), BF)
    for p in range(heads // 2):
        cols = slice(p * pair, (p + 1) * pair)
        xp, dp = xd[:, cols], dy[:, cols]
        stacked = jnp.concatenate([jnp.where(whole_first, xp, none), jnp.where(whole_first, none, xp)], axis=0)
        dm = mm_nt(stacked, dp)
        upper, lower = [], []
        for n, h in enumerate((2 * p, 2 * p + 1)):
            k0, k1 = cum_t[:half, h : h + 1], cum_t[half:, h : h + 1]
            q0, q1 = cum[h : h + 1, :half], cum[h : h + 1, half:]
            l00 = jnp.exp(jnp.minimum(q0 - k0, 0.0))
            l01 = jnp.exp(jnp.minimum(q1 - k0, 0.0))
            l11 = jnp.exp(jnp.minimum(q1 - k1, 0.0))
            at = n * length
            d00 = d00 + l00 * dm[at : at + half, :half]
            d01 = d01 + l01 * dm[at : at + half, half:]
            d11 = d11 + l11 * dm[at + half : at + length, half:]
            upper.append(jnp.concatenate([(l00 * s00).astype(BF), (l01 * s01).astype(BF)], axis=1))
            lower.append((l11 * s11).astype(BF))
        y0 = mm(jnp.concatenate(upper, axis=0), dp)
        y1 = mm(jnp.concatenate(lower, axis=0), dp[half:])
        dxw_ref[:half, cols] = jnp.where(first, y0[:half], y0[half:])
        dxw_ref[half:, cols] = jnp.where(first, y1[:half], y1[half:])
    d00 = jnp.where(diag, d00, 0.0).astype(BF)
    d01 = d01.astype(BF)
    d11 = jnp.where(diag, d11, 0.0).astype(BF)
    c0, c1 = c_ref[:half, :], c_ref[half:, :]
    b0, b1 = b_ref[:half, :], b_ref[half:, :]
    bg_ref[:half, :] = (mm(d00, c0) + mm(d01, c1)).astype(BF)
    bg_ref[half:, :] = mm(d11, c1).astype(BF)
    ec = expand(jnp.exp(cum), hmap)
    carried = mm_nt((dy.astype(F32) * ec).astype(BF), inc_ref[...])
    cg_ref[:half, :] = (carried[:half] + mm_tn(d00, b0).astype(BF).astype(F32)).astype(BF)
    cg_ref[half:, :] = (carried[half:] + (mm_tn(d01, b0) + mm_tn(d11, b1)).astype(BF).astype(F32)).astype(BF)
    dxw = dxw_ref[...]
    cols_ref[...] = head_sums(xd.astype(F32) * dxw, hmap)
    skip = params_ref[0:1, :]
    xg_ref[...] = delta_e * dxw + skip * dy.astype(F32)


def last_kernel(
    gains_here, b_in, x_in, rows_in, cols_in, bg_in, xg_in, sums_in, aux_ref, inc_ref, *more,
):
    parts, (x_out, b_out, step_out, sums_out, later_ref) = more[:-5], more[-5:]
    gains_ref, parts = (parts[0], parts[1:]) if gains_here else (None, parts)
    count = len(parts)
    if count > 1:
        gather_rows(parts, later_ref)
    else:
        later_ref[...] = parts[0][...]
    v, delta, ld, cum, a = load_decay(aux_ref)
    x_ref, b_ref = x_in.ready(), b_in.ready()
    heads, length = cum.shape
    width = x_ref.shape[1]
    hmap = head_map(heads, width)
    last = cum[:, -1:]
    tailing = jnp.exp(last - cum)
    tail = tailing * delta
    tail_e = expand(tail, hmap)
    x = x_ref[...].astype(F32)
    later = later_ref[...]
    dweighted = mm(b_ref[...], later)
    x_out[...] = (xg_in.ready()[...] + tail_e * dweighted).astype(BF)
    weighted = (x * tail_e).astype(BF)
    b_out[...] = (bg_in.ready()[...].astype(F32) + mm_nt(weighted, later)).astype(BF)
    dtail = head_sums(x * dweighted, hmap)
    cross = jnp.sum(later.astype(F32) * inc_ref[...].astype(F32), axis=0, keepdims=True)
    dtotal = jnp.sum(cross * hmap, axis=1, keepdims=True) * jnp.exp(last)
    cols = cols_in.ready()[...]
    dld = along_frames(rows_in.ready()[...] - cols, triangle(length, lambda i, j: i >= j))
    dld = dld + along_frames(dtail * tail, triangle(length, lambda i, j: i < j)) + dtotal
    ddelta = cols / delta + dtail * tailing + a * dld
    dstep = ddelta / (1.0 + jnp.exp(-v))
    step_out[...] = dstep
    drate = jnp.sum(dld * ld, axis=1, keepdims=True)
    dbias = jnp.sum(dstep, axis=1, keepdims=True)
    i = lax.broadcasted_iota(jnp.int32, (heads, 128), 0)
    j = lax.broadcasted_iota(jnp.int32, (heads, 128), 1)

    def lay(col, at):
        return jnp.sum(jnp.where(j == i + at, col, 0.0), axis=0, keepdims=True)

    small = lay(drate, 0) + lay(dbias, heads) + lay(jnp.sum(sums_in.ready()[1:2, :] * hmap, axis=1, keepdims=True), 2 * heads)
    if gains_ref is None:
        sums_out[0] = small
        return
    each = gains_ref.shape[0] // count
    shares = [gains_ref[pl.ds(lax.axis_index("tm") * each + n, 1), :] for n in range(each)]
    row = jnp.concatenate([small] + shares, axis=1)
    for k in range(sums_out.shape[0]):
        sums_out[k] = row


def sums_kernel(all_in, rate_out, bias_out, skip_out, gain_out):
    every = all_in.ready()[...]
    heads = rate_out.shape[0]
    small = jnp.sum(every[:, 0, :128], axis=0)
    rate_out[...] = small[:heads]
    bias_out[...] = small[heads : 2 * heads]
    skip_out[...] = small[2 * heads : 3 * heads]
    share = every.shape[2] - 128
    parts = gain_out.shape[0] // share
    group = every.shape[0] // parts
    for k in range(parts):
        gain_out[k * share : (k + 1) * share] = jnp.sum(every[k * group : (k + 1) * group, 0, 128:], axis=0)


def scan_far(value, total, axis, reverse):
    count = lax.axis_size(axis)
    position = lax.axis_index(axis)
    decayed, state = total, value.astype(F32)
    step = 1
    while step < count:
        pairs = [(k, k - step) for k in range(step, count)] if reverse else [(k, k + step) for k in range(count - step)]
        inside = position + step < count if reverse else position >= step
        got_state = lax.ppermute(state.astype(BF), axis, pairs).astype(F32)
        got_total = lax.ppermute(decayed, axis, pairs)
        state = jnp.where(inside, decayed * got_state + state, state)
        decayed = jnp.where(inside, decayed * got_total, decayed)
        step *= 2
    pairs = [(k, k - 1) for k in range(1, count)] if reverse else [(k, k + 1) for k in range(count - 1)]
    return lax.ppermute(state.astype(BF), axis, pairs)


def shards(x_branch, z_gate, b_input, c_input, step_raw, rate_log, step_bias, skip_gain, norm_gain, out_weight, out_grad):
    seqs, length, width = x_branch.shape
    model = out_grad.shape[2]
    heads = rate_log.shape[0]
    state_size = b_input.shape[2]
    x, z, b, c, s, g = x_branch[0], z_gate[0], b_input[0], c_input[0], step_raw[0], out_grad[0]
    n_tm, n_tok, n_rep = lax.axis_size("tm"), lax.axis_size("tok"), lax.axis_size("rep")
    near = (n_tm, n_tok, n_rep) == (4, 2, 4)
    rows = out_weight.shape[0]
    full = (width, model)
    wide = (length, width)
    core = [(k, k ^ 1) for k in range(4)]
    side = [(k, k ^ 2) for k in range(4)]
    front = [(0, 1), (1, 0)]
    diagonal = [(k, k ^ 6) for k in range(8)]
    ahead = [[(i, (i + k) % n_tm) for i in range(n_tm)] for k in range(1, n_tm)]

    raw = (s, rate_log, step_bias, b, x, skip_gain, norm_gain, out_weight)
    aux_shapes = [((5 * heads, length), F32, near_by), ((8, width), F32, near_by), (out_weight.shape, BF, away)]
    if near:
        part = (n_tm, state_size // n_tm)
        row_part = (part[1], width)
        blocks_of = width // 128
        part_shape = (n_tm, blocks_of * part[1] + 2 * blocks_of, 128)
        aux, params, out_weight, *payload = call(
            payload_kernel, aux_shapes + [(part_shape[1:], BF, away)] * n_tm, raw, name="state",
            scratch=[pltpu.VMEM(part_shape, BF)],
        )
        blocks = [payload[0]] + [lax.ppermute(v, "tm", pairs) for v, pairs in zip(payload[1:], ahead)]
        gc = lax.ppermute(g, "rep", core)
        wx = lax.ppermute(out_weight, "rep", side)
        wy = lax.ppermute(out_weight, "tok", front)
        wd = lax.ppermute(out_weight, ("tok", "rep"), diagonal)
        wc, wxc, wyc, wdc = (lax.ppermute(v, "rep", core) for v in (out_weight, wx, wy, wd))
        (local,) = call(
            inner_kernel, [(wide, F32, near_by)], (b, c, x), aux, params, name="inner", after=(payload[0],)
        )
        prefixes, decays = call(
            prefix_kernel, [(part + (width,), BF, away), ((n_tm * blocks_of, 128), F32, near_by)], (), *blocks,
            name="prefix", beside=(local,), scratch=[pltpu.VMEM(part_shape, BF)],
        )
        incoming = lax.all_to_all(prefixes, "tm", 0, 0, tiled=True).reshape(state_size, width)
        pieces = (out_weight, wc, wx, wxc, wy, wyc, wd, wdc)
        after = (prefixes,)
    else:
        aux, params, out_weight, state, total = call(
            payload_kernel, aux_shapes + [((state_size, width), BF, free), ((1, width), F32, free)], raw, name="state"
        )
        incoming = scan_far(state, total, "tm", False)
        (local,) = call(inner_kernel, [(wide, F32, near_by)], (b, c, x), aux, params, name="inner")
        pieces = (lax.all_gather(out_weight, ("tok", "rep"), axis=0, tiled=True),)
        after = ()
    ng, weight = call(
        weight_kernel, [(wide, BF, near_by), (full, BF, away)], (g,), *pieces, name="normed_grad", after=after, held=len(pieces), loose=True,
        scratch=[pltpu.SemaphoreType.DMA((len(pieces),))],
    )
    normed, other, dy, zg, row_sums, gains, *carry = call(
        norm_kernel,
        [
            (wide, BF, near_by), ((length, width // 2), BF, away), (wide, BF, away),
            (wide, BF, away), ((heads, length), F32, away), ((8, width), F32, away),
        ]
        + ([(part_shape[1:], BF, away)] * n_tm if near else [((state_size, width), BF, away)]),
        (c, z, x), aux, params, local, ng, incoming, name="norm",
        scratch=[pltpu.VMEM(part_shape if near else (8, 128), BF)] + [pltpu.VMEM(wide, F32)] * 2 + [pltpu.VMEM(wide, BF)] * 3,
    )

    def mixed_of(*after):
        return call(mixed_kernel, [(wide, BF, away)], (weight,), normed, name="mixed", after=after)[0]

    def back(*after):
        return call(
            back_kernel,
            [
                ((length, state_size), BF, away), (wide, F32, away), ((length, state_size), BF, away),
                ((heads, length), F32, away),
            ],
            (dy, b, c, x), aux, params, incoming, name="back", after=after, scratch=[pltpu.VMEM(wide, F32)],
        )

    everywhere = ("tm", "tok", "rep")

    def last(row, parts, *more, after=()):
        return call(
            functools.partial(last_kernel, bool(more)),
            [(wide, BF, away), ((length, state_size), BF, away), ((heads, length), F32, away), (row, F32, away)],
            (b, x, row_sums, col_sums, bg, xg, gains), aux, incoming, *more, *parts, name="last", after=after,
            scratch=[pltpu.VMEM((state_size, width), BF)],
        )

    if near:
        theirs = lax.ppermute(other, "rep", core)
        (products,) = call(
            outer_kernel, [((4, rows, model), BF, away)], (g, gc), normed, theirs, name="outer", after=(carry[0],)
        )
        grads = [carry[0]] + [lax.ppermute(v, "tm", pairs) for v, pairs in zip(carry[1:], ahead)]
        mixed = mixed_of(products)
        own, *sends, gains_tm = call(
            suffix_kernel, [(row_part, BF, away)] * n_tm + [((blocks_of, 128), F32, near_by)], (),
            decays, *grads, name="suffix", scratch=[pltpu.VMEM(part + (width,), BF), pltpu.VMEM(part_shape, BF)], after=(mixed,),
        )
        parts = [own] + [lax.ppermute(v, "tm", pairs) for v, pairs in zip(sends, ahead)]
        chips = lax.all_to_all(
            products, ("tok", "rep"), 0, 0, axis_index_groups=[[0, 2, 4, 6], [1, 3, 5, 7]], tiled=True
        )
        c_grad, xg, bg, col_sums = back(own)
        quarter = (rows // n_tm, model)
        own, token, *sends = call(
            share_kernel, [(quarter, F32, near_by), (quarter, BF, away)] + [(quarter, BF, away)] * (n_tm - 1), (), chips, name="add_chips",
            after=(col_sums,), beside=parts[1:], scratch=[pltpu.VMEM((rows, model), F32)],
        )
        shares = [lax.ppermute(v, "tm", pairs) for v, pairs in zip(sends, ahead)]
        row = (n_tm * n_tok * n_rep, 1, 128 + width // n_tm)
        x_grad, b_grad, step_grad, sums = last(row, parts, gains_tm, after=(token,))
        (quarter,) = call(add_kernel, [(quarter, BF, away)], (), own, *shares, name="add_blocks", after=(step_grad,))
        pieces = [lax.ppermute(quarter, "tm", pairs) for pairs in ahead]
        (weight_grad,) = call(join_kernel, [((rows, model), BF, away)], (quarter,), *pieces, name="join")
        sums = lax.all_to_all(sums, everywhere, 0, 0, tiled=True)
    else:
        later = scan_far(carry[0], total, "tm", True)
        (outer,) = call(outer_full_kernel, [(full, F32, free)], (), normed, g, name="outer")
        share = lax.psum_scatter(outer, ("tok", "rep"), scatter_dimension=0, tiled=True)
        weight_grad = lax.psum(share, "tm").astype(BF)
        mixed = mixed_of()
        c_grad, xg, bg, col_sums = back()
        x_grad, b_grad, step_grad, sums = last((1, 1, 128), (later,))
        sums = lax.psum(jnp.concatenate([sums, gains[None, :1]], axis=2), everywhere)
    rate_grad, bias_grad, skip_grad, gain_grad = call(
        sums_kernel, [((heads,), F32, away)] * 3 + [((width,), F32, away)], (sums,), name="sums", loose=True
    )
    return (
        mixed[None], x_grad[None], zg[None], b_grad[None], c_grad[None], step_grad[None],
        rate_grad, bias_grad, skip_grad, gain_grad, weight_grad,
    )


def solution(mesh):
    tokens = P(("tok", "rep"), "tm", None)
    frames = P(("tok", "rep"), None, "tm")
    weight = P(("tok", "rep"), None)
    return jax.shard_map(
        shards,
        mesh=mesh,
        in_specs=(tokens, tokens, tokens, tokens, frames, P(), P(), P(), P(), weight, tokens),
        out_specs=(tokens, tokens, tokens, tokens, tokens, frames, P(), P(), P(), P(), weight),
        check_vma=False,
    )
```

```python
import functools

import jax
import jax.numpy as jnp
from jax import lax
from jax.experimental import pallas as pl
from jax.experimental.pallas import tpu as pltpu
from jax.sharding import PartitionSpec as P

BF = jnp.bfloat16
F32 = jnp.float32
ROWS = ((0,), (0,))
LAST = ((1,), (1,))
CHUNKS = 8
VMEM_LIMIT = 24 * 1024 * 1024


def mm(a, b):
    return jnp.dot(a, b, preferred_element_type=F32)


def mm_tn(a, b):
    return lax.dot_general(a, b, (ROWS, ((), ())), preferred_element_type=F32)


def mm_nt(a, b):
    return lax.dot_general(a, b, (LAST, ((), ())), preferred_element_type=F32)


def split(v, parts):
    pieces = []
    for _ in range(parts):
        piece = v.astype(BF)
        pieces.append(piece)
        v = v - piece.astype(F32)
    return pieces


def column(ref):
    row = ref[...].reshape(1, -1)
    heads = row.shape[1]
    i = lax.broadcasted_iota(jnp.int32, (heads, heads), 0)
    j = lax.broadcasted_iota(jnp.int32, (heads, heads), 1)
    return jnp.sum(jnp.where(i == j, row, 0.0), axis=1, keepdims=True)


def head_map(heads, width):
    i = lax.broadcasted_iota(jnp.int32, (heads, width), 0)
    j = lax.broadcasted_iota(jnp.int32, (heads, width), 1)
    wide = width // heads
    return jnp.where((j >= i * wide) & (j < (i + 1) * wide), 1.0, 0.0).astype(F32)


def triangle(length, keep):
    i = lax.broadcasted_iota(jnp.int32, (length, length), 0)
    j = lax.broadcasted_iota(jnp.int32, (length, length), 1)
    return jnp.where(keep(i, j), 1.0, 0.0).astype(BF)


def along_frames(v, tri):
    heads = v.shape[0]
    out = mm(jnp.concatenate(split(v, 3), axis=0), tri)
    return out[:heads] + out[heads : 2 * heads] + out[2 * heads :]


def expand(v, hmap):
    return mm_tn(jnp.concatenate(split(v, 2), axis=0), jnp.concatenate([hmap, hmap], axis=0).astype(BF))


def expand_row(col, hmap):
    return jnp.sum(col * hmap, axis=0, keepdims=True)


def head_sums(y, hmap):
    hb = hmap.astype(BF)
    hi, lo = split(y, 2)
    return mm_nt(hb, hi) + mm_nt(hb, lo)


def decay(s_ref, rate_ref, bias_ref):
    v = s_ref[...] + column(bias_ref)
    e = jnp.exp(-jnp.abs(v))
    u = 1.0 + e
    d = u - 1.0
    log1p = jnp.where(d == 0.0, e, jnp.log(u) * (e / jnp.where(d == 0.0, 1.0, d)))
    delta = jnp.maximum(v, 0.0) + log1p
    a = -jnp.exp(column(rate_ref))
    ld = delta * a
    cum = along_frames(ld, triangle(ld.shape[1], lambda i, j: i <= j))
    return v, delta, a, ld, cum


class Coming:
    def __init__(self, source, target, semaphore):
        self.copy = pltpu.make_async_copy(source, target, semaphore)
        self.copy.start()
        self.target, self.waited = target, False

    def ready(self):
        if not self.waited:
            self.copy.wait()
            self.waited = True
        return self.target


def near_by(shape, dtype):
    return pltpu.VMEM(shape, dtype)


def away(shape, dtype):
    return pltpu.HBM(shape, dtype)


def free(shape, dtype):
    return jax.ShapeDtypeStruct(shape, dtype)


def call(kernel, outs, far, *args, name=None, scratch=(), after=(), beside=(), aliases=None, far_operands=(), held=0, loose=False):
    waits = len(after) + len(beside)
    anywhere = [isinstance(v, list) for v in far]
    far = [v[0] if isinstance(v, list) else v for v in far]

    def fix(v):
        return v if loose else pltpu.with_memory_space_constraint(v, pltpu.HBM)

    far_operands = (*far_operands, *range(len(args) - held, len(args)))
    args = args[: len(args) - held] + tuple(fix(v) for v in args[len(args) - held :])
    specs = [pl.BlockSpec(memory_space=pl.ANY)] * len(far)
    specs += [
        pl.BlockSpec(memory_space=pl.ANY if k in far_operands else pltpu.VMEM) for k in range(len(args))
    ]
    specs += [pl.BlockSpec(memory_space=pl.ANY)] * waits
    first, used = len(far), len(far) + len(args)
    landing = [pltpu.VMEM(v.shape, v.dtype) for v in far]
    semaphores = [pltpu.SemaphoreType.DMA((len(far),))] if far else []

    def body(*refs):
        refs, own = list(refs), len(far)
        coming = []
        if far:
            refs, targets, semaphore = refs[: -own - 1], refs[-own - 1 : -1], refs[-1]
            coming = [Coming(refs[k], targets[k], semaphore.at[k]) for k in range(own)]
        kernel(*coming, *refs[first:used], *refs[used + waits :])
        for one in coming:
            one.ready()

    return pl.pallas_call(
        body,
        out_shape=[where(shape, dtype) for shape, dtype, where in outs],
        in_specs=specs,
        out_specs=[
            pl.BlockSpec(memory_space=pl.ANY if k in (aliases or {}).values() else pltpu.VMEM) for k in range(len(outs))
        ],
        scratch_shapes=list(scratch) + landing + semaphores,
        input_output_aliases=aliases or {},
        compiler_params=pltpu.CompilerParams(vmem_limit_bytes=VMEM_LIMIT),
        name=name,
    )(*[v if any_place else fix(v) for v, any_place in zip(far, anywhere)], *args, *[pltpu.with_memory_space_constraint(v, pltpu.HBM) for v in after], *beside)


def store_decay(aux_ref, rows_ref, v, delta, a, ld, cum, skip, gain):
    heads = cum.shape[0]
    for k, value in enumerate((v, delta, ld, cum, jnp.broadcast_to(a, cum.shape))):
        aux_ref[k * heads : (k + 1) * heads, :] = value
    rows_ref[0:1, :] = skip
    rows_ref[1:2, :] = gain


def load_decay(aux_ref):
    heads = aux_ref.shape[0] // 5
    return [aux_ref[k * heads : (k + 1) * heads, :] for k in range(5)]


def store_parts(out_ref, state, row):
    count, blocks = out_ref.shape[0], row.shape[1] // 128
    rows = state.shape[0] // count
    tail = [v[:, n * 128 : (n + 1) * 128].astype(F32) for v in split(row, 2) for n in range(blocks)]
    tail = jnp.concatenate(tail, axis=0).astype(BF)
    for k in range(count):
        for n in range(blocks):
            out_ref[k, n * rows : (n + 1) * rows, :] = state[k * rows : (k + 1) * rows, n * 128 : (n + 1) * 128]
        out_ref[k, blocks * rows :, :] = tail


def payload_kernel(s_in, rate_in, bias_in, b_in, x_in, skip_in, gain_in, w_in, aux_ref, rows_ref, w_ref, *outs):
    v, delta, a, ld, cum = decay(s_in.ready(), rate_in.ready(), bias_in.ready())
    x_ref, b_ref = x_in.ready(), b_in.ready()
    width = x_ref.shape[1]
    hmap = head_map(cum.shape[0], width)
    skip = expand_row(column(skip_in.ready()), hmap)
    store_decay(aux_ref, rows_ref, v, delta, a, ld, cum, skip, gain_in.ready()[...].reshape(1, -1))
    last = cum[:, -1:]
    tail = expand(jnp.exp(last - cum) * delta, hmap)
    weighted = (x_ref[...].astype(F32) * tail).astype(BF)
    state = mm_tn(b_ref[...], weighted).astype(BF)
    total = expand_row(jnp.exp(last), hmap)
    w_ref[...] = w_in.ready()[...]
    if len(outs) == 2:
        outs[0][...] = state
        outs[1][...] = total
        return
    outs, out_ref = outs[:-1], outs[-1]
    store_parts(out_ref, state, total)
    for k, part_ref in enumerate(outs):
        part_ref[...] = out_ref[turn(k, len(outs))]


def turn(k, count):
    return lax.rem(lax.axis_index("tm") + k + count, count)


def prefix_kernel(*refs):
    gots, (out_ref, decays_ref, all_ref) = refs[:-3], refs[-3:]
    count, rows, width = out_ref.shape
    for k, got in enumerate(gots):
        all_ref[turn(-k, count)] = got[...]
    blocks = width // 128
    decays = []
    for k in range(count):
        pair = all_ref[k, blocks * rows :, :].astype(F32)
        decays.append(pair[:blocks] + pair[blocks:])
        decays_ref[k * blocks : (k + 1) * blocks, :] = decays[k]
    for n in range(blocks):
        cols = slice(n * 128, (n + 1) * 128)
        carried = jnp.zeros((rows, 128), F32)
        for k in range(count):
            out_ref[k, :, cols] = carried.astype(BF)
            if k + 1 < count:
                state = all_ref[k, n * rows : (n + 1) * rows, :].astype(F32)
                carried = state + decays[k][n : n + 1] * carried


def gather_rows(parts, out_ref):
    count, rows = len(parts), parts[0].shape[0]
    for k, one in enumerate(parts):
        out_ref[pl.ds(pl.multiple_of(turn(-k, count) * rows, rows), rows), :] = one[...]


def suffix_kernel(decays_ref, products_ref, *refs):
    count = (len(refs) - 4) // 2
    gots, outs, (passed_ref, gains_ref, out_ref, all_ref) = refs[:count], refs[count:-4], refs[-4:]
    del products_ref, passed_ref
    _, rows, width = out_ref.shape
    blocks = width // 128
    for k, got in enumerate(gots):
        all_ref[turn(-k, count)] = got[...]
    decays = decays_ref[...]
    for n in range(blocks):
        cols = slice(n * 128, (n + 1) * 128)
        carried = jnp.zeros((rows, 128), F32)
        for k in reversed(range(count)):
            out_ref[k, :, cols] = carried.astype(BF)
            if k > 0:
                grad = all_ref[k, n * rows : (n + 1) * rows, :].astype(F32)
                carried = grad + decays[k * blocks + n : k * blocks + n + 1] * carried
    for k, part_ref in enumerate(outs):
        part_ref[...] = out_ref[turn(k, count)]
    gains = sum(all_ref[k, blocks * rows :, :].astype(F32) for k in range(count))
    gains_ref[...] = gains[:blocks] + gains[blocks:]


def inner_kernel(b_in, c_in, x_in, aux_ref, rows_ref, inner_ref):
    _, delta, _, cum, _ = load_decay(aux_ref)
    x_ref, b_ref, c_ref = x_in.ready(), b_in.ready(), c_in.ready()
    heads, length = cum.shape
    width = x_ref.shape[1]
    hmap = head_map(heads, width)
    cum_t = cum.T
    x = x_ref[...].astype(F32)
    xd = (x * expand(delta, hmap)).astype(BF)
    skip = rows_ref[0:1, :]
    half = length // 2
    scores = mm_nt(c_ref[...], b_ref[...])
    i = lax.broadcasted_iota(jnp.int32, (half, half), 0)
    j = lax.broadcasted_iota(jnp.int32, (half, half), 1)
    diag = i >= j
    s00 = jnp.where(diag, scores[:half, :half], 0.0)
    s10 = scores[half:, :half]
    s11 = jnp.where(diag, scores[half:, half:], 0.0)
    pair = 2 * (width // heads)
    first = lax.broadcasted_iota(jnp.int32, (half, pair), 1) < pair // 2
    for p in range(heads // 2):
        cols = slice(p * pair, (p + 1) * pair)
        upper, lower = [], []
        for h in (2 * p, 2 * p + 1):
            q0, q1 = cum_t[:half, h : h + 1], cum_t[half:, h : h + 1]
            k0, k1 = cum[h : h + 1, :half], cum[h : h + 1, half:]
            m00 = jnp.exp(jnp.minimum(q0 - k0, 0.0)) * s00
            m10 = jnp.exp(jnp.minimum(q1 - k0, 0.0)) * s10
            m11 = jnp.exp(jnp.minimum(q1 - k1, 0.0)) * s11
            upper.append(m00.astype(BF))
            lower.append(jnp.concatenate([m10.astype(BF), m11.astype(BF)], axis=1))
        y0 = mm(jnp.concatenate(upper, axis=0), xd[:half, cols])
        y1 = mm(jnp.concatenate(lower, axis=0), xd[:, cols])
        inner_ref[:half, cols] = jnp.where(first, y0[:half], y0[half:]) + skip[:, cols] * x[:half, cols]
        inner_ref[half:, cols] = jnp.where(first, y1[:half], y1[half:]) + skip[:, cols] * x[half:, cols]


def unit():
    return lax.axis_index("tok") * lax.axis_size("rep") + lax.axis_index("rep")


def weight_pieces(refs, full_ref, semaphore):
    copies = []
    for k, piece in enumerate(refs):
        rows = piece.shape[0]
        at = pl.ds(pl.multiple_of((unit() ^ k) * rows, rows), rows) if len(refs) > 1 else pl.ds(0, rows)
        copies.append(Coming(piece, full_ref.at[at, :], semaphore.at[k]))
    return copies


def weight_kernel(g_in, *refs):
    pieces, (ng_ref, full_ref, semaphore) = refs[:-3], refs[-3:]
    copies = weight_pieces(pieces, full_ref, semaphore)
    g = g_in.ready()[...]
    for one in copies:
        one.ready()
    ng_ref[...] = mm_nt(g, full_ref[...]).astype(BF)


def norm_kernel(
    c_in, z_in, x_in, aux_ref, params_ref, local_ref, ng_ref, inc_ref,
    normed_ref, other_ref, dy_ref, zg_ref, rows_ref, sums_ref, *refs,
):
    carries, (all_ref, inner_ref, ec_ref, de_ref, hi_ref, lo_ref) = refs[:-6], refs[-6:]
    _, _, _, cum, _ = load_decay(aux_ref)
    heads, length = cum.shape
    width = params_ref.shape[1]
    hmap = head_map(heads, width)
    ec_ref[...] = expand(jnp.exp(cum), hmap)
    c_ref = c_in.ready()
    inner_ref[...] = mm(c_ref[...], inc_ref[...])
    z_ref, x_ref = z_in.ready(), x_in.ready()
    skip, gain = params_ref[0:1, :], params_ref[1:2, :]
    step = length // CHUNKS
    gains = jnp.zeros((1, width), F32)
    skips = jnp.zeros((1, width), F32)
    for n in range(CHUNKS):
        at = slice(n * step, (n + 1) * step)
        ec = ec_ref[at, :]
        inner = local_ref[at, :] + inner_ref[at, :] * ec
        z = z_ref[at, :].astype(F32)
        sig = 1.0 / (1.0 + jnp.exp(-z))
        silu = z * sig
        gated = inner * silu
        r = lax.rsqrt(jnp.mean(gated * gated, axis=1, keepdims=True) + 1e-05)
        nhat = gated * r
        normed_ref[at, :] = (nhat * gain).astype(BF)
        ng = ng_ref[at, :].astype(F32)
        prod = ng * nhat
        gains = gains + jnp.sum(prod, axis=0, keepdims=True)
        m = jnp.mean(prod * gain, axis=1, keepdims=True)
        dgated = r * (ng * gain - nhat * m)
        dinner = dgated * silu
        dy = dinner.astype(BF)
        dy_ref[at, :] = dy
        de_ref[at, :] = (dinner * ec).astype(BF)
        zg_ref[at, :] = (dgated * inner * (sig + silu * (1.0 - sig))).astype(BF)
        x = x_ref[at, :].astype(F32)
        skips = skips + jnp.sum(dinner * x, axis=0, keepdims=True)
        hi_ref[at, :], lo_ref[at, :] = split(dy.astype(F32) * (inner - skip * x), 2)
    carry = mm_tn(c_ref[...], de_ref[...]).astype(BF)
    if len(carries) == 1:
        carries[0][...] = carry
    else:
        store_parts(all_ref, carry, gains)
        for k, part_ref in enumerate(carries):
            part_ref[...] = all_ref[turn(k, len(carries))]
    hb = hmap.astype(BF)
    rows_ref[...] = mm_nt(hb, hi_ref[...]) + mm_nt(hb, lo_ref[...])
    sums_ref[0:1, :] = gains
    sums_ref[1:2, :] = skips
    block = other_ref.shape[1] // 4
    for k in range(4):
        at = (2 * k + 1 - lax.rem(lax.axis_index("rep"), 2)) * block
        other_ref[:, k * block : (k + 1) * block] = normed_ref[:, pl.ds(pl.multiple_of(at, block), block)]


def outer_kernel(g_in, gc_in, normed_ref, got_ref, out_ref):
    g_ref, gc_ref = g_in.ready(), gc_in.ready()
    core = lax.rem(lax.axis_index("rep"), 2)
    chips, rows = out_ref.shape[:2]
    for k in range(chips):
        mine = pl.ds(pl.multiple_of((2 * k + core) * rows, rows), rows)
        part = mm_tn(normed_ref[:, mine], g_ref[...]) + mm_tn(got_ref[:, k * rows : (k + 1) * rows], gc_ref[...])
        out_ref[k] = part.astype(BF)


def share_kernel(all_ref, *refs):
    outs, total_ref = refs[:-1], refs[-1]
    total = all_ref[0].astype(F32)
    for k in range(1, all_ref.shape[0]):
        total = total + all_ref[k].astype(F32)
    total_ref[...] = total
    rows = outs[0].shape[0]
    for k, out_ref in enumerate(outs):
        part = total_ref[pl.ds(pl.multiple_of(turn(k, len(outs)) * rows, rows), rows), :]
        out_ref[...] = part.astype(out_ref.dtype)


def add_kernel(*refs):
    own_ref, gots, out_ref = refs[0], refs[1:-1], refs[-1]
    total = own_ref[...]
    for got in gots:
        total = total + got[...].astype(F32)
    out_ref[...] = total.astype(BF)


def mixed_kernel(weight_in, normed_ref, mixed_ref):
    mixed_ref[...] = mm(normed_ref[...], weight_in.ready()[...]).astype(BF)


def join_kernel(*refs):
    gather_rows(refs[:-1], refs[-1])


def outer_full_kernel(normed_ref, g_ref, out_ref):
    out_ref[...] = mm_tn(normed_ref[...], g_ref[...])


def back_kernel(
    dy_in, b_in, c_in, x_in, aux_ref, params_ref, inc_ref,
    cg_ref, xg_ref, bg_ref, cols_ref, dxw_ref,
):
    _, delta, _, cum, _ = load_decay(aux_ref)
    x_ref, b_ref, c_ref = x_in.ready(), b_in.ready(), c_in.ready()
    dy_ref = dy_in.ready()
    heads, length = cum.shape
    width = x_ref.shape[1]
    hmap = head_map(heads, width)
    cum_t = cum.T
    delta_e = expand(delta, hmap)
    xd = (x_ref[...].astype(F32) * delta_e).astype(BF)
    dy = dy_ref[...]
    half = length // 2
    scores = mm_nt(b_ref[...], c_ref[...])
    i = lax.broadcasted_iota(jnp.int32, (half, half), 0)
    j = lax.broadcasted_iota(jnp.int32, (half, half), 1)
    diag = j >= i
    s00 = jnp.where(diag, scores[:half, :half], 0.0)
    s01 = scores[:half, half:]
    s11 = jnp.where(diag, scores[half:, half:], 0.0)
    pair = 2 * (width // heads)
    first = lax.broadcasted_iota(jnp.int32, (half, pair), 1) < pair // 2
    whole_first = lax.broadcasted_iota(jnp.int32, (length, pair), 1) < pair // 2
    d00 = jnp.zeros((half, half), F32)
    d01 = jnp.zeros((half, half), F32)
    d11 = jnp.zeros((half, half), F32)
    none = jnp.zeros((length, pair), BF)
    for p in range(heads // 2):
        cols = slice(p * pair, (p + 1) * pair)
        xp, dp = xd[:, cols], dy[:, cols]
        stacked = jnp.concatenate([jnp.where(whole_first, xp, none), jnp.where(whole_first, none, xp)], axis=0)
        dm = mm_nt(stacked, dp)
        upper, lower = [], []
        for n, h in enumerate((2 * p, 2 * p + 1)):
            k0, k1 = cum_t[:half, h : h + 1], cum_t[half:, h : h + 1]
            q0, q1 = cum[h : h + 1, :half], cum[h : h + 1, half:]
            l00 = jnp.exp(jnp.minimum(q0 - k0, 0.0))
            l01 = jnp.exp(jnp.minimum(q1 - k0, 0.0))
            l11 = jnp.exp(jnp.minimum(q1 - k1, 0.0))
            at = n * length
            d00 = d00 + l00 * dm[at : at + half, :half]
            d01 = d01 + l01 * dm[at : at + half, half:]
            d11 = d11 + l11 * dm[at + half : at + length, half:]
            upper.append(jnp.concatenate([(l00 * s00).astype(BF), (l01 * s01).astype(BF)], axis=1))
            lower.append((l11 * s11).astype(BF))
        y0 = mm(jnp.concatenate(upper, axis=0), dp)
        y1 = mm(jnp.concatenate(lower, axis=0), dp[half:])
        dxw_ref[:half, cols] = jnp.where(first, y0[:half], y0[half:])
        dxw_ref[half:, cols] = jnp.where(first, y1[:half], y1[half:])
    d00 = jnp.where(diag, d00, 0.0).astype(BF)
    d01 = d01.astype(BF)
    d11 = jnp.where(diag, d11, 0.0).astype(BF)
    c0, c1 = c_ref[:half, :], c_ref[half:, :]
    b0, b1 = b_ref[:half, :], b_ref[half:, :]
    bg_ref[:half, :] = (mm(d00, c0) + mm(d01, c1)).astype(BF)
    bg_ref[half:, :] = mm(d11, c1).astype(BF)
    ec = expand(jnp.exp(cum), hmap)
    carried = mm_nt((dy.astype(F32) * ec).astype(BF), inc_ref[...])
    cg_ref[:half, :] = (carried[:half] + mm_tn(d00, b0).astype(BF).astype(F32)).astype(BF)
    cg_ref[half:, :] = (carried[half:] + (mm_tn(d01, b0) + mm_tn(d11, b1)).astype(BF).astype(F32)).astype(BF)
    dxw = dxw_ref[...]
    cols_ref[...] = head_sums(xd.astype(F32) * dxw, hmap)
    skip = params_ref[0:1, :]
    xg_ref[...] = delta_e * dxw + skip * dy.astype(F32)


def last_kernel(
    gains_here, b_in, x_in, rows_in, cols_in, bg_in, xg_in, sums_in, aux_ref, inc_ref, *more,
):
    parts, (x_out, b_out, step_out, sums_out, later_ref) = more[:-5], more[-5:]
    gains_ref, parts = (parts[0], parts[1:]) if gains_here else (None, parts)
    count = len(parts)
    if count > 1:
        gather_rows(parts, later_ref)
    else:
        later_ref[...] = parts[0][...]
    v, delta, ld, cum, a = load_decay(aux_ref)
    heads, length = cum.shape
    width = xg_in.target.shape[1]
    hmap = head_map(heads, width)
    last = cum[:, -1:]
    tailing = jnp.exp(last - cum)
    tail = tailing * delta
    tail_e = expand(tail, hmap)
    b_ref = b_in.ready()
    later = later_ref[...]
    dweighted = mm(b_ref[...], later)
    x = x_in.ready()[...].astype(F32)
    x_out[...] = (xg_in.ready()[...] + tail_e * dweighted).astype(BF)
    weighted = (x * tail_e).astype(BF)
    b_out[...] = (bg_in.ready()[...].astype(F32) + mm_nt(weighted, later)).astype(BF)
    dtail = head_sums(x * dweighted, hmap)
    cross = jnp.sum(later.astype(F32) * inc_ref[...].astype(F32), axis=0, keepdims=True)
    dtotal = jnp.sum(cross * hmap, axis=1, keepdims=True) * jnp.exp(last)
    cols = cols_in.ready()[...]
    dld = along_frames(rows_in.ready()[...] - cols, triangle(length, lambda i, j: i >= j))
    dld = dld + along_frames(dtail * tail, triangle(length, lambda i, j: i < j)) + dtotal
    ddelta = cols / delta + dtail * tailing + a * dld
    dstep = ddelta / (1.0 + jnp.exp(-v))
    step_out[...] = dstep
    drate = jnp.sum(dld * ld, axis=1, keepdims=True)
    dbias = jnp.sum(dstep, axis=1, keepdims=True)
    i = lax.broadcasted_iota(jnp.int32, (heads, 128), 0)
    j = lax.broadcasted_iota(jnp.int32, (heads, 128), 1)

    def lay(col, at):
        return jnp.sum(jnp.where(j == i + at, col, 0.0), axis=0, keepdims=True)

    small = lay(drate, 0) + lay(dbias, heads) + lay(jnp.sum(sums_in.ready()[1:2, :] * hmap, axis=1, keepdims=True), 2 * heads)
    if gains_ref is None:
        sums_out[0] = small
        return
    each = gains_ref.shape[0] // count
    shares = [gains_ref[pl.ds(lax.axis_index("tm") * each + n, 1), :] for n in range(each)]
    row = jnp.concatenate([small] + shares, axis=1)
    for k in range(sums_out.shape[0]):
        sums_out[k] = row


def sums_kernel(all_in, rate_out, bias_out, skip_out, gain_out):
    every = all_in.ready()[...]
    heads = rate_out.shape[0]
    small = jnp.sum(every[:, 0, :128], axis=0)
    rate_out[...] = small[:heads]
    bias_out[...] = small[heads : 2 * heads]
    skip_out[...] = small[2 * heads : 3 * heads]
    share = every.shape[2] - 128
    parts = gain_out.shape[0] // share
    group = every.shape[0] // parts
    for k in range(parts):
        gain_out[k * share : (k + 1) * share] = jnp.sum(every[k * group : (k + 1) * group, 0, 128:], axis=0)


def scan_far(value, total, axis, reverse):
    count = lax.axis_size(axis)
    position = lax.axis_index(axis)
    decayed, state = total, value.astype(F32)
    step = 1
    while step < count:
        pairs = [(k, k - step) for k in range(step, count)] if reverse else [(k, k + step) for k in range(count - step)]
        inside = position + step < count if reverse else position >= step
        got_state = lax.ppermute(state.astype(BF), axis, pairs).astype(F32)
        got_total = lax.ppermute(decayed, axis, pairs)
        state = jnp.where(inside, decayed * got_state + state, state)
        decayed = jnp.where(inside, decayed * got_total, decayed)
        step *= 2
    pairs = [(k, k - 1) for k in range(1, count)] if reverse else [(k, k + 1) for k in range(count - 1)]
    return lax.ppermute(state.astype(BF), axis, pairs)


def shards(x_branch, z_gate, b_input, c_input, step_raw, rate_log, step_bias, skip_gain, norm_gain, out_weight, out_grad):
    seqs, length, width = x_branch.shape
    model = out_grad.shape[2]
    heads = rate_log.shape[0]
    state_size = b_input.shape[2]
    x, z, b, c, s, g = x_branch[0], z_gate[0], b_input[0], c_input[0], step_raw[0], out_grad[0]
    n_tm, n_tok, n_rep = lax.axis_size("tm"), lax.axis_size("tok"), lax.axis_size("rep")
    near = (n_tm, n_tok, n_rep) == (4, 2, 4)
    rows = out_weight.shape[0]
    full = (width, model)
    wide = (length, width)
    core = [(k, k ^ 1) for k in range(4)]
    side = [(k, k ^ 2) for k in range(4)]
    front = [(0, 1), (1, 0)]
    diagonal = [(k, k ^ 6) for k in range(8)]
    ahead = [[(i, (i + k) % n_tm) for i in range(n_tm)] for k in range(1, n_tm)]

    raw = (s, rate_log, step_bias, b, x, skip_gain, norm_gain, out_weight)
    aux_shapes = [((5 * heads, length), F32, near_by), ((8, width), F32, near_by), (out_weight.shape, BF, away)]
    if near:
        part = (n_tm, state_size // n_tm)
        row_part = (part[1], width)
        blocks_of = width // 128
        part_shape = (n_tm, blocks_of * part[1] + 2 * blocks_of, 128)
        aux, params, out_weight, *payload = call(
            payload_kernel, aux_shapes + [(part_shape[1:], BF, free)] * n_tm, raw, name="state",
            scratch=[pltpu.VMEM(part_shape, BF)],
        )
        blocks = [payload[0]] + [lax.ppermute(v, "tm", pairs) for v, pairs in zip(payload[1:], ahead)]
        gc = lax.ppermute(g, "rep", core)
        wx = lax.ppermute(out_weight, "rep", side)
        wy = lax.ppermute(out_weight, "tok", front)
        wd = lax.ppermute(out_weight, ("tok", "rep"), diagonal)
        wc, wxc, wyc, wdc = (lax.ppermute(v, "rep", core) for v in (out_weight, wx, wy, wd))
        prefixes, decays = call(
            prefix_kernel, [(part + (width,), BF, free), ((n_tm * blocks_of, 128), F32, near_by)], (), *blocks,
            name="prefix", scratch=[pltpu.VMEM(part_shape, BF)],
        )
        incoming = lax.all_to_all(prefixes, "tm", 0, 0, tiled=True).reshape(state_size, width)
        (local,) = call(
            inner_kernel, [(wide, F32, near_by)], (b, c, x), aux, params, name="inner", beside=(prefixes,)
        )
        pieces = (out_weight, wc, wx, wxc, wy, wyc, wd, wdc)
        after = ()
    else:
        aux, params, out_weight, state, total = call(
            payload_kernel, aux_shapes + [((state_size, width), BF, free), ((1, width), F32, free)], raw, name="state"
        )
        incoming = scan_far(state, total, "tm", False)
        (local,) = call(inner_kernel, [(wide, F32, near_by)], (b, c, x), aux, params, name="inner")
        pieces = (lax.all_gather(out_weight, ("tok", "rep"), axis=0, tiled=True),)
        after = ()
    ng, weight = call(
        weight_kernel, [(wide, BF, near_by), (full, BF, away)], (g,), *pieces, name="normed_grad", after=after, beside=(local,), held=len(pieces), loose=True,
        scratch=[pltpu.SemaphoreType.DMA((len(pieces),))],
    )
    normed, other, dy, zg, row_sums, gains, *carry = call(
        norm_kernel,
        [
            (wide, BF, near_by), ((length, width // 2), BF, free), (wide, BF, free),
            (wide, BF, away), ((heads, length), F32, free), ((8, width), F32, free),
        ]
        + ([(part_shape[1:], BF, free)] * n_tm if near else [((state_size, width), BF, away)]),
        (c, z, x), aux, params, local, ng, incoming, name="norm",
        scratch=[pltpu.VMEM(part_shape if near else (8, 128), BF)] + [pltpu.VMEM(wide, F32)] * 2 + [pltpu.VMEM(wide, BF)] * 3,
    )

    def mixed_of(*after):
        return call(mixed_kernel, [(wide, BF, away)], (weight,), normed, name="mixed", after=after)[0]

    def back(*after):
        return call(
            back_kernel,
            [
                ((length, state_size), BF, away), (wide, F32, free), ((length, state_size), BF, free),
                ((heads, length), F32, free),
            ],
            ([dy], b, c, x), aux, params, incoming, name="back", beside=after, scratch=[pltpu.VMEM(wide, F32)],
        )

    everywhere = ("tm", "tok", "rep")

    def last(row, parts, *more, after=()):
        return call(
            functools.partial(last_kernel, bool(more)),
            [(wide, BF, away), ((length, state_size), BF, away), ((heads, length), F32, away), (row, F32, away)],
            (b, x, [row_sums], [col_sums], [bg], [xg], [gains]), aux, incoming, *more, *parts, name="last", after=after,
            scratch=[pltpu.VMEM((state_size, width), BF)],
        )

    if near:
        theirs = lax.ppermute(other, "rep", core)
        (products,) = call(
            outer_kernel, [((4, rows, model), BF, away)], (g, gc), normed, theirs, name="outer", beside=(carry[0],)
        )
        grads = [carry[0]] + [lax.ppermute(v, "tm", pairs) for v, pairs in zip(carry[1:], ahead)]
        mixed = mixed_of(products)
        own, *sends, products, gains_tm = call(
            suffix_kernel, [(row_part, BF, free)] * n_tm + [(products.shape, BF, away), ((blocks_of, 128), F32, near_by)], (),
            decays, products, *grads, name="suffix", far_operands=(1,), aliases={1: n_tm}, scratch=[pltpu.VMEM(part + (width,), BF), pltpu.VMEM(part_shape, BF)], after=(mixed,),
        )
        parts = [own] + [lax.ppermute(v, "tm", pairs) for v, pairs in zip(sends, ahead)]
        chips = lax.all_to_all(
            products, ("tok", "rep"), 0, 0, axis_index_groups=[[0, 2, 4, 6], [1, 3, 5, 7]], tiled=True
        )
        c_grad, xg, bg, col_sums = back(own)
        row = (n_tm * n_tok * n_rep, 1, 128 + width // n_tm)
        x_grad, b_grad, step_grad, sums = last(row, parts, gains_tm)
        quarter = (rows // n_tm, model)
        own, *sends = call(
            share_kernel, [(quarter, F32, near_by)] + [(quarter, BF, free)] * (n_tm - 1), (), chips, name="add_chips",
            after=(step_grad,), scratch=[pltpu.VMEM((rows, model), F32)],
        )
        shares = [lax.ppermute(v, "tm", pairs) for v, pairs in zip(sends, ahead)]
        (quarter,) = call(add_kernel, [(quarter, BF, free)], (), own, *shares, name="add_blocks")
        pieces = [lax.ppermute(quarter, "tm", pairs) for pairs in ahead]
        (weight_grad,) = call(join_kernel, [((rows, model), BF, away)], (), quarter, *pieces, name="join")
        sums = lax.all_to_all(sums, everywhere, 0, 0, tiled=True)
    else:
        later = scan_far(carry[0], total, "tm", True)
        (outer,) = call(outer_full_kernel, [(full, F32, free)], (), normed, g, name="outer")
        share = lax.psum_scatter(outer, ("tok", "rep"), scatter_dimension=0, tiled=True)
        weight_grad = lax.psum(share, "tm").astype(BF)
        mixed = mixed_of()
        c_grad, xg, bg, col_sums = back()
        x_grad, b_grad, step_grad, sums = last((1, 1, 128), (later,))
        sums = lax.psum(jnp.concatenate([sums, gains[None, :1]], axis=2), everywhere)
    rate_grad, bias_grad, skip_grad, gain_grad = call(
        sums_kernel, [((heads,), F32, away)] * 3 + [((width,), F32, away)], (sums,), name="sums", loose=True
    )
    return (
        mixed[None], x_grad[None], zg[None], b_grad[None], c_grad[None], step_grad[None],
        rate_grad, bias_grad, skip_grad, gain_grad, weight_grad,
    )


def solution(mesh):
    tokens = P(("tok", "rep"), "tm", None)
    frames = P(("tok", "rep"), None, "tm")
    weight = P(("tok", "rep"), None)
    return jax.shard_map(
        shards,
        mesh=mesh,
        in_specs=(tokens, tokens, tokens, tokens, frames, P(), P(), P(), P(), weight, tokens),
        out_specs=(tokens, tokens, tokens, tokens, tokens, frames, P(), P(), P(), P(), weight),
        check_vma=False,
    )
```

```python
import functools

import jax
import jax.numpy as jnp
from jax import lax
from jax.experimental import pallas as pl
from jax.experimental.pallas import tpu as pltpu
from jax.sharding import PartitionSpec as P

BF = jnp.bfloat16
F32 = jnp.float32
ROWS = ((0,), (0,))
LAST = ((1,), (1,))
CHUNKS = 8
VMEM_LIMIT = 16 * 1024 * 1024


def mm(a, b):
    return jnp.dot(a, b, preferred_element_type=F32)


def mm_tn(a, b):
    return lax.dot_general(a, b, (ROWS, ((), ())), preferred_element_type=F32)


def mm_nt(a, b):
    return lax.dot_general(a, b, (LAST, ((), ())), preferred_element_type=F32)


def split(v, parts):
    pieces = []
    for _ in range(parts):
        piece = v.astype(BF)
        pieces.append(piece)
        v = v - piece.astype(F32)
    return pieces


def column(ref):
    row = ref[...].reshape(1, -1)
    heads = row.shape[1]
    i = lax.broadcasted_iota(jnp.int32, (heads, heads), 0)
    j = lax.broadcasted_iota(jnp.int32, (heads, heads), 1)
    return jnp.sum(jnp.where(i == j, row, 0.0), axis=1, keepdims=True)


def head_map(heads, width):
    i = lax.broadcasted_iota(jnp.int32, (heads, width), 0)
    j = lax.broadcasted_iota(jnp.int32, (heads, width), 1)
    wide = width // heads
    return jnp.where((j >= i * wide) & (j < (i + 1) * wide), 1.0, 0.0).astype(F32)


def triangle(length, keep):
    i = lax.broadcasted_iota(jnp.int32, (length, length), 0)
    j = lax.broadcasted_iota(jnp.int32, (length, length), 1)
    return jnp.where(keep(i, j), 1.0, 0.0).astype(BF)


def along_frames(v, tri):
    heads = v.shape[0]
    out = mm(jnp.concatenate(split(v, 3), axis=0), tri)
    return out[:heads] + out[heads : 2 * heads] + out[2 * heads :]


def expand(v, hmap):
    return mm_tn(jnp.concatenate(split(v, 2), axis=0), jnp.concatenate([hmap, hmap], axis=0).astype(BF))


def expand_row(col, hmap):
    return jnp.sum(col * hmap, axis=0, keepdims=True)


def head_sums(y, hmap):
    hb = hmap.astype(BF)
    hi, lo = split(y, 2)
    return mm_nt(hb, hi) + mm_nt(hb, lo)


def decay(s_ref, rate_ref, bias_ref):
    v = s_ref[...] + column(bias_ref)
    e = jnp.exp(-jnp.abs(v))
    u = 1.0 + e
    d = u - 1.0
    log1p = jnp.where(d == 0.0, e, jnp.log(u) * (e / jnp.where(d == 0.0, 1.0, d)))
    delta = jnp.maximum(v, 0.0) + log1p
    a = -jnp.exp(column(rate_ref))
    ld = delta * a
    cum = along_frames(ld, triangle(ld.shape[1], lambda i, j: i <= j))
    return v, delta, a, ld, cum


class Coming:
    def __init__(self, source, target, semaphore):
        self.copy = pltpu.make_async_copy(source, target, semaphore)
        self.copy.start()
        self.target, self.waited = target, False

    def ready(self):
        if not self.waited:
            self.copy.wait()
            self.waited = True
        return self.target


def near_by(shape, dtype):
    return pltpu.VMEM(shape, dtype)


def away(shape, dtype):
    return pltpu.HBM(shape, dtype)


def free(shape, dtype):
    return jax.ShapeDtypeStruct(shape, dtype)


def call(kernel, outs, far, *args, name=None, scratch=(), after=(), beside=(), aliases=None, far_operands=(), held=0, loose=False):
    waits = len(after) + len(beside)
    anywhere = [isinstance(v, list) for v in far]
    far = [v[0] if isinstance(v, list) else v for v in far]

    def fix(v):
        return v if loose else pltpu.with_memory_space_constraint(v, pltpu.HBM)

    far_operands = (*far_operands, *range(len(args) - held, len(args)))
    args = args[: len(args) - held] + tuple(fix(v) for v in args[len(args) - held :])
    specs = [pl.BlockSpec(memory_space=pl.ANY)] * len(far)
    specs += [
        pl.BlockSpec(memory_space=pl.ANY if k in far_operands else pltpu.VMEM) for k in range(len(args))
    ]
    specs += [pl.BlockSpec(memory_space=pl.ANY)] * waits
    first, used = len(far), len(far) + len(args)
    landing = [pltpu.VMEM(v.shape, v.dtype) for v in far]
    semaphores = [pltpu.SemaphoreType.DMA((len(far),))] if far else []

    def body(*refs):
        refs, own = list(refs), len(far)
        coming = []
        if far:
            refs, targets, semaphore = refs[: -own - 1], refs[-own - 1 : -1], refs[-1]
            coming = [Coming(refs[k], targets[k], semaphore.at[k]) for k in range(own)]
        kernel(*coming, *refs[first:used], *refs[used + waits :])
        for one in coming:
            one.ready()

    return pl.pallas_call(
        body,
        out_shape=[where(shape, dtype) for shape, dtype, where in outs],
        in_specs=specs,
        out_specs=[
            pl.BlockSpec(memory_space=pl.ANY if k in (aliases or {}).values() else pltpu.VMEM) for k in range(len(outs))
        ],
        scratch_shapes=list(scratch) + landing + semaphores,
        input_output_aliases=aliases or {},
        compiler_params=pltpu.CompilerParams(vmem_limit_bytes=VMEM_LIMIT),
        name=name,
    )(*[v if any_place else fix(v) for v, any_place in zip(far, anywhere)], *args, *[pltpu.with_memory_space_constraint(v, pltpu.HBM) for v in after], *beside)


def store_decay(aux_ref, rows_ref, v, delta, a, ld, cum, skip, gain):
    heads = cum.shape[0]
    for k, value in enumerate((v, delta, ld, cum, jnp.broadcast_to(a, cum.shape))):
        aux_ref[k * heads : (k + 1) * heads, :] = value
    rows_ref[0:1, :] = skip
    rows_ref[1:2, :] = gain


def load_decay(aux_ref):
    heads = aux_ref.shape[0] // 5
    return [aux_ref[k * heads : (k + 1) * heads, :] for k in range(5)]


def store_parts(out_ref, state, row):
    count, blocks = out_ref.shape[0], row.shape[1] // 128
    rows = state.shape[0] // count
    tail = [v[:, n * 128 : (n + 1) * 128].astype(F32) for v in split(row, 2) for n in range(blocks)]
    tail = jnp.concatenate(tail, axis=0).astype(BF)
    for k in range(count):
        for n in range(blocks):
            out_ref[k, n * rows : (n + 1) * rows, :] = state[k * rows : (k + 1) * rows, n * 128 : (n + 1) * 128]
        out_ref[k, blocks * rows :, :] = tail


def payload_kernel(s_in, rate_in, bias_in, b_in, x_in, skip_in, gain_in, w_in, aux_ref, rows_ref, w_ref, *outs):
    v, delta, a, ld, cum = decay(s_in.ready(), rate_in.ready(), bias_in.ready())
    x_ref, b_ref = x_in.ready(), b_in.ready()
    width = x_ref.shape[1]
    hmap = head_map(cum.shape[0], width)
    skip = expand_row(column(skip_in.ready()), hmap)
    store_decay(aux_ref, rows_ref, v, delta, a, ld, cum, skip, gain_in.ready()[...].reshape(1, -1))
    last = cum[:, -1:]
    tail = expand(jnp.exp(last - cum) * delta, hmap)
    weighted = (x_ref[...].astype(F32) * tail).astype(BF)
    state = mm_tn(b_ref[...], weighted).astype(BF)
    total = expand_row(jnp.exp(last), hmap)
    w_ref[...] = w_in.ready()[...]
    if len(outs) == 2:
        outs[0][...] = state
        outs[1][...] = total
        return
    outs, out_ref = outs[:-1], outs[-1]
    store_parts(out_ref, state, total)
    for k, part_ref in enumerate(outs):
        part_ref[...] = out_ref[turn(k, len(outs))]


def turn(k, count):
    return lax.rem(lax.axis_index("tm") + k + count, count)


def prefix_kernel(*refs):
    gots, (out_ref, decays_ref, all_ref) = refs[:-3], refs[-3:]
    count, rows, width = out_ref.shape
    for k, got in enumerate(gots):
        all_ref[turn(-k, count)] = got[...]
    blocks = width // 128
    decays = []
    for k in range(count):
        pair = all_ref[k, blocks * rows :, :].astype(F32)
        decays.append(pair[:blocks] + pair[blocks:])
        decays_ref[k * blocks : (k + 1) * blocks, :] = decays[k]
    for n in range(blocks):
        cols = slice(n * 128, (n + 1) * 128)
        carried = jnp.zeros((rows, 128), F32)
        for k in range(count):
            out_ref[k, :, cols] = carried.astype(BF)
            if k + 1 < count:
                state = all_ref[k, n * rows : (n + 1) * rows, :].astype(F32)
                carried = state + decays[k][n : n + 1] * carried


def gather_rows(parts, out_ref):
    count, rows = len(parts), parts[0].shape[0]
    for k, one in enumerate(parts):
        out_ref[pl.ds(pl.multiple_of(turn(-k, count) * rows, rows), rows), :] = one[...]


def suffix_kernel(decays_ref, products_ref, *refs):
    count = (len(refs) - 4) // 2
    gots, outs, (passed_ref, gains_ref, out_ref, all_ref) = refs[:count], refs[count:-4], refs[-4:]
    del products_ref, passed_ref
    _, rows, width = out_ref.shape
    blocks = width // 128
    for k, got in enumerate(gots):
        all_ref[turn(-k, count)] = got[...]
    decays = decays_ref[...]
    for n in range(blocks):
        cols = slice(n * 128, (n + 1) * 128)
        carried = jnp.zeros((rows, 128), F32)
        for k in reversed(range(count)):
            out_ref[k, :, cols] = carried.astype(BF)
            if k > 0:
                grad = all_ref[k, n * rows : (n + 1) * rows, :].astype(F32)
                carried = grad + decays[k * blocks + n : k * blocks + n + 1] * carried
    for k, part_ref in enumerate(outs):
        part_ref[...] = out_ref[turn(k, count)]
    gains = sum(all_ref[k, blocks * rows :, :].astype(F32) for k in range(count))
    gains_ref[...] = gains[:blocks] + gains[blocks:]


def inner_kernel(b_in, c_in, x_in, aux_ref, rows_ref, inner_ref):
    _, delta, _, cum, _ = load_decay(aux_ref)
    x_ref, b_ref, c_ref = x_in.ready(), b_in.ready(), c_in.ready()
    heads, length = cum.shape
    width = x_ref.shape[1]
    hmap = head_map(heads, width)
    cum_t = cum.T
    x = x_ref[...].astype(F32)
    xd = (x * expand(delta, hmap)).astype(BF)
    skip = rows_ref[0:1, :]
    half = length // 2
    scores = mm_nt(c_ref[...], b_ref[...])
    i = lax.broadcasted_iota(jnp.int32, (half, half), 0)
    j = lax.broadcasted_iota(jnp.int32, (half, half), 1)
    diag = i >= j
    s00 = jnp.where(diag, scores[:half, :half], 0.0)
    s10 = scores[half:, :half]
    s11 = jnp.where(diag, scores[half:, half:], 0.0)
    pair = 2 * (width // heads)
    first = lax.broadcasted_iota(jnp.int32, (half, pair), 1) < pair // 2
    for p in range(heads // 2):
        cols = slice(p * pair, (p + 1) * pair)
        upper, lower = [], []
        for h in (2 * p, 2 * p + 1):
            q0, q1 = cum_t[:half, h : h + 1], cum_t[half:, h : h + 1]
            k0, k1 = cum[h : h + 1, :half], cum[h : h + 1, half:]
            m00 = jnp.exp(jnp.minimum(q0 - k0, 0.0)) * s00
            m10 = jnp.exp(jnp.minimum(q1 - k0, 0.0)) * s10
            m11 = jnp.exp(jnp.minimum(q1 - k1, 0.0)) * s11
            upper.append(m00.astype(BF))
            lower.append(jnp.concatenate([m10.astype(BF), m11.astype(BF)], axis=1))
        y0 = mm(jnp.concatenate(upper, axis=0), xd[:half, cols])
        y1 = mm(jnp.concatenate(lower, axis=0), xd[:, cols])
        inner_ref[:half, cols] = jnp.where(first, y0[:half], y0[half:]) + skip[:, cols] * x[:half, cols]
        inner_ref[half:, cols] = jnp.where(first, y1[:half], y1[half:]) + skip[:, cols] * x[half:, cols]


def unit():
    return lax.axis_index("tok") * lax.axis_size("rep") + lax.axis_index("rep")


def weight_pieces(refs, full_ref, semaphore):
    copies = []
    for k, piece in enumerate(refs):
        rows = piece.shape[0]
        at = pl.ds(pl.multiple_of((unit() ^ k) * rows, rows), rows) if len(refs) > 1 else pl.ds(0, rows)
        copies.append(Coming(piece, full_ref.at[at, :], semaphore.at[k]))
    return copies


def weight_kernel(g_in, *refs):
    pieces, (ng_ref, full_ref, semaphore) = refs[:-3], refs[-3:]
    copies = weight_pieces(pieces, full_ref, semaphore)
    g = g_in.ready()[...]
    for one in copies:
        one.ready()
    ng_ref[...] = mm_nt(g, full_ref[...]).astype(BF)


def norm_kernel(
    c_in, z_in, x_in, aux_ref, params_ref, local_ref, ng_ref, inc_ref,
    normed_ref, other_ref, dy_ref, zg_ref, rows_ref, sums_ref, *refs,
):
    carries, (all_ref, inner_ref, ec_ref, de_ref, hi_ref, lo_ref) = refs[:-6], refs[-6:]
    _, _, _, cum, _ = load_decay(aux_ref)
    heads, length = cum.shape
    width = params_ref.shape[1]
    hmap = head_map(heads, width)
    ec_ref[...] = expand(jnp.exp(cum), hmap)
    c_ref = c_in.ready()
    inner_ref[...] = mm(c_ref[...], inc_ref[...])
    z_ref, x_ref = z_in.ready(), x_in.ready()
    skip, gain = params_ref[0:1, :], params_ref[1:2, :]
    step = length // CHUNKS
    gains = jnp.zeros((1, width), F32)
    skips = jnp.zeros((1, width), F32)
    for n in range(CHUNKS):
        at = slice(n * step, (n + 1) * step)
        ec = ec_ref[at, :]
        inner = local_ref[at, :] + inner_ref[at, :] * ec
        z = z_ref[at, :].astype(F32)
        sig = 1.0 / (1.0 + jnp.exp(-z))
        silu = z * sig
        gated = inner * silu
        r = lax.rsqrt(jnp.mean(gated * gated, axis=1, keepdims=True) + 1e-05)
        nhat = gated * r
        normed_ref[at, :] = (nhat * gain).astype(BF)
        ng = ng_ref[at, :].astype(F32)
        prod = ng * nhat
        gains = gains + jnp.sum(prod, axis=0, keepdims=True)
        m = jnp.mean(prod * gain, axis=1, keepdims=True)
        dgated = r * (ng * gain - nhat * m)
        dinner = dgated * silu
        dy = dinner.astype(BF)
        dy_ref[at, :] = dy
        de_ref[at, :] = (dinner * ec).astype(BF)
        zg_ref[at, :] = (dgated * inner * (sig + silu * (1.0 - sig))).astype(BF)
        x = x_ref[at, :].astype(F32)
        skips = skips + jnp.sum(dinner * x, axis=0, keepdims=True)
        hi_ref[at, :], lo_ref[at, :] = split(dy.astype(F32) * (inner - skip * x), 2)
    carry = mm_tn(c_ref[...], de_ref[...]).astype(BF)
    if len(carries) == 1:
        carries[0][...] = carry
    else:
        store_parts(all_ref, carry, gains)
        for k, part_ref in enumerate(carries):
            part_ref[...] = all_ref[turn(k, len(carries))]
    hb = hmap.astype(BF)
    rows_ref[...] = mm_nt(hb, hi_ref[...]) + mm_nt(hb, lo_ref[...])
    sums_ref[0:1, :] = gains
    sums_ref[1:2, :] = skips
    block = other_ref.shape[1] // 4
    for k in range(4):
        at = (2 * k + 1 - lax.rem(lax.axis_index("rep"), 2)) * block
        other_ref[:, k * block : (k + 1) * block] = normed_ref[:, pl.ds(pl.multiple_of(at, block), block)]


def outer_kernel(g_in, gc_in, normed_ref, got_ref, out_ref):
    g_ref, gc_ref = g_in.ready(), gc_in.ready()
    core = lax.rem(lax.axis_index("rep"), 2)
    chips, rows = out_ref.shape[:2]
    for k in range(chips):
        mine = pl.ds(pl.multiple_of((2 * k + core) * rows, rows), rows)
        part = mm_tn(normed_ref[:, mine], g_ref[...]) + mm_tn(got_ref[:, k * rows : (k + 1) * rows], gc_ref[...])
        out_ref[k] = part.astype(BF)


def share_kernel(all_ref, *refs):
    outs, total_ref = refs[:-1], refs[-1]
    total = all_ref[0].astype(F32)
    for k in range(1, all_ref.shape[0]):
        total = total + all_ref[k].astype(F32)
    total_ref[...] = total
    rows = outs[0].shape[0]
    for k, out_ref in enumerate(outs):
        part = total_ref[pl.ds(pl.multiple_of(turn(k, len(outs)) * rows, rows), rows), :]
        out_ref[...] = part.astype(out_ref.dtype)


def add_kernel(*refs):
    own_ref, gots, out_ref = refs[0], refs[1:-1], refs[-1]
    total = own_ref[...]
    for got in gots:
        total = total + got[...].astype(F32)
    out_ref[...] = total.astype(BF)


def mixed_kernel(weight_in, normed_ref, mixed_ref):
    mixed_ref[...] = mm(normed_ref[...], weight_in.ready()[...]).astype(BF)


def join_kernel(*refs):
    gather_rows(refs[:-1], refs[-1])


def outer_full_kernel(normed_ref, g_ref, out_ref):
    out_ref[...] = mm_tn(normed_ref[...], g_ref[...])


def back_kernel(
    dy_in, b_in, c_in, x_in, aux_ref, params_ref, inc_ref,
    cg_ref, xg_ref, bg_ref, cols_ref, dxw_ref,
):
    _, delta, _, cum, _ = load_decay(aux_ref)
    x_ref, b_ref, c_ref = x_in.ready(), b_in.ready(), c_in.ready()
    dy_ref = dy_in.ready()
    heads, length = cum.shape
    width = x_ref.shape[1]
    hmap = head_map(heads, width)
    cum_t = cum.T
    delta_e = expand(delta, hmap)
    xd = (x_ref[...].astype(F32) * delta_e).astype(BF)
    dy = dy_ref[...]
    half = length // 2
    scores = mm_nt(b_ref[...], c_ref[...])
    i = lax.broadcasted_iota(jnp.int32, (half, half), 0)
    j = lax.broadcasted_iota(jnp.int32, (half, half), 1)
    diag = j >= i
    s00 = jnp.where(diag, scores[:half, :half], 0.0)
    s01 = scores[:half, half:]
    s11 = jnp.where(diag, scores[half:, half:], 0.0)
    pair = 2 * (width // heads)
    first = lax.broadcasted_iota(jnp.int32, (half, pair), 1) < pair // 2
    whole_first = lax.broadcasted_iota(jnp.int32, (length, pair), 1) < pair // 2
    d00 = jnp.zeros((half, half), F32)
    d01 = jnp.zeros((half, half), F32)
    d11 = jnp.zeros((half, half), F32)
    none = jnp.zeros((length, pair), BF)
    for p in range(heads // 2):
        cols = slice(p * pair, (p + 1) * pair)
        xp, dp = xd[:, cols], dy[:, cols]
        stacked = jnp.concatenate([jnp.where(whole_first, xp, none), jnp.where(whole_first, none, xp)], axis=0)
        dm = mm_nt(stacked, dp)
        upper, lower = [], []
        for n, h in enumerate((2 * p, 2 * p + 1)):
            k0, k1 = cum_t[:half, h : h + 1], cum_t[half:, h : h + 1]
            q0, q1 = cum[h : h + 1, :half], cum[h : h + 1, half:]
            l00 = jnp.exp(jnp.minimum(q0 - k0, 0.0))
            l01 = jnp.exp(jnp.minimum(q1 - k0, 0.0))
            l11 = jnp.exp(jnp.minimum(q1 - k1, 0.0))
            at = n * length
            d00 = d00 + l00 * dm[at : at + half, :half]
            d01 = d01 + l01 * dm[at : at + half, half:]
            d11 = d11 + l11 * dm[at + half : at + length, half:]
            upper.append(jnp.concatenate([(l00 * s00).astype(BF), (l01 * s01).astype(BF)], axis=1))
            lower.append((l11 * s11).astype(BF))
        y0 = mm(jnp.concatenate(upper, axis=0), dp)
        y1 = mm(jnp.concatenate(lower, axis=0), dp[half:])
        dxw_ref[:half, cols] = jnp.where(first, y0[:half], y0[half:])
        dxw_ref[half:, cols] = jnp.where(first, y1[:half], y1[half:])
    d00 = jnp.where(diag, d00, 0.0).astype(BF)
    d01 = d01.astype(BF)
    d11 = jnp.where(diag, d11, 0.0).astype(BF)
    c0, c1 = c_ref[:half, :], c_ref[half:, :]
    b0, b1 = b_ref[:half, :], b_ref[half:, :]
    bg_ref[:half, :] = (mm(d00, c0) + mm(d01, c1)).astype(BF)
    bg_ref[half:, :] = mm(d11, c1).astype(BF)
    ec = expand(jnp.exp(cum), hmap)
    carried = mm_nt((dy.astype(F32) * ec).astype(BF), inc_ref[...])
    cg_ref[:half, :] = (carried[:half] + mm_tn(d00, b0).astype(BF).astype(F32)).astype(BF)
    cg_ref[half:, :] = (carried[half:] + (mm_tn(d01, b0) + mm_tn(d11, b1)).astype(BF).astype(F32)).astype(BF)
    dxw = dxw_ref[...]
    cols_ref[...] = head_sums(xd.astype(F32) * dxw, hmap)
    skip = params_ref[0:1, :]
    xg_ref[...] = delta_e * dxw + skip * dy.astype(F32)


def last_kernel(
    gains_here, b_in, x_in, rows_in, cols_in, bg_in, xg_in, sums_in, aux_ref, inc_ref, *more,
):
    parts, (x_out, b_out, step_out, sums_out, later_ref) = more[:-5], more[-5:]
    gains_ref, parts = (parts[0], parts[1:]) if gains_here else (None, parts)
    count = len(parts)
    if count > 1:
        gather_rows(parts, later_ref)
    else:
        later_ref[...] = parts[0][...]
    v, delta, ld, cum, a = load_decay(aux_ref)
    heads, length = cum.shape
    width = xg_in.target.shape[1]
    hmap = head_map(heads, width)
    last = cum[:, -1:]
    tailing = jnp.exp(last - cum)
    tail = tailing * delta
    tail_e = expand(tail, hmap)
    b_ref = b_in.ready()
    later = later_ref[...]
    dweighted = mm(b_ref[...], later)
    x = x_in.ready()[...].astype(F32)
    x_out[...] = (xg_in.ready()[...] + tail_e * dweighted).astype(BF)
    weighted = (x * tail_e).astype(BF)
    b_out[...] = (bg_in.ready()[...].astype(F32) + mm_nt(weighted, later)).astype(BF)
    dtail = head_sums(x * dweighted, hmap)
    cross = jnp.sum(later.astype(F32) * inc_ref[...].astype(F32), axis=0, keepdims=True)
    dtotal = jnp.sum(cross * hmap, axis=1, keepdims=True) * jnp.exp(last)
    cols = cols_in.ready()[...]
    dld = along_frames(rows_in.ready()[...] - cols, triangle(length, lambda i, j: i >= j))
    dld = dld + along_frames(dtail * tail, triangle(length, lambda i, j: i < j)) + dtotal
    ddelta = cols / delta + dtail * tailing + a * dld
    dstep = ddelta / (1.0 + jnp.exp(-v))
    step_out[...] = dstep
    drate = jnp.sum(dld * ld, axis=1, keepdims=True)
    dbias = jnp.sum(dstep, axis=1, keepdims=True)
    i = lax.broadcasted_iota(jnp.int32, (heads, 128), 0)
    j = lax.broadcasted_iota(jnp.int32, (heads, 128), 1)

    def lay(col, at):
        return jnp.sum(jnp.where(j == i + at, col, 0.0), axis=0, keepdims=True)

    small = lay(drate, 0) + lay(dbias, heads) + lay(jnp.sum(sums_in.ready()[1:2, :] * hmap, axis=1, keepdims=True), 2 * heads)
    if gains_ref is None:
        sums_out[0] = small
        return
    each = gains_ref.shape[0] // count
    shares = [gains_ref[pl.ds(lax.axis_index("tm") * each + n, 1), :] for n in range(each)]
    row = jnp.concatenate([small] + shares, axis=1)
    for k in range(sums_out.shape[0]):
        sums_out[k] = row


def sums_kernel(all_in, rate_out, bias_out, skip_out, gain_out):
    every = all_in.ready()[...]
    heads = rate_out.shape[0]
    small = jnp.sum(every[:, 0, :128], axis=0)
    rate_out[...] = small[:heads]
    bias_out[...] = small[heads : 2 * heads]
    skip_out[...] = small[2 * heads : 3 * heads]
    share = every.shape[2] - 128
    parts = gain_out.shape[0] // share
    group = every.shape[0] // parts
    for k in range(parts):
        gain_out[k * share : (k + 1) * share] = jnp.sum(every[k * group : (k + 1) * group, 0, 128:], axis=0)


def scan_far(value, total, axis, reverse):
    count = lax.axis_size(axis)
    position = lax.axis_index(axis)
    decayed, state = total, value.astype(F32)
    step = 1
    while step < count:
        pairs = [(k, k - step) for k in range(step, count)] if reverse else [(k, k + step) for k in range(count - step)]
        inside = position + step < count if reverse else position >= step
        got_state = lax.ppermute(state.astype(BF), axis, pairs).astype(F32)
        got_total = lax.ppermute(decayed, axis, pairs)
        state = jnp.where(inside, decayed * got_state + state, state)
        decayed = jnp.where(inside, decayed * got_total, decayed)
        step *= 2
    pairs = [(k, k - 1) for k in range(1, count)] if reverse else [(k, k + 1) for k in range(count - 1)]
    return lax.ppermute(state.astype(BF), axis, pairs)


def shards(x_branch, z_gate, b_input, c_input, step_raw, rate_log, step_bias, skip_gain, norm_gain, out_weight, out_grad):
    seqs, length, width = x_branch.shape
    model = out_grad.shape[2]
    heads = rate_log.shape[0]
    state_size = b_input.shape[2]
    x, z, b, c, s, g = x_branch[0], z_gate[0], b_input[0], c_input[0], step_raw[0], out_grad[0]
    n_tm, n_tok, n_rep = lax.axis_size("tm"), lax.axis_size("tok"), lax.axis_size("rep")
    near = (n_tm, n_tok, n_rep) == (4, 2, 4)
    rows = out_weight.shape[0]
    full = (width, model)
    wide = (length, width)
    core = [(k, k ^ 1) for k in range(4)]
    side = [(k, k ^ 2) for k in range(4)]
    front = [(0, 1), (1, 0)]
    diagonal = [(k, k ^ 6) for k in range(8)]
    ahead = [[(i, (i + k) % n_tm) for i in range(n_tm)] for k in range(1, n_tm)]

    raw = (s, rate_log, step_bias, b, x, skip_gain, norm_gain, out_weight)
    aux_shapes = [((5 * heads, length), F32, near_by), ((8, width), F32, near_by), (out_weight.shape, BF, free)]
    if near:
        part = (n_tm, state_size // n_tm)
        row_part = (part[1], width)
        blocks_of = width // 128
        part_shape = (n_tm, blocks_of * part[1] + 2 * blocks_of, 128)
        aux, params, out_weight, *payload = call(
            payload_kernel, aux_shapes + [(part_shape[1:], BF, free)] * n_tm, raw, name="state",
            scratch=[pltpu.VMEM(part_shape, BF)],
        )
        blocks = [payload[0]] + [lax.ppermute(v, "tm", pairs) for v, pairs in zip(payload[1:], ahead)]
        gc = lax.ppermute(g, "rep", core)
        wx = lax.ppermute(out_weight, "rep", side)
        wy = lax.ppermute(out_weight, "tok", front)
        wd = lax.ppermute(out_weight, ("tok", "rep"), diagonal)
        wc, wxc, wyc, wdc = (lax.ppermute(v, "rep", core) for v in (out_weight, wx, wy, wd))
        prefixes, decays = call(
            prefix_kernel, [(part + (width,), BF, free), ((n_tm * blocks_of, 128), F32, near_by)], (), *blocks,
            name="prefix", scratch=[pltpu.VMEM(part_shape, BF)],
        )
        incoming = lax.all_to_all(prefixes, "tm", 0, 0, tiled=True).reshape(state_size, width)
        (local,) = call(
            inner_kernel, [(wide, F32, near_by)], (b, c, x), aux, params, name="inner", beside=(prefixes,)
        )
        pieces = (out_weight, wc, wx, wxc, wy, wyc, wd, wdc)
        after = ()
    else:
        aux, params, out_weight, state, total = call(
            payload_kernel, aux_shapes + [((state_size, width), BF, free), ((1, width), F32, free)], raw, name="state"
        )
        incoming = scan_far(state, total, "tm", False)
        (local,) = call(inner_kernel, [(wide, F32, near_by)], (b, c, x), aux, params, name="inner")
        pieces = (lax.all_gather(out_weight, ("tok", "rep"), axis=0, tiled=True),)
        after = ()
    ng, weight = call(
        weight_kernel, [(wide, BF, near_by), (full, BF, away)], (g,), *pieces, name="normed_grad", after=after, beside=(local,), held=len(pieces), loose=True,
        scratch=[pltpu.SemaphoreType.DMA((len(pieces),))],
    )
    normed, other, dy, zg, row_sums, gains, *carry = call(
        norm_kernel,
        [
            (wide, BF, near_by), ((length, width // 2), BF, free), (wide, BF, free),
            (wide, BF, away), ((heads, length), F32, free), ((8, width), F32, free),
        ]
        + ([(part_shape[1:], BF, free)] * n_tm if near else [((state_size, width), BF, away)]),
        (c, z, x), aux, params, local, ng, incoming, name="norm",
        scratch=[pltpu.VMEM(part_shape if near else (8, 128), BF)] + [pltpu.VMEM(wide, F32)] * 2 + [pltpu.VMEM(wide, BF)] * 3,
    )

    def mixed_of(*after):
        return call(mixed_kernel, [(wide, BF, away)], (weight,), normed, name="mixed", beside=after)[0]

    def back(*after):
        return call(
            back_kernel,
            [
                ((length, state_size), BF, away), (wide, F32, free), ((length, state_size), BF, free),
                ((heads, length), F32, free),
            ],
            ([dy], b, c, x), aux, params, incoming, name="back", beside=after, scratch=[pltpu.VMEM(wide, F32)],
        )

    everywhere = ("tm", "tok", "rep")

    def last(row, parts, *more, after=()):
        return call(
            functools.partial(last_kernel, bool(more)),
            [(wide, BF, away), ((length, state_size), BF, away), ((heads, length), F32, away), (row, F32, away)],
            (b, x, [row_sums], [col_sums], [bg], [xg], [gains]), aux, incoming, *more, *parts, name="last", after=after,
            scratch=[pltpu.VMEM((state_size, width), BF)],
        )

    if near:
        theirs = lax.ppermute(other, "rep", core)
        (products,) = call(
            outer_kernel, [((4, rows, model), BF, free)], (g, gc), normed, theirs, name="outer", beside=(carry[0],)
        )
        grads = [carry[0]] + [lax.ppermute(v, "tm", pairs) for v, pairs in zip(carry[1:], ahead)]
        mixed = mixed_of(products)
        own, *sends, products, gains_tm = call(
            suffix_kernel, [(row_part, BF, free)] * n_tm + [(products.shape, BF, free), ((blocks_of, 128), F32, near_by)], (),
            decays, products, *grads, name="suffix", far_operands=(1,), aliases={1: n_tm}, scratch=[pltpu.VMEM(part + (width,), BF), pltpu.VMEM(part_shape, BF)], after=(mixed,),
        )
        parts = [own] + [lax.ppermute(v, "tm", pairs) for v, pairs in zip(sends, ahead)]
        chips = lax.all_to_all(
            products, ("tok", "rep"), 0, 0, axis_index_groups=[[0, 2, 4, 6], [1, 3, 5, 7]], tiled=True
        )
        c_grad, xg, bg, col_sums = back(own)
        row = (n_tm * n_tok * n_rep, 1, 128 + width // n_tm)
        x_grad, b_grad, step_grad, sums = last(row, parts, gains_tm)
        quarter = (rows // n_tm, model)
        own, *sends = call(
            share_kernel, [(quarter, F32, near_by)] + [(quarter, BF, free)] * (n_tm - 1), (), chips, name="add_chips",
            after=(step_grad,), scratch=[pltpu.VMEM((rows, model), F32)],
        )
        shares = [lax.ppermute(v, "tm", pairs) for v, pairs in zip(sends, ahead)]
        (quarter,) = call(add_kernel, [(quarter, BF, free)], (), own, *shares, name="add_blocks")
        pieces = [lax.ppermute(quarter, "tm", pairs) for pairs in ahead]
        (weight_grad,) = call(join_kernel, [((rows, model), BF, away)], (), quarter, *pieces, name="join")
        sums = lax.all_to_all(sums, everywhere, 0, 0, tiled=True)
    else:
        later = scan_far(carry[0], total, "tm", True)
        (outer,) = call(outer_full_kernel, [(full, F32, free)], (), normed, g, name="outer")
        share = lax.psum_scatter(outer, ("tok", "rep"), scatter_dimension=0, tiled=True)
        weight_grad = lax.psum(share, "tm").astype(BF)
        mixed = mixed_of()
        c_grad, xg, bg, col_sums = back()
        x_grad, b_grad, step_grad, sums = last((1, 1, 128), (later,))
        sums = lax.psum(jnp.concatenate([sums, gains[None, :1]], axis=2), everywhere)
    rate_grad, bias_grad, skip_grad, gain_grad = call(
        sums_kernel, [((heads,), F32, away)] * 3 + [((width,), F32, away)], (sums,), name="sums", loose=True
    )
    return (
        mixed[None], x_grad[None], zg[None], b_grad[None], c_grad[None], step_grad[None],
        rate_grad, bias_grad, skip_grad, gain_grad, weight_grad,
    )


def solution(mesh):
    tokens = P(("tok", "rep"), "tm", None)
    frames = P(("tok", "rep"), None, "tm")
    weight = P(("tok", "rep"), None)
    return jax.shard_map(
        shards,
        mesh=mesh,
        in_specs=(tokens, tokens, tokens, tokens, frames, P(), P(), P(), P(), weight, tokens),
        out_specs=(tokens, tokens, tokens, tokens, tokens, frames, P(), P(), P(), P(), weight),
        check_vma=False,
    )
```
